256 devices in a mesh: lat: 64 (over x, y, z_lo, core), lev: 4 (over z_hi).
Axes of the slice: x: 4, y: 4, z: 8 (z_hi: 4, z_lo: 2; z = z_hi * 2 + z_lo), core: 2. Of those that a mesh axis runs over, the one named last changes fastest.
Arguments:
- zonal_wind: float32 [768, 128, 576], P('lat', 'lev'), may hold values from -3 to 3
- meridional_wind: float32 [768, 128, 576], P('lat', 'lev'), may hold values from -3 to 3
- thickness: float32 [768, 128, 576], P('lat', 'lev'), may hold values from 0.00390625 to 0.01171875
- potential_temp: float32 [768, 128, 576], P('lat', 'lev'), may hold values from 0.8 to 1.6
- surface_geo: float32 [768, 576], P('lat'), may hold values from -1.5 to 1.5
- polar_mask: int32 [768], P('lat'), may hold values from 0 to 1, as said below
- cutoff: int32 [768], P('lat'), may hold values from 1 to 143
- damping: float32 [768, 576], P('lat'), may hold values from 0.05 to 0.8
Outputs:
- zonal_next: float32 [768, 128, 576], P('lat', 'lev')
- meridional_next: float32 [768, 128, 576], P('lat', 'lev')
- thickness_next: float32 [768, 128, 576], P('lat', 'lev')
- potential_next: float32 [768, 128, 576], P('lat', 'lev')
The draws below stay inside these ranges and needn't reach their ends.
Inputs may be any that keep to these rules, and one draw needn't show every extreme that they name: `polar_mask`: 1 exactly on the first s and the last n latitude rows and 0 elsewhere; the larger of s and n is 192, the smaller lies between 128 and 192.
All inputs are finite; a program needn't handle non-finite values.
Results may differ from the reference program's by a relative error of at most 0.0003.
Values sent between devices are 32-bit elements; how exact they have to be, the bound alone decides.
No kernel may reach another device: no remote copies, remote signals or barrier semaphores. Data moves between devices by JAX's collectives and lax.ppermute only.
A program may use at most 128 MiB of HBM per device.

```python
import math
import jax
import jax.numpy as jnp
from jax import lax

NLON = 576
NLEV = 128
NLAT = 768


def draw_polar_mask(key, part):
    inner = jax.random.fold_in(key, 11)
    first_key, second_key = jax.random.split(inner)
    lowest = NLAT // 6
    highest = NLAT // 4
    other = jax.random.randint(first_key, (), lowest, highest + 1)
    which_side = jax.random.randint(second_key, (), 0, 2)
    south_rows = jnp.where(which_side == 0, highest, other)
    north_rows = jnp.where(which_side == 0, other, highest)
    row_ids = jnp.arange(NLAT, dtype=jnp.int32)
    marked = (row_ids < south_rows) | (row_ids >= NLAT - north_rows)
    return marked.astype(jnp.int32)


def set_ends(result, key, smallest, top_value):
    dims = result.shape
    index_at = [jax.random.randint(jax.random.fold_in(key, axis), (), 0, dims[axis]) for axis in range(len(dims))]
    result = result.at[tuple(index_at)].set(smallest)
    longest = dims.index(max(dims))
    index_at[longest] = (index_at[longest] + 1) % dims[longest]
    return result.at[tuple(index_at)].set(top_value)


def block_scale(rng, shape, cuts, low, top_value):
    gain, own = 1.0, jax.random.fold_in(rng, 6)
    for position, blocks in cuts:
        heights = jnp.exp(jax.random.uniform(jax.random.fold_in(own, position), (blocks,), jnp.float32, low / len(cuts), top_value / len(cuts)))
        gain = gain * jnp.repeat(heights, shape[position] // blocks).reshape([-1 if axis == position else 1 for axis in range(len(shape))])
    return gain


def bell_draw(own_key, shape, spread, reach, cuts=(), kind=jnp.bfloat16):
    values = jax.random.normal(own_key, shape, jnp.float32) * spread
    if len(cuts) > 0:
        values = block_scale(own_key, shape, cuts, -0.22, 0.18) * values
    return jnp.clip(values, min=-reach, max=reach).astype(kind)


def setup_inputs(seed: int = 0) -> dict:
    splits = jax.random.split(jax.random.key(seed), 9)
    zonal_wind = bell_draw(splits[0], (NLAT, NLEV, NLON), 1.0, 3.0, ((0, 64), (1, 4)), jnp.float32)
    meridional_wind = bell_draw(splits[1], (NLAT, NLEV, NLON), 1.0, 3.0, ((0, 64), (1, 4)), jnp.float32)
    thickness = jnp.clip(0.00390625 + 0.0078125 * jax.random.uniform(splits[2], (NLAT, NLEV, NLON), jnp.float32) ** block_scale(splits[2], (NLAT, NLEV, NLON), ((0, 64), (1, 4)), -0.2, 0.2), 0.00390625, 0.01171875)
    potential_temp = jnp.clip(0.8 + 0.8 * jax.random.uniform(splits[3], (NLAT, NLEV, NLON), jnp.float32) ** block_scale(splits[3], (NLAT, NLEV, NLON), ((0, 64), (1, 4)), -0.2, 0.2), 0.8, 1.6)
    surface_geo = bell_draw(splits[4], (NLAT, NLON), 0.3, 1.5, ((0, 64),), jnp.float32)
    polar_mask = draw_polar_mask(jax.random.fold_in(splits[8], 71), 0)
    cutoff = set_ends(jax.random.randint(splits[6], (NLAT,), 1, NLON // 4), jax.random.fold_in(splits[6], 1), 1, (NLON // 4) - 1).astype(jnp.int32)
    damping = jnp.clip(jnp.exp(math.log(0.8) - 2.7725887 * jax.random.uniform(splits[7], (NLAT, NLON), jnp.float32) ** block_scale(splits[7], (NLAT, NLON), ((0, 64),), -0.2, 0.2)), 0.05, 0.8)
    return dict(zonal_wind=zonal_wind, meridional_wind=meridional_wind, thickness=thickness, potential_temp=potential_temp, surface_geo=surface_geo, polar_mask=polar_mask, cutoff=cutoff, damping=damping)


TOP_PRESSURE = 0.01
HYBRID_SCALE = 0.2
EXNER_POWER = 2.0 / 7.0
ZONAL_COURANT = 0.012
MERIDIONAL_COURANT = 0.012
HIGHEST = lax.Precision.HIGHEST

def fourier_basis(count):
    middle = count // 2
    points = jnp.arange(count, dtype=jnp.int32)
    column_ids = jnp.arange(count, dtype=jnp.int32)
    wave = jnp.where(column_ids <= middle, column_ids, column_ids - middle)
    phase = points[:, None] * wave[None, :] % count
    angle = 2.0 * math.pi / count * phase.astype(jnp.float32)
    edge_cols = (column_ids == 0) | (column_ids == middle)
    weight = jnp.where(edge_cols, 1.0 / math.sqrt(count), math.sqrt(2.0 / count)).astype(jnp.float32)
    basis = jnp.where((column_ids <= middle)[None, :], jnp.cos(angle), jnp.sin(angle)) * weight[None, :]
    return (basis, wave)

def damping_table(polar_mask, cutoff, damping, wave):
    active = (wave[None, :] >= cutoff[:, None]) & (polar_mask[:, None] != 0)
    return jnp.where(active, damping - 1.0, 0.0).astype(jnp.float32)

def target_interfaces(surface, first_level, count, levels):
    sigma = (first_level + jnp.arange(count + 1, dtype=jnp.int32)).astype(jnp.float32) / levels
    curve = sigma * sigma
    hybrid = sigma - curve
    return TOP_PRESSURE + HYBRID_SCALE * hybrid[:, None] + (surface[..., None, :] - TOP_PRESSURE) * curve[:, None]

def remap_column(thick_col, theta_col):
    levels = thick_col.shape[0]
    edge_ids = jnp.arange(levels + 1, dtype=jnp.int32)
    level_ids = jnp.arange(levels, dtype=jnp.int32)
    lower_tri = (edge_ids[:, None] > level_ids[None, :]).astype(jnp.float32)
    source_edges = TOP_PRESSURE + jnp.dot(lower_tri, thick_col, precision=HIGHEST)
    surface = source_edges[levels]
    target_edges = target_interfaces(surface, 0, levels, levels)
    target_thick = target_edges[1:] - target_edges[:-1]
    exner_edges = target_edges ** EXNER_POWER
    exner_mid = 0.5 * (exner_edges[:-1] + exner_edges[1:])
    block_levels = min(32, levels)
    pieces = []
    for first_level in range(0, levels, block_levels):
        upper_edge = target_edges[first_level:first_level + block_levels]
        lower_edge = target_edges[first_level + 1:first_level + block_levels + 1]
        intersection = jnp.maximum(jnp.minimum(lower_edge[:, None, :], source_edges[None, 1:, :]) - jnp.maximum(upper_edge[:, None, :], source_edges[None, :-1, :]), 0.0)
        pieces.append(lax.optimization_barrier(jnp.sum(intersection * theta_col[None], axis=1)))
    theta_remap = jnp.concatenate(pieces, 0) / target_thick
    layer_term = theta_remap * (exner_edges[1:] - exner_edges[:-1])
    strictly_below = (level_ids[None, :] > level_ids[:, None]).astype(jnp.float32)
    geo_rel = jnp.dot(strictly_below, layer_term, precision=HIGHEST) + 0.5 * layer_term
    return (target_thick, theta_remap, geo_rel, exner_mid, surface)

def polar_filter(field, table, basis):
    spectral = jnp.einsum('lkn,nc->lkc', field, basis, precision=HIGHEST)
    return field + jnp.einsum('lkc,nc->lkn', spectral * table[:, None, :], basis, precision=HIGHEST)

def reference(zonal_wind, meridional_wind, thickness, potential_temp, surface_geo, polar_mask, cutoff, damping):
    total_rows = zonal_wind.shape[0]
    row_ids = jnp.arange(total_rows + 1, dtype=jnp.int32).astype(jnp.float32)
    faces = jnp.sin(math.pi * row_ids / total_rows)[:, None, None]
    centres = jnp.sin(math.pi * (row_ids[:-1] + 0.5) / total_rows)[:, None, None]
    heat = potential_temp * thickness
    zero_row = jnp.zeros_like(thickness[:1])
    thick_pad = jnp.concatenate([zero_row, thickness, zero_row], 0)
    heat_pad = jnp.concatenate([zero_row, heat, zero_row], 0)
    wind_ext = jnp.concatenate([meridional_wind, zero_row], 0)
    merid_mass = wind_ext * faces * 0.5 * (thick_pad[1:] + thick_pad[:-1])
    merid_heat = wind_ext * faces * 0.5 * (heat_pad[1:] + heat_pad[:-1])
    zonal_mass = zonal_wind * 0.5 * (thickness + jnp.roll(thickness, 1, axis=2))
    zonal_heat = zonal_wind * 0.5 * (heat + jnp.roll(heat, 1, axis=2))
    thick_new = thickness - ZONAL_COURANT * (jnp.roll(zonal_mass, -1, axis=2) - zonal_mass) - MERIDIONAL_COURANT * (merid_mass[1:] - merid_mass[:-1]) / centres
    heat_new = heat - ZONAL_COURANT * (jnp.roll(zonal_heat, -1, axis=2) - zonal_heat) - MERIDIONAL_COURANT * (merid_heat[1:] - merid_heat[:-1]) / centres
    theta_new = heat_new / thick_new

    def one_row(pair):
        return remap_column(pair[0], pair[1])[:4]
    thick_out, theta_out, geo_rel, exner_mid = lax.map(one_row, (thick_new, theta_new))
    geopot = surface_geo[:, None, :] + geo_rel
    zonal_push = geopot - jnp.roll(geopot, 1, axis=2) + 0.5 * (theta_out + jnp.roll(theta_out, 1, axis=2)) * (exner_mid - jnp.roll(exner_mid, 1, axis=2))
    zonal_pre = zonal_wind - zonal_push
    geo_south = jnp.concatenate([zero_row, geopot[:-1]], 0)
    exner_south = jnp.concatenate([zero_row, exner_mid[:-1]], 0)
    theta_south = jnp.concatenate([zero_row, theta_out[:-1]], 0)
    merid_push = geopot - geo_south + 0.5 * (theta_out + theta_south) * (exner_mid - exner_south)
    meridional_pre = meridional_wind - faces[:-1] * merid_push
    basis, wave = fourier_basis(zonal_wind.shape[2])
    table = damping_table(polar_mask, cutoff, damping, wave)
    zonal_next = polar_filter(zonal_pre, table, basis)
    meridional_next = polar_filter(meridional_pre, table, basis)
    return (zonal_next, meridional_next, thick_out, theta_out)
```

```python
import math

import jax
import jax.numpy as jnp
import numpy as np
from jax import lax
from jax.experimental import pallas as pl
from jax.experimental.pallas import tpu as pltpu
from jax.sharding import PartitionSpec as P

TOP_PRESSURE = 0.01
HYBRID_SCALE = 0.2
EXNER_POWER = 2.0 / 7.0
COURANT = 0.012
HIGHEST = lax.Precision.HIGHEST
F32 = jnp.float32
BF16 = jnp.bfloat16
VMEM = pl.BlockSpec(memory_space=pltpu.VMEM)
SMEM = pl.BlockSpec(memory_space=pltpu.SMEM)
LANES = 128
ROLL_PAD = 64


def params(mib):
    return pltpu.CompilerParams(vmem_limit_bytes=mib * 1024 * 1024)


def fourier_tables(count):
    middle = count // 2
    ids = np.arange(count)
    wave = np.where(ids <= middle, ids, ids - middle)
    angle = 2.0 * np.pi / count * (ids[:, None] * wave[None, :] % count)
    edge = (ids == 0) | (ids == middle)
    weight = np.where(edge, 1.0 / math.sqrt(count), math.sqrt(2.0 / count))
    basis = np.where((ids <= middle)[None, :], np.cos(angle), np.sin(angle)) * weight[None, :]
    basis = basis.astype(np.float32)
    high = basis.astype(jnp.bfloat16)
    low = (basis - high.astype(np.float32)).astype(jnp.bfloat16)
    return high, low, wave.astype(np.int32)


def packed_rows(rows, width):
    return rows * width // LANES


def store_packed(ref, index, value):
    rows, width = value.shape
    full = width // LANES
    for tile in range(full):
        ref[(*index, pl.ds(tile * rows, rows), slice(None))] = value[:, tile * LANES : (tile + 1) * LANES]
    if width % LANES:
        rest = value[:, full * LANES :]
        half = rows // 2
        ref[(*index, pl.ds(full * rows, half), slice(None))] = jnp.concatenate([rest[:half], rest[half:]], axis=1)


def load_tile(ref, index, rows, width, tile):
    full = width // LANES
    if tile < full:
        return ref[(*index, pl.ds(tile * rows, rows), slice(None))]
    half = rows // 2
    both = ref[(*index, pl.ds(full * rows, half), slice(None))]
    return jnp.concatenate([both[:, : LANES // 2], both[:, LANES // 2 :]], axis=0)


def tile_count(width):
    return -(-width // LANES)


def advect_kernel(offsets, rows_each, coef, zonal, merid, thick, theta, halo_s, halo_n, out):
    lat_rows, levels, width = thick.shape

    def row_of(array, halo_low, halo_high, row):
        if row < 0:
            return halo_low
        return halo_high if row >= lat_rows else array[row]

    for owner in range(lat_rows // rows_each):
        for place, offset in enumerate(offsets):
            row = owner * rows_each + offset
            t = thick[row]
            h = theta[row] * t
            t_s = halo_s[0] if row == 0 else thick[row - 1]
            h_s = halo_s[1] if row == 0 else theta[row - 1] * t_s
            last = row == lat_rows - 1
            t_n = halo_n[0] if last else thick[row + 1]
            h_n = halo_n[1] if last else theta[row + 1] * t_n
            w_n = halo_n[2] if last else merid[row + 1]
            u = zonal[row] * (0.5 * COURANT)
            w_n = w_n * coef[1, row]
            w_s = merid[row] * coef[0, row]
            for field, (x, x_s, x_n) in enumerate(((t, t_s, t_n), (h, h_s, h_n))):
                flux = u * (x + jnp.roll(x, 1, axis=1))
                new = x - (jnp.roll(flux, -1, axis=1) - flux) - (w_n * (x_n + x) - w_s * (x + x_s))
                store_packed(out, (owner, place, field), new)


def target_edges(surface, sigma):
    curve = sigma * sigma
    return TOP_PRESSURE + HYBRID_SCALE * (sigma - curve) + (surface - TOP_PRESSURE) * curve


def target_thickness(surface, first, levels):
    step = 1.0 / levels
    curve = (2.0 * first + 1.0) * (step * step)
    return HYBRID_SCALE * (step - curve) + (surface - TOP_PRESSURE) * curve


def exner(pressure):
    return jnp.exp(EXNER_POWER * jnp.log(pressure))


def remap_kernel(width, block, columns, out):
    peers, count = columns.shape[0], columns.shape[1]
    levels = peers * block
    level_r = lax.broadcasted_iota(jnp.int32, (levels, levels), 0)
    level_c = lax.broadcasted_iota(jnp.int32, (levels, levels), 1)
    running = (level_r <= level_c).astype(F32)
    below = (
        lax.broadcasted_iota(jnp.int32, (8, levels), 1)
        >= block * (1 + lax.broadcasted_iota(jnp.int32, (8, levels), 0))
    ).astype(F32)
    full = width // LANES
    data_rows = packed_rows(block, width)
    for place in range(count):
        for tile in range(tile_count(width)):
            thick = jnp.concatenate(
                [load_tile(columns, (p, place, 0), block, width, tile) for p in range(peers)], axis=0
            )
            heat = jnp.concatenate(
                [load_tile(columns, (p, place, 1), block, width, tile) for p in range(peers)], axis=0
            )
            surface_row = TOP_PRESSURE + jnp.sum(thick, axis=0, keepdims=True)
            thick = thick.T
            heat = heat.T
            cols = thick.shape[0]
            upper = TOP_PRESSURE + jnp.dot(thick, running, precision=HIGHEST, preferred_element_type=F32)
            heat_sum = jnp.dot(heat, running, precision=HIGHEST, preferred_element_type=F32)
            theta = heat / thick
            surface = upper[:, levels - 1 :]
            lane = lax.broadcasted_iota(jnp.int32, (cols, levels), 1)
            lane_f = lane.astype(F32)
            edge = target_edges(surface, (lane_f + 1.0) * (1.0 / levels))
            at = jnp.zeros((cols, levels), jnp.int32)
            step = levels // 2
            while step:
                probe = jnp.take_along_axis(upper, at + (step - 1), axis=1, mode="promise_in_bounds")
                at = jnp.where(probe < edge, at + step, at)
                step //= 2
            pick = lambda table: jnp.take_along_axis(table, at, axis=1, mode="promise_in_bounds")
            heat_to = pick(heat_sum) - pick(theta) * (pick(upper) - edge)
            heat_from = jnp.where(lane == 0, 0.0, pltpu.roll(heat_to, 1, 1))
            theta_next = (heat_to - heat_from) / target_thickness(surface, lane_f, levels)
            exner_to = exner(edge)
            exner_from = jnp.where(lane == 0, TOP_PRESSURE**EXNER_POWER, pltpu.roll(exner_to, 1, 1))
            layer = theta_next * (exner_to - exner_from)
            bases = lax.dot_general(
                below, layer, (((1,), (1,)), ((), ())), precision=HIGHEST, preferred_element_type=F32
            )
            result = theta_next.T
            for p in range(peers):
                part = result[p * block : (p + 1) * block]
                if tile < full:
                    out[p, place, pl.ds(tile * block, block), :] = part
                else:
                    half = block // 2
                    out[p, place, pl.ds(full * block, half), :] = jnp.concatenate([part[:half], part[half:]], axis=1)
                out[p, place, pl.ds(data_rows + tile, 1), pl.ds(0, cols)] = surface_row
                out[p, place, pl.ds(data_rows + 8 + tile, 1), pl.ds(0, cols)] = bases[p : p + 1]


def below_sum(layer):
    rows, width = layer.shape
    groups = rows // 8
    carry = None
    pieces = []
    sub = lax.broadcasted_iota(jnp.int32, (8, width), 0)
    for g in reversed(range(groups)):
        x = layer[g * 8 : (g + 1) * 8]
        total = x
        for step in (1, 2, 4):
            total = total + jnp.where(sub < 8 - step, pltpu.roll(total, 8 - step, 0), 0.0)
        under = total - x
        if carry is not None:
            under = under + carry
            carry = carry + total[0:1]
        else:
            carry = total[0:1]
        pieces.append(under)
    return jnp.concatenate(pieces[::-1], axis=0)


def column_state(message, index, block, width, first_level, levels, ground):
    tiles = tile_count(width)
    data_rows = packed_rows(block, width)
    theta = jnp.concatenate([load_tile(message, index, block, width, t) for t in range(tiles)], axis=1)

    def line(first):
        return jnp.concatenate(
            [message[(*index, pl.ds(first + t, 1), pl.ds(0, min(LANES, width - t * LANES)))] for t in range(tiles)],
            axis=1,
        )

    surface = line(data_rows)
    base = line(data_rows + 8)
    sub = lax.broadcasted_iota(jnp.int32, (block, width), 0).astype(F32) + first_level
    thick = target_thickness(surface, sub, levels)
    top = exner(target_edges(surface, sub * (1.0 / levels)))
    bottom_edge = exner(target_edges(surface, (first_level + block) * (1.0 / levels)))
    sub_i = lax.broadcasted_iota(jnp.int32, (block, width), 0)
    bottom = jnp.where(sub_i == block - 1, bottom_edge, pltpu.roll(top, block - 1, 0))
    layer = theta * (bottom - top)
    geopot = (ground + base) + (below_sum(layer) + 0.5 * layer)
    return theta, thick, 0.5 * (top + bottom), geopot


def push(now, before):
    theta, exner_mid, geopot = now
    theta_b, exner_b, geopot_b = before
    return (geopot - geopot_b) + 0.5 * (theta + theta_b) * (exner_mid - exner_b)


def filtered(value, table, high, low, high_t, low_t, block):
    def product(x, b_high, b_low):
        x_high = x.astype(BF16)
        x_low = (x - x_high.astype(F32)).astype(BF16)
        dot = lambda a, b: jnp.dot(a, b, preferred_element_type=F32)
        return dot(x_high, b_high) + (dot(x_low, b_high) + dot(x_high, b_low))

    spectral = product(value, high, low)
    rows, width = value.shape
    spectral = (spectral.reshape(rows // block, block, width) * table[:, None, :]).reshape(rows, width)
    return value + product(spectral, high_t, low_t)


def final_kernel(
    levels, scalars, faces, message, south, ground, south_ground, zonal, merid, table,
    high, low, high_t, low_t, zonal_out, merid_out, thick_out, theta_out, carried,
):
    lat_rows, block, width = zonal.shape
    first_level = scalars[0].astype(F32)

    def state(ref, index, ground_row):
        theta, thick, mid, geopot = column_state(ref, index, block, width, first_level, levels, ground_row)
        return theta, thick, mid, geopot

    theta, _, mid, geopot = state(south, (0,), south_ground[...])
    carried[0] = theta
    carried[1] = mid
    carried[2] = geopot

    def one_row(row, _):
        theta, thick, mid, geopot = state(message, (row,), ground[pl.ds(row, 1), :])
        theta_out[row] = theta
        thick_out[row] = thick
        now = (theta, mid, geopot)
        zonal_out[row] = zonal[row] - push(now, tuple(jnp.roll(x, 1, axis=1) for x in now))
        merid_out[row] = merid[row] - faces[row] * push(now, (carried[0], carried[1], carried[2]))
        carried[0] = theta
        carried[1] = mid
        carried[2] = geopot
        return 0

    lax.fori_loop(0, lat_rows, one_row, 0)

    @pl.when(scalars[1] != 0)
    def _():
        step = 4
        for out in (zonal_out, merid_out):
            def some_rows(i, _):
                rows = pl.ds(i * step, step)
                value = out[rows].reshape(step * block, width)
                value = filtered(value, table[i], high[...], low[...], high_t[...], low_t[...], block)
                out[rows] = value.reshape(step, block, width)
                return 0
            lax.fori_loop(0, lat_rows // step, some_rows, 0)


def body(
    zonal_wind, meridional_wind, thickness, potential_temp, surface_geo, polar_mask, cutoff, damping
):
    lat_rows, block, width = zonal_wind.shape
    lat_count = lax.axis_size("lat")
    peers = lax.axis_size("lev")
    levels = block * peers
    total_rows = lat_rows * lat_count
    first_row = lax.axis_index("lat") * lat_rows
    row_ids = (first_row + jnp.arange(lat_rows + 1, dtype=jnp.int32)).astype(F32)
    faces = jnp.sin(math.pi * row_ids / total_rows)
    centres = jnp.sin(math.pi * (row_ids[:-1] + 0.5) / total_rows)
    coef = jnp.stack([faces[:-1], faces[1:]]) * (0.5 * COURANT) / centres
    northward = [(i, i + 1) for i in range(lat_count - 1)]
    southward = [(i + 1, i) for i in range(lat_count - 1)]
    heat_first = potential_temp[0] * thickness[0]
    heat_last = potential_temp[-1] * thickness[-1]
    halo_s = lax.ppermute(jnp.stack([thickness[-1], heat_last]), "lat", northward)
    halo_n = lax.ppermute(jnp.stack([thickness[0], heat_first, meridional_wind[0]]), "lat", southward)
    south_ground = lax.ppermute(surface_geo[-1:], "lat", northward)

    rows_each = lat_rows // peers
    offsets = tuple(range(rows_each))
    data_rows = packed_rows(block, width)
    message_rows = data_rows + 16
    sent = pl.pallas_call(
        lambda *refs: advect_kernel(offsets, rows_each, *refs),
        out_shape=jax.ShapeDtypeStruct((peers, len(offsets), 2, data_rows, LANES), F32),
        in_specs=[SMEM] + [VMEM] * 6,
        out_specs=VMEM,
        compiler_params=params(32),
        name="advect",
    )(coef, zonal_wind, meridional_wind, thickness, potential_temp, halo_s, halo_n)
    columns = lax.all_to_all(sent, "lev", split_axis=0, concat_axis=0, tiled=True)
    remapped = pl.pallas_call(
        lambda *refs: remap_kernel(width, block, *refs),
        out_shape=jax.ShapeDtypeStruct((peers, len(offsets), message_rows, LANES), F32),
        in_specs=[VMEM],
        out_specs=VMEM,
        compiler_params=params(32),
        name="remap",
    )(columns)
    message = lax.all_to_all(remapped, "lev", split_axis=0, concat_axis=0, tiled=True)
    message = message.reshape(lat_rows, message_rows, LANES)
    south = lax.ppermute(message[-1:], "lat", northward)

    high, low, wave = fourier_tables(width)
    active = (jnp.asarray(wave)[None, :] >= cutoff[:, None]) & (polar_mask[:, None] != 0)
    table = jnp.where(active, damping - 1.0, 0.0).reshape(lat_rows // 4, 4, width)
    scalars = jnp.stack([lax.axis_index("lev") * block, jnp.any(polar_mask != 0).astype(jnp.int32)])
    shape = jax.ShapeDtypeStruct((lat_rows, block, width), F32)
    return pl.pallas_call(
        lambda *refs: final_kernel(levels, *refs),
        out_shape=(shape,) * 4,
        in_specs=[SMEM, SMEM] + [VMEM] * 11,
        out_specs=(VMEM,) * 4,
        scratch_shapes=[pltpu.VMEM((3, block, width), F32)],
        compiler_params=params(48),
        name="final",
    )(
        scalars, faces, message, south, surface_geo, south_ground, zonal_wind, meridional_wind, table,
        jnp.asarray(high), jnp.asarray(low), jnp.asarray(high.T), jnp.asarray(low.T),
    )


def solution(mesh):
    field = P("lat", "lev", None)
    in_specs = (field, field, field, field, P("lat", None), P("lat"), P("lat"), P("lat", None))
    return jax.shard_map(body, mesh=mesh, in_specs=in_specs, out_specs=(field,) * 4, check_vma=False)
```

```python
import math

import jax
import jax.numpy as jnp
import numpy as np
from jax import lax
from jax.experimental import pallas as pl
from jax.experimental.pallas import tpu as pltpu
from jax.sharding import PartitionSpec as P

TOP_PRESSURE = 0.01
HYBRID_SCALE = 0.2
EXNER_POWER = 2.0 / 7.0
COURANT = 0.012
HIGHEST = lax.Precision.HIGHEST
F32 = jnp.float32
BF16 = jnp.bfloat16
VMEM = pl.BlockSpec(memory_space=pltpu.VMEM)
SMEM = pl.BlockSpec(memory_space=pltpu.SMEM)
LANES = 128


def params(mib):
    return pltpu.CompilerParams(vmem_limit_bytes=mib * 1024 * 1024)


def fourier_tables(count):
    middle = count // 2
    ids = np.arange(count)
    wave = np.where(ids <= middle, ids, ids - middle)
    angle = 2.0 * np.pi / count * (ids[:, None] * wave[None, :] % count)
    edge = (ids == 0) | (ids == middle)
    weight = np.where(edge, 1.0 / math.sqrt(count), math.sqrt(2.0 / count))
    basis = np.where((ids <= middle)[None, :], np.cos(angle), np.sin(angle)) * weight[None, :]
    basis = basis.astype(np.float32)
    high = basis.astype(jnp.bfloat16)
    low = (basis - high.astype(np.float32)).astype(jnp.bfloat16)
    return high, low, wave.astype(np.int32)


def packed_rows(rows, width):
    return rows * width // LANES


def store_packed(ref, index, value):
    rows, width = value.shape
    full = width // LANES
    for tile in range(full):
        ref[(*index, pl.ds(tile * rows, rows), slice(None))] = value[:, tile * LANES : (tile + 1) * LANES]
    if width % LANES:
        rest = value[:, full * LANES :]
        half = rows // 2
        ref[(*index, pl.ds(full * rows, half), slice(None))] = jnp.concatenate([rest[:half], rest[half:]], axis=1)


def load_tile(ref, index, rows, width, tile):
    full = width // LANES
    if tile < full:
        return ref[(*index, pl.ds(tile * rows, rows), slice(None))]
    half = rows // 2
    both = ref[(*index, pl.ds(full * rows, half), slice(None))]
    return jnp.concatenate([both[:, : LANES // 2], both[:, LANES // 2 :]], axis=0)


def tile_count(width):
    return -(-width // LANES)


def wrapped(me, step, peers):
    other = me + step
    return jnp.where(other >= peers, other - peers, other)


def advect_row(row, coef, zonal, merid, t, h, t_s, h_s, t_n, h_n, w_n):
    u = zonal[row] * (0.5 * COURANT)
    w_n = w_n * coef[1, row]
    w_s = merid[row] * coef[0, row]
    for x, x_s, x_n in ((t, t_s, t_n), (h, h_s, h_n)):
        flux = u * (x + jnp.roll(x, 1, axis=1))
        yield x - (jnp.roll(flux, -1, axis=1) - flux) - (w_n * (x_n + x) - w_s * (x + x_s))


def advect_inner_kernel(first, rows_each, me_ref, coef, zonal, merid, thick, theta, ground, *outs):
    lat_rows, levels, _ = thick.shape
    peers = len(outs) - 2
    to_north, to_south = outs[peers:]
    for step in range(peers):
        owner = wrapped(me_ref[0], step, peers)
        for place in range(rows_each):
            row = first + owner * rows_each + place
            t, t_s, t_n = thick[row], thick[row - 1], thick[row + 1]
            h, h_s, h_n = theta[row] * t, theta[row - 1] * t_s, theta[row + 1] * t_n
            fields = advect_row(row, coef, zonal, merid, t, h, t_s, h_s, t_n, h_n, merid[row + 1])
            for field, new in enumerate(fields):
                store_packed(outs[step], (place, field), new)
    top = lat_rows - 1
    to_north[pl.ds(0, levels), :] = thick[top]
    to_north[pl.ds(levels, levels), :] = theta[top] * thick[top]
    to_north[pl.ds(2 * levels, 1), :] = ground[pl.ds(top, 1), :]
    to_south[pl.ds(0, levels), :] = thick[0]
    to_south[pl.ds(levels, levels), :] = theta[0] * thick[0]
    to_south[pl.ds(2 * levels, levels), :] = merid[0]


def advect_outer_kernel(me_ref, coef, zonal, merid, thick, theta, halo_s, halo_n, *outs):
    lat_rows, levels, _ = thick.shape
    peers = len(outs)
    top = lat_rows - 1
    for step in range(peers):
        owner = wrapped(me_ref[0], step, peers)
        is_first, is_last = owner == 0, owner == peers - 1
        row = jnp.where(is_last, top, owner)
        low, high = jnp.maximum(row - 1, 0), jnp.minimum(row + 1, top)
        t, t_s, t_n = thick[row], thick[low], thick[high]
        h, h_s, h_n = theta[row] * t, theta[low] * t_s, theta[high] * t_n
        w_n = merid[high]
        part = lambda ref, i: ref[pl.ds(i * levels, levels), :]
        t_s = jnp.where(is_first, part(halo_s, 0), t_s)
        h_s = jnp.where(is_first, part(halo_s, 1), h_s)
        t_n = jnp.where(is_last, part(halo_n, 0), t_n)
        h_n = jnp.where(is_last, part(halo_n, 1), h_n)
        w_n = jnp.where(is_last, part(halo_n, 2), w_n)
        fields = advect_row(row, coef, zonal, merid, t, h, t_s, h_s, t_n, h_n, w_n)
        for field, new in enumerate(fields):
            store_packed(outs[step], (0, field), new)


def target_edges(surface, sigma):
    curve = sigma * sigma
    return TOP_PRESSURE + HYBRID_SCALE * (sigma - curve) + (surface - TOP_PRESSURE) * curve


def target_thickness(surface, first, levels):
    step = 1.0 / levels
    curve = (2.0 * first + 1.0) * (step * step)
    return HYBRID_SCALE * (step - curve) + (surface - TOP_PRESSURE) * curve


def exner(pressure):
    return jnp.exp(EXNER_POWER * jnp.log(pressure))


def remap_kernel(width, block, me_ref, *refs):
    peers = (len(refs) - 3) // 2
    parts, outs, (gathered, spread, base_rows) = refs[:peers], refs[peers : 2 * peers], refs[2 * peers :]
    count = parts[0].shape[0]
    levels = peers * block
    level_r = lax.broadcasted_iota(jnp.int32, (levels, levels), 0)
    level_c = lax.broadcasted_iota(jnp.int32, (levels, levels), 1)
    running = (level_r <= level_c).astype(F32)
    below = (
        lax.broadcasted_iota(jnp.int32, (8, levels), 1)
        >= block * (1 + lax.broadcasted_iota(jnp.int32, (8, levels), 0))
    ).astype(F32)
    full = width // LANES
    data_rows = packed_rows(block, width)
    half = block // 2
    sources = [wrapped(me_ref[0], (peers - step) % peers, peers) for step in range(peers)]
    targets = [wrapped(me_ref[0], step, peers) for step in range(peers)]
    for place in range(count):
        for tile in range(tile_count(width)):
            cols = min(LANES, width - tile * LANES)
            slot = tile % 2

            def whole_columns(field):
                for step in range(peers):
                    at = pl.ds(pl.multiple_of(sources[step] * block, block), block)
                    gathered[slot, field, at, pl.ds(0, cols)] = load_tile(parts[step], (place, field), block, width, tile)
                return gathered[slot, field, :, pl.ds(0, cols)]

            thick = whole_columns(0)
            heat = whole_columns(1)
            surface_row = TOP_PRESSURE + jnp.sum(thick, axis=0, keepdims=True)
            thick = thick.T
            heat = heat.T
            upper = TOP_PRESSURE + jnp.dot(thick, running, precision=HIGHEST, preferred_element_type=F32)
            heat_sum = jnp.dot(heat, running, precision=HIGHEST, preferred_element_type=F32)
            theta = heat / thick
            surface = upper[:, levels - 1 :]
            lane = lax.broadcasted_iota(jnp.int32, (cols, levels), 1)
            lane_f = lane.astype(F32)
            edge = target_edges(surface, (lane_f + 1.0) * (1.0 / levels))
            at = jnp.zeros((cols, levels), jnp.int32)
            jump = levels // 2
            while jump:
                probe = jnp.take_along_axis(upper, at + (jump - 1), axis=1, mode="promise_in_bounds")
                at = jnp.where(probe < edge, at + jump, at)
                jump //= 2
            pick = lambda table: jnp.take_along_axis(table, at, axis=1, mode="promise_in_bounds")
            heat_to = pick(heat_sum) - pick(theta) * (pick(upper) - edge)
            heat_from = jnp.where(lane == 0, 0.0, pltpu.roll(heat_to, 1, 1))
            theta_next = (heat_to - heat_from) / target_thickness(surface, lane_f, levels)
            exner_to = exner(edge)
            exner_from = jnp.where(lane == 0, TOP_PRESSURE**EXNER_POWER, pltpu.roll(exner_to, 1, 1))
            layer = theta_next * (exner_to - exner_from)
            base_rows[slot, :, pl.ds(0, cols)] = lax.dot_general(
                below, layer, (((1,), (1,)), ((), ())), precision=HIGHEST, preferred_element_type=F32
            )
            spread[slot, :, pl.ds(0, cols)] = theta_next.T
            for step in range(peers):
                out = outs[step]
                start = pl.multiple_of(targets[step] * block, block)
                if tile < full:
                    out[place, pl.ds(tile * block, block), :] = spread[slot, pl.ds(start, block), :]
                else:
                    part = spread[slot, pl.ds(start, block), pl.ds(0, cols)]
                    out[place, pl.ds(full * block, half), :] = jnp.concatenate([part[:half], part[half:]], axis=1)
                out[place, pl.ds(data_rows + tile, 1), pl.ds(0, cols)] = surface_row
                out[place, pl.ds(data_rows + 8 + tile, 1), pl.ds(0, cols)] = base_rows[
                    slot, pl.ds(targets[step], 1), pl.ds(0, cols)
                ]


def below_sum(layer):
    rows, width = layer.shape
    groups = rows // 8
    carry = None
    pieces = []
    sub = lax.broadcasted_iota(jnp.int32, (8, width), 0)
    for g in reversed(range(groups)):
        x = layer[g * 8 : (g + 1) * 8]
        total = x
        for step in (1, 2, 4):
            total = total + jnp.where(sub < 8 - step, pltpu.roll(total, 8 - step, 0), 0.0)
        under = total - x
        if carry is not None:
            under = under + carry
            carry = carry + total[0:1]
        else:
            carry = total[0:1]
        pieces.append(under)
    return jnp.concatenate(pieces[::-1], axis=0)


def column_state(message, index, block, width, first_level, levels, ground):
    tiles = tile_count(width)
    data_rows = packed_rows(block, width)
    theta = jnp.concatenate([load_tile(message, index, block, width, t) for t in range(tiles)], axis=1)

    def line(first):
        return jnp.concatenate(
            [message[(*index, pl.ds(first + t, 1), pl.ds(0, min(LANES, width - t * LANES)))] for t in range(tiles)],
            axis=1,
        )

    surface = line(data_rows)
    base = line(data_rows + 8)
    sub = lax.broadcasted_iota(jnp.int32, (block, width), 0).astype(F32) + first_level
    thick = target_thickness(surface, sub, levels)
    top = exner(target_edges(surface, sub * (1.0 / levels)))
    bottom_edge = exner(target_edges(surface, (first_level + block) * (1.0 / levels)))
    sub_i = lax.broadcasted_iota(jnp.int32, (block, width), 0)
    bottom = jnp.where(sub_i == block - 1, bottom_edge, pltpu.roll(top, block - 1, 0))
    layer = theta * (bottom - top)
    geopot = (ground + base) + (below_sum(layer) + 0.5 * layer)
    return theta, thick, 0.5 * (top + bottom), geopot


def push(now, before):
    theta, exner_mid, geopot = now
    theta_b, exner_b, geopot_b = before
    return (geopot - geopot_b) + 0.5 * (theta + theta_b) * (exner_mid - exner_b)


def filtered(value, table, high, low, high_t, low_t, block):
    def product(x, b_high, b_low):
        x_high = x.astype(BF16)
        x_low = (x - x_high.astype(F32)).astype(BF16)
        dot = lambda a, b: jnp.dot(a, b, preferred_element_type=F32)
        return dot(x_high, b_high) + (dot(x_low, b_high) + dot(x_high, b_low))

    spectral = product(value, high, low)
    rows, width = value.shape
    spectral = (spectral.reshape(rows // block, block, width) * table[:, None, :]).reshape(rows, width)
    return value + product(spectral, high_t, low_t)


def gather_messages(me, parts, order):
    peers = len(parts)
    for step, part in enumerate(parts):
        owner = wrapped(me, (peers - step) % peers, peers)
        for place in range(part.shape[0]):
            order[owner * part.shape[0] + place] = part[place]


def copy_all(copies, sems):
    started = [pltpu.make_async_copy(source, target, sems.at[i]) for i, (source, target) in enumerate(copies)]
    for copy in started:
        copy.start()
    return started


def filter_rows(ref, count, table, tables, block):
    width = ref.shape[-1]
    value = ref[pl.ds(0, count)].reshape(count * block, width)
    value = filtered(value, table, *(t[...] for t in tables), block)
    ref[pl.ds(0, count)] = value.reshape(count, block, width)


def around(x):
    return jnp.roll(x, 1, axis=1)


def inner_final_kernel(
    levels, first, scalars, faces, p0, p1, p2, p3, ground, zonal, merid, table,
    high, low, high_t, low_t,
    zonal_out, merid_out, thick_out, theta_out, edge_states,
    order, zonal_s, merid_s, thick_s, theta_s, carried, sems,
):
    _, block, width = zonal.shape
    count = order.shape[0]
    level = scalars[0].astype(F32) * float(block)
    gather_messages(scalars[0], (p0, p1, p2, p3), order)

    def one_row(i, _):
        row = first + i
        theta, thick, mid, geopot = column_state(order, (i,), block, width, level, levels, ground[pl.ds(row, 1), :])
        theta_s[i] = theta
        thick_s[i] = thick
        now = (theta, mid, geopot)
        zonal_s[i] = zonal[row] - push(now, tuple(around(x) for x in now))
        before = (carried[0], carried[1], carried[2])
        merid_s[jnp.maximum(i - 1, 0)] = merid[row] - faces[row] * push(now, before)
        for field, x in enumerate(now):
            carried[field] = x

        @pl.when(i == 0)
        def _():
            for field, x in enumerate(now):
                edge_states[0, field] = x

        return 0

    carried[...] = jnp.zeros_like(carried)
    lax.fori_loop(0, count, one_row, 0)
    for field in range(3):
        edge_states[1, field] = carried[field]
    early = copy_all(
        [(theta_s, theta_out.at[pl.ds(first, count)]), (thick_s, thick_out.at[pl.ds(first, count)])],
        sems.at[pl.ds(0, 2)],
    )

    @pl.when(scalars[1] != 0)
    def _():
        tables = (high, low, high_t, low_t)
        filter_rows(zonal_s, count, table[pl.ds(first, count), :], tables, block)
        filter_rows(merid_s, count - 1, table[pl.ds(first + 1, count - 1), :], tables, block)

    late = copy_all(
        [
            (zonal_s, zonal_out.at[pl.ds(first, count)]),
            (merid_s.at[pl.ds(0, count - 1)], merid_out.at[pl.ds(first + 1, count - 1)]),
        ],
        sems.at[pl.ds(2, 2)],
    )
    for copy in early + late:
        copy.wait()


def outer_zonal_kernel(
    levels, scalars, p0, p1, p2, p3, ground, zonal, table, high, low, high_t, low_t, zonal_in, thick_in, theta_in,
    zonal_out, thick_out, theta_out, states, order, zonal_s, thick_s, theta_s, sems,
):
    del zonal_in, thick_in, theta_in
    lat_rows, block, width = zonal.shape
    count = order.shape[0]
    level = scalars[0].astype(F32) * float(block)
    gather_messages(scalars[0], (p0, p1, p2, p3), order)
    rows = [*range(count - 1), lat_rows - 1]
    for i, row in enumerate(rows):
        theta, thick, mid, geopot = column_state(order, (i,), block, width, level, levels, ground[pl.ds(row, 1), :])
        theta_s[i] = theta
        thick_s[i] = thick
        now = (theta, mid, geopot)
        zonal_s[i] = zonal[row] - push(now, tuple(around(x) for x in now))
        for field, x in enumerate(now):
            states[i, field] = x

    def out_copies(source, target):
        low = count - 1
        return [
            (source.at[pl.ds(0, low)], target.at[pl.ds(0, low)]),
            (source.at[pl.ds(low, 1)], target.at[pl.ds(lat_rows - 1, 1)]),
        ]

    early = copy_all(out_copies(theta_s, theta_out) + out_copies(thick_s, thick_out), sems.at[pl.ds(0, 4)])

    @pl.when(scalars[1] != 0)
    def _():
        picked = jnp.concatenate([table[pl.ds(0, count - 1), :], table[pl.ds(lat_rows - 1, 1), :]], axis=0)
        filter_rows(zonal_s, count, picked, (high, low, high_t, low_t), block)

    late = copy_all(out_copies(zonal_s, zonal_out), sems.at[pl.ds(4, 2)])
    for copy in early + late:
        copy.wait()


def outer_merid_kernel(
    levels, scalars, faces, south, halo_s, states, edge_states, merid, table, high, low, high_t, low_t, merid_in,
    merid_out, merid_s, sems,
):
    del merid_in
    lat_rows, block, width = merid.shape
    level = scalars[0].astype(F32) * float(block)
    outer = states.shape[0]
    theta, _, mid, geopot = column_state(
        south, (0,), block, width, level, levels, halo_s[pl.ds(2 * block, 1), :]
    )
    before = (theta, mid, geopot)
    fields = lambda ref, i: tuple(ref[i, f] for f in range(3))
    top = lat_rows - 1
    steps = [(i, fields(states, i)) for i in range(outer - 1)] + [(outer - 1, fields(edge_states, 0))]
    for row, now in steps:
        merid_s[row] = merid[row] - faces[row] * push(now, before)
        before = now
    merid_s[outer] = merid[top] - faces[top] * push(fields(states, outer - 1), fields(edge_states, 1))

    @pl.when(scalars[1] != 0)
    def _():
        picked = jnp.concatenate([table[pl.ds(0, outer), :], table[pl.ds(top, 1), :]], axis=0)
        filter_rows(merid_s, outer + 1, picked, (high, low, high_t, low_t), block)

    late = copy_all(
        [
            (merid_s.at[pl.ds(0, outer)], merid_out.at[pl.ds(0, outer)]),
            (merid_s.at[pl.ds(outer, 1)], merid_out.at[pl.ds(top, 1)]),
        ],
        sems,
    )
    for copy in late:
        copy.wait()


def exchanged(parts):
    peers = lax.axis_size("lev")
    return [parts[0]] + [
        lax.ppermute(parts[step], "lev", [(i, (i + step) % peers) for i in range(peers)]) for step in range(1, peers)
    ]


def body(
    zonal_wind, meridional_wind, thickness, potential_temp, surface_geo, polar_mask, cutoff, damping
):
    lat_rows, block, width = zonal_wind.shape
    lat_count = lax.axis_size("lat")
    peers = lax.axis_size("lev")
    levels = block * peers
    total_rows = lat_rows * lat_count
    first_row = lax.axis_index("lat") * lat_rows
    row_ids = (first_row + jnp.arange(lat_rows + 1, dtype=jnp.int32)).astype(F32)
    faces = jnp.sin(math.pi * row_ids / total_rows)
    centres = jnp.sin(math.pi * (row_ids[:-1] + 0.5) / total_rows)
    coef = jnp.stack([faces[:-1], faces[1:]]) * (0.5 * COURANT) / centres
    northward = [(i, i + 1) for i in range(lat_count - 1)]
    southward = [(i + 1, i) for i in range(lat_count - 1)]
    me = lax.axis_index("lev").astype(jnp.int32)
    scalars = jnp.stack([me, jnp.any(polar_mask != 0).astype(jnp.int32)])
    shape = lambda *dims: jax.ShapeDtypeStruct(dims, F32)

    inner_each = lat_rows // peers - 1
    inner = inner_each * peers
    first = peers - 1
    data_rows = packed_rows(block, width)
    message_rows = data_rows + 16

    *inner_sent, to_north, to_south = pl.pallas_call(
        lambda *refs: advect_inner_kernel(first, inner_each, *refs),
        out_shape=[shape(inner_each, 2, data_rows, LANES)] * peers
        + [shape(2 * block + 8, width), shape(3 * block, width)],
        in_specs=[SMEM] * 2 + [VMEM] * 5,
        out_specs=[VMEM] * (peers + 2),
        compiler_params=params(16),
        name="advect_inner",
    )(scalars, coef, zonal_wind, meridional_wind, thickness, potential_temp, surface_geo)
    inner_columns = exchanged(inner_sent)
    halo_s = lax.ppermute(to_north, "lat", northward)
    halo_n = lax.ppermute(to_south, "lat", southward)
    outer_sent = pl.pallas_call(
        advect_outer_kernel,
        out_shape=[shape(1, 2, data_rows, LANES)] * peers,
        in_specs=[SMEM] * 2 + [VMEM] * 6,
        out_specs=[VMEM] * peers,
        compiler_params=params(16),
        name="advect_outer",
    )(scalars, coef, zonal_wind, meridional_wind, thickness, potential_temp, halo_s, halo_n)
    outer_columns = exchanged(outer_sent)

    def remap(columns, each, name):
        return pl.pallas_call(
            lambda *refs: remap_kernel(width, block, *refs),
            out_shape=[shape(each, message_rows, LANES)] * peers,
            in_specs=[SMEM] + [VMEM] * peers,
            out_specs=[VMEM] * peers,
            scratch_shapes=[
                pltpu.VMEM((2, 2, levels, LANES), F32),
                pltpu.VMEM((2, levels, LANES), F32),
                pltpu.VMEM((2, 8, LANES), F32),
            ],
            compiler_params=params(16),
            name=name,
        )(scalars, *columns)

    inner_messages = exchanged(remap(inner_columns, inner_each, "remap_inner"))
    outer_messages = exchanged(remap(outer_columns, 1, "remap_outer"))

    high, low, wave = fourier_tables(width)
    active = (jnp.asarray(wave)[None, :] >= cutoff[:, None]) & (polar_mask[:, None] != 0)
    table = jnp.where(active, damping - 1.0, 0.0)
    tables = [jnp.asarray(x) for x in (high, low, np.ascontiguousarray(high.T), np.ascontiguousarray(low.T))]
    field = shape(lat_rows, block, width)
    hbm = pl.BlockSpec(memory_space=pltpu.HBM)
    rows_of = lambda n: pltpu.VMEM((n, block, width), F32)

    zonal_next, merid_next, thick_next, theta_next, edge_states = pl.pallas_call(
        lambda *refs: inner_final_kernel(levels, first, *refs),
        out_shape=[field] * 4 + [shape(2, 3, block, width)],
        in_specs=[SMEM] * 2 + [VMEM] * (peers + 8),
        out_specs=[hbm] * 4 + [VMEM],
        scratch_shapes=[pltpu.VMEM((inner, message_rows, LANES), F32)]
        + [rows_of(inner)] * 4
        + [rows_of(3), pltpu.SemaphoreType.DMA((4,))],
        compiler_params=params(24),
        name="final_inner",
    )(scalars, faces, *inner_messages, surface_geo, zonal_wind, meridional_wind, table, *tables)

    owner_of_last = peers - 1
    step_of_last = (me + peers - owner_of_last) % peers
    last_message = outer_messages[0]
    for step in range(1, peers):
        last_message = jnp.where(step_of_last == step, outer_messages[step], last_message)
    south = lax.ppermute(last_message, "lat", northward)

    outer = peers
    aliased = 2 + peers + 3 + 4 - 1
    zonal_next, thick_next, theta_next, states = pl.pallas_call(
        lambda *refs: outer_zonal_kernel(levels, *refs),
        out_shape=[field] * 3 + [shape(outer, 3, block, width)],
        in_specs=[SMEM] + [VMEM] * (peers + 7) + [hbm] * 3,
        out_specs=[hbm] * 3 + [VMEM],
        scratch_shapes=[pltpu.VMEM((outer, message_rows, LANES), F32)]
        + [rows_of(outer)] * 3
        + [pltpu.SemaphoreType.DMA((6,))],
        input_output_aliases={aliased: 0, aliased + 1: 1, aliased + 2: 2},
        compiler_params=params(16),
        name="final_outer_zonal",
    )(
        scalars, *outer_messages, surface_geo, zonal_wind, table, *tables, zonal_next, thick_next, theta_next
    )
    merid_next = pl.pallas_call(
        lambda *refs: outer_merid_kernel(levels, *refs),
        out_shape=field,
        in_specs=[SMEM] * 2 + [VMEM] * 10 + [hbm],
        out_specs=hbm,
        scratch_shapes=[rows_of(outer + 1), pltpu.SemaphoreType.DMA((2,))],
        input_output_aliases={12: 0},
        compiler_params=params(16),
        name="final_outer_merid",
    )(scalars, faces, south, halo_s, states, edge_states, meridional_wind, table, *tables, merid_next)
    return zonal_next, merid_next, thick_next, theta_next


def solution(mesh):
    field = P("lat", "lev", None)
    in_specs = (field, field, field, field, P("lat", None), P("lat"), P("lat"), P("lat", None))
    return jax.shard_map(body, mesh=mesh, in_specs=in_specs, out_specs=(field,) * 4, check_vma=False)
```

```python
import math

import jax
import jax.numpy as jnp
import numpy as np
from jax import lax
from jax.experimental import pallas as pl
from jax.experimental.pallas import tpu as pltpu
from jax.sharding import PartitionSpec as P

TOP_PRESSURE = 0.01
HYBRID_SCALE = 0.2
EXNER_POWER = 2.0 / 7.0
COURANT = 0.012
HIGHEST = lax.Precision.HIGHEST
F32 = jnp.float32
BF16 = jnp.bfloat16
VMEM = pl.BlockSpec(memory_space=pltpu.VMEM)
SMEM = pl.BlockSpec(memory_space=pltpu.SMEM)
LANES = 128


def params(mib):
    return pltpu.CompilerParams(vmem_limit_bytes=mib * 1024 * 1024)


def cost(microseconds):
    return pl.CostEstimate(
        flops=int(microseconds * 1.1e9), bytes_accessed=int(microseconds * 3.6e6), transcendentals=0
    )


def fourier_tables(count):
    middle = count // 2
    ids = np.arange(count)
    wave = np.where(ids <= middle, ids, ids - middle)
    angle = 2.0 * np.pi / count * (ids[:, None] * wave[None, :] % count)
    edge = (ids == 0) | (ids == middle)
    weight = np.where(edge, 1.0 / math.sqrt(count), math.sqrt(2.0 / count))
    basis = np.where((ids <= middle)[None, :], np.cos(angle), np.sin(angle)) * weight[None, :]
    basis = basis.astype(np.float32)
    high = basis.astype(jnp.bfloat16)
    low = (basis - high.astype(np.float32)).astype(jnp.bfloat16)
    return high, low, wave.astype(np.int32)


def packed_rows(rows, width):
    return rows * width // LANES


def store_packed(ref, index, value):
    rows, width = value.shape
    full = width // LANES
    for tile in range(full):
        ref[(*index, pl.ds(tile * rows, rows), slice(None))] = value[:, tile * LANES : (tile + 1) * LANES]
    if width % LANES:
        rest = value[:, full * LANES :]
        half = rows // 2
        ref[(*index, pl.ds(full * rows, half), slice(None))] = jnp.concatenate([rest[:half], rest[half:]], axis=1)


def load_tile(ref, index, rows, width, tile):
    full = width // LANES
    if tile < full:
        return ref[(*index, pl.ds(tile * rows, rows), slice(None))]
    half = rows // 2
    both = ref[(*index, pl.ds(full * rows, half), slice(None))]
    return jnp.concatenate([both[:, : LANES // 2], both[:, LANES // 2 :]], axis=0)


def tile_count(width):
    return -(-width // LANES)


def wrapped(me, step, peers):
    other = me + step
    return jnp.where(other >= peers, other - peers, other)


def advect_row(row, coef, zonal, merid, t, h, t_s, h_s, t_n, h_n, w_n):
    u = zonal * (0.5 * COURANT)
    w_n = w_n * coef[1, row]
    w_s = merid * coef[0, row]
    for x, x_s, x_n in ((t, t_s, t_n), (h, h_s, h_n)):
        flux = u * (x + jnp.roll(x, 1, axis=1))
        yield x - (jnp.roll(flux, -1, axis=1) - flux) - (w_n * (x_n + x) - w_s * (x + x_s))


def advect_inner_kernel(first, rows_each, peers, coef, *refs):
    sources, outs, held, sems = refs[:5], refs[5 : 5 + peers + 2], refs[-6:-1], refs[-1]
    for copy in copy_all(list(zip(sources, held)), sems):
        copy.wait()
    zonal, merid, thick, theta, ground = held
    lat_rows, levels, _ = thick.shape
    to_north, to_south = outs[peers:]
    me = lax.axis_index("lev")
    for step in range(peers):
        owner = wrapped(me, step, peers)
        for place in range(rows_each):
            row = first + owner * rows_each + place
            t, t_s, t_n = thick[row], thick[row - 1], thick[row + 1]
            h, h_s, h_n = theta[row] * t, theta[row - 1] * t_s, theta[row + 1] * t_n
            fields = advect_row(row, coef, zonal[row], merid[row], t, h, t_s, h_s, t_n, h_n, merid[row + 1])
            for field, new in enumerate(fields):
                store_packed(outs[step], (place, field), new)
    top = lat_rows - 1
    to_north[pl.ds(0, levels), :] = thick[top]
    to_north[pl.ds(levels, levels), :] = theta[top] * thick[top]
    to_north[pl.ds(2 * levels, 1), :] = ground[pl.ds(top, 1), :]
    to_south[pl.ds(0, levels), :] = thick[0]
    to_south[pl.ds(levels, levels), :] = theta[0] * thick[0]
    to_south[pl.ds(2 * levels, levels), :] = merid[0]


def ends_of(source, target, low, high):
    rows = source.shape[0]
    return [
        (source.at[pl.ds(0, low)], target.at[pl.ds(0, low)]),
        (source.at[pl.ds(rows - high, high)], target.at[pl.ds(low, high)]),
    ]


def advect_outer_kernel(peers, coef, *refs):
    sources, (halo_s, halo_n) = refs[:4], refs[4:6]
    outs, held, sems = refs[6 : 6 + peers], refs[-5:-1], refs[-1]
    lat_rows, levels, _ = sources[0].shape
    copies = []
    for source, target in zip(sources, held):
        copies += ends_of(source, target, peers, 2)
    for copy in copy_all(copies, sems):
        copy.wait()
    zonal, merid, thick, theta = held
    top = lat_rows - 1
    me = lax.axis_index("lev")
    for step in range(peers):
        owner = wrapped(me, step, peers)
        is_first, is_last = owner == 0, owner == peers - 1
        row = jnp.where(is_last, top, owner)
        at = jnp.where(is_last, peers + 1, owner)
        low, high = jnp.maximum(at - 1, 0), jnp.minimum(at + 1, peers + 1)
        t, t_s, t_n = thick[at], thick[low], thick[high]
        h, h_s, h_n = theta[at] * t, theta[low] * t_s, theta[high] * t_n
        part = lambda ref, i: ref[pl.ds(i * levels, levels), :]
        t_s = jnp.where(is_first, part(halo_s, 0), t_s)
        h_s = jnp.where(is_first, part(halo_s, 1), h_s)
        t_n = jnp.where(is_last, part(halo_n, 0), t_n)
        h_n = jnp.where(is_last, part(halo_n, 1), h_n)
        w_n = jnp.where(is_last, part(halo_n, 2), merid[high])
        fields = advect_row(row, coef, zonal[at], merid[at], t, h, t_s, h_s, t_n, h_n, w_n)
        for field, new in enumerate(fields):
            store_packed(outs[step], (0, field), new)


def target_edges(surface, sigma):
    curve = sigma * sigma
    return TOP_PRESSURE + HYBRID_SCALE * (sigma - curve) + (surface - TOP_PRESSURE) * curve


def target_thickness(surface, first, levels):
    step = 1.0 / levels
    curve = (2.0 * first + 1.0) * (step * step)
    return HYBRID_SCALE * (step - curve) + (surface - TOP_PRESSURE) * curve


def exner(pressure):
    return jnp.exp(EXNER_POWER * jnp.log(pressure))


def split_dot(x, ones):
    a = x.astype(BF16)
    r = x - a.astype(F32)
    b = r.astype(BF16)
    c = (r - b.astype(F32)).astype(BF16)
    dot = lambda v: jnp.dot(v, ones, preferred_element_type=F32)
    return dot(a) + (dot(b) + dot(c))

def remap_kernel(width, block, peers, *refs):
    parts = refs[:peers]
    gathered, spread, base_rows, base_s = refs[-4:]
    outs = refs[-4 - peers : -4]
    me = lax.axis_index("lev")
    count = parts[0].shape[0]
    levels = peers * block
    level_r = lax.broadcasted_iota(jnp.int32, (levels, levels), 0)
    level_c = lax.broadcasted_iota(jnp.int32, (levels, levels), 1)
    running = (level_r <= level_c).astype(F32).astype(BF16)
    below = (
        lax.broadcasted_iota(jnp.int32, (8, levels), 1)
        >= block * (1 + lax.broadcasted_iota(jnp.int32, (8, levels), 0))
    ).astype(F32)
    full = width // LANES
    data_rows = packed_rows(block, width)
    half = block // 2
    sources = [wrapped(me, (peers - step) % peers, peers) for step in range(peers)]
    targets = [wrapped(me, step, peers) for step in range(peers)]
    for place in range(count):
        for step in range(peers):
            at = pl.ds(pl.multiple_of(sources[step] * block, block), block)
            for field in range(2):
                for tile in range(tile_count(width)):
                    cols = min(LANES, width - tile * LANES)
                    gathered[place, field, at, pl.ds(tile * LANES, cols)] = load_tile(
                        parts[step], (place, field), block, width, tile)
    for place in range(count):
        cols = width
        here = pl.ds(0, cols)
        thick = gathered[place, 0, :, here]
        surface_row = TOP_PRESSURE + jnp.sum(thick, axis=0, keepdims=True)
        thick = thick.T
        heat = gathered[place, 1, :, here].T
        upper = TOP_PRESSURE + split_dot(thick, running)
        theta = heat / thick
        offset = split_dot(heat, running) - theta * upper
        surface = upper[:, levels - 1 :]
        lane = lax.broadcasted_iota(jnp.int32, (cols, levels), 1)
        lane_f = lane.astype(F32)
        edge = target_edges(surface, (lane_f + 1.0) * (1.0 / levels))
        at = jnp.zeros((cols, levels), jnp.int32)
        jump = levels // 2
        while jump:
            probe = jnp.take_along_axis(upper, at + (jump - 1), axis=1, mode="promise_in_bounds")
            at = jnp.where(probe < edge, at + jump, at)
            jump //= 2
        pick = lambda table: jnp.take_along_axis(table, at, axis=1, mode="promise_in_bounds")
        heat_to = pick(offset) + pick(theta) * edge
        heat_from = jnp.where(lane == 0, 0.0, pltpu.roll(heat_to, 1, 1))
        theta_next = (heat_to - heat_from) / target_thickness(surface, lane_f, levels)
        exner_to = exner(edge)
        exner_from = jnp.where(lane == 0, TOP_PRESSURE**EXNER_POWER, pltpu.roll(exner_to, 1, 1))
        layer = theta_next * (exner_to - exner_from)
        bases = lax.dot_general(
            below, layer, (((1,), (1,)), ((), ())), precision=HIGHEST, preferred_element_type=F32
        )
        base_s[place, :, here] = bases
        base_s[place, pl.ds(7, 1), here] = surface_row
        spread[place, :, here] = theta_next.T
    for place in range(count):
        for tile in range(tile_count(width)):
            base_rows[place, tile] = base_s[place, :, pl.ds(tile * LANES, LANES)]
        for step in range(peers):
            out = outs[step]
            start = pl.multiple_of(targets[step] * block, block)
            for tile in range(tile_count(width)):
                cols = min(LANES, width - tile * LANES)
                here = pl.ds(tile * LANES, cols)
                if tile < full:
                    out[place, pl.ds(tile * block, block), :] = spread[place, pl.ds(start, block), here]
                else:
                    part = spread[place, pl.ds(start, block), here]
                    out[place, pl.ds(full * block, half), :] = jnp.concatenate([part[:half], part[half:]], axis=1)
                out[place, pl.ds(data_rows + tile, 1), pl.ds(0, cols)] = base_rows[place, tile, pl.ds(7, 1), pl.ds(0, cols)]
                out[place, pl.ds(data_rows + 8 + tile, 1), pl.ds(0, cols)] = base_rows[place, tile, pl.ds(targets[step], 1), pl.ds(0, cols)]


def below_sum(layer):
    rows, width = layer.shape
    groups = rows // 8
    carry = None
    pieces = []
    sub = lax.broadcasted_iota(jnp.int32, (8, width), 0)
    for g in reversed(range(groups)):
        x = layer[g * 8 : (g + 1) * 8]
        total = x
        for step in (1, 2, 4):
            total = total + jnp.where(sub < 8 - step, pltpu.roll(total, 8 - step, 0), 0.0)
        under = total - x
        if carry is not None:
            under = under + carry
            carry = carry + total[0:1]
        else:
            carry = total[0:1]
        pieces.append(under)
    return jnp.concatenate(pieces[::-1], axis=0)


def column_state(message, index, block, width, first_level, levels, ground):
    tiles = tile_count(width)
    data_rows = packed_rows(block, width)
    theta = jnp.concatenate([load_tile(message, index, block, width, t) for t in range(tiles)], axis=1)

    def line(first):
        return jnp.concatenate(
            [message[(*index, pl.ds(first + t, 1), pl.ds(0, min(LANES, width - t * LANES)))] for t in range(tiles)],
            axis=1,
        )

    surface = line(data_rows)
    base = line(data_rows + 8)
    sub = lax.broadcasted_iota(jnp.int32, (block, width), 0).astype(F32) + first_level
    thick = target_thickness(surface, sub, levels)
    top = exner(target_edges(surface, sub * (1.0 / levels)))
    bottom_edge = exner(target_edges(surface, (first_level + block) * (1.0 / levels)))
    sub_i = lax.broadcasted_iota(jnp.int32, (block, width), 0)
    bottom = jnp.where(sub_i == block - 1, bottom_edge, pltpu.roll(top, block - 1, 0))
    layer = theta * (bottom - top)
    geopot = (ground + base) + (below_sum(layer) + 0.5 * layer)
    return theta, thick, 0.5 * (top + bottom), geopot


def push(now, before):
    theta, exner_mid, geopot = now
    theta_b, exner_b, geopot_b = before
    return (geopot - geopot_b) + 0.5 * (theta + theta_b) * (exner_mid - exner_b)


def filtered(value, table, high, low, high_t, low_t, block):
    def product(x, b_high, b_low):
        x_high = x.astype(BF16)
        x_low = (x - x_high.astype(F32)).astype(BF16)
        dot = lambda a, b: jnp.dot(a, b, preferred_element_type=F32)
        return dot(x_high, b_high) + (dot(x_low, b_high) + dot(x_high, b_low))

    spectral = product(value, high, low)
    rows, width = value.shape
    spectral = (spectral.reshape(rows // block, block, width) * table[:, None, :]).reshape(rows, width)
    return value + product(spectral, high_t, low_t)


def gather_messages(me, parts, order):
    peers = len(parts)
    for step, part in enumerate(parts):
        owner = wrapped(me, (peers - step) % peers, peers)
        for place in range(part.shape[0]):
            order[owner * part.shape[0] + place] = part[place]


def copy_all(copies, sems, first=0):
    started = [pltpu.make_async_copy(source, target, sems.at[first + i]) for i, (source, target) in enumerate(copies)]
    for copy in started:
        copy.start()
    return started


def wait_all(copies):
    for copy in copies:
        copy.wait()


def filter_rows(ref, count, table, tables, block):
    width = ref.shape[-1]
    value = ref[pl.ds(0, count)].reshape(count * block, width)
    value = filtered(value, table, *(t[...] for t in tables), block)
    ref[pl.ds(0, count)] = value.reshape(count, block, width)


def around(x):
    return jnp.roll(x, 1, axis=1)


def inner_final_kernel(
    levels, first, flag, faces, p0, p1, p2, p3, ground, table, zonal_h, merid_h, t0, t1, t2, t3, after,
    zonal_out, merid_out, thick_out, theta_out, edge_states,
    order, zonal, merid, zonal_s, merid_s, thick_s, theta_s, carried, b0, b1, b2, b3, sems,
):
    del after
    count, _, _ = zonal.shape
    _, block, width = zonal_h.shape
    inner = pl.ds(first, count)
    winds = copy_all([(zonal_h.at[inner], zonal), (merid_h.at[inner], merid)], sems)
    tables = (b0, b1, b2, b3)
    basis = copy_all(list(zip((t0, t1, t2, t3), tables)), sems, 2)
    me = lax.axis_index("lev")
    level = (me * block).astype(F32)
    gather_messages(me, (p0, p1, p2, p3), order)
    carried[...] = jnp.zeros_like(carried)
    wait_all(winds)

    def one_row(i, _):
        row = first + i
        theta, thick, mid, geopot = column_state(order, (i,), block, width, level, levels, ground[pl.ds(row, 1), :])
        theta_s[i] = theta
        thick_s[i] = thick
        now = (theta, mid, geopot)
        zonal_s[i] = zonal[i] - push(now, tuple(around(x) for x in now))
        before = (carried[0], carried[1], carried[2])
        merid_s[jnp.maximum(i - 1, 0)] = merid[i] - faces[row] * push(now, before)
        for field, x in enumerate(now):
            carried[field] = x

        @pl.when(i == 0)
        def _():
            for field, x in enumerate(now):
                edge_states[0, field] = x

        return 0

    lax.fori_loop(0, count, one_row, 0)
    for field in range(3):
        edge_states[1, field] = carried[field]
    early = copy_all([(theta_s, theta_out.at[inner]), (thick_s, thick_out.at[inner])], sems, 6)
    wait_all(basis)

    @pl.when(flag[0] != 0)
    def _():
        filter_rows(zonal_s, count, table[pl.ds(first, count), :], tables, block)
        filter_rows(merid_s, count - 1, table[pl.ds(first + 1, count - 1), :], tables, block)

    late = copy_all(
        [
            (zonal_s, zonal_out.at[inner]),
            (merid_s.at[pl.ds(0, count - 1)], merid_out.at[pl.ds(first + 1, count - 1)]),
        ],
        sems,
        8,
    )
    wait_all(early + late)


def rows_back(source, target, low):
    rows = target.shape[0]
    return [
        (source.at[pl.ds(0, low)], target.at[pl.ds(0, low)]),
        (source.at[pl.ds(low, 1)], target.at[pl.ds(rows - 1, 1)]),
    ]


def outer_zonal_kernel(
    levels, flag, p0, p1, p2, p3, ground, table, zonal_h, t0, t1, t2, t3, zonal_in, thick_in, theta_in,
    zonal_out, thick_out, theta_out, states,
    order, zonal, zonal_s, thick_s, theta_s, b0, b1, b2, b3, sems,
):
    del zonal_in, thick_in, theta_in
    lat_rows, block, width = zonal_h.shape
    count = order.shape[0]
    winds = copy_all(ends_of(zonal_h, zonal, count - 1, 1), sems)
    tables = (b0, b1, b2, b3)
    basis = copy_all(list(zip((t0, t1, t2, t3), tables)), sems, 2)
    me = lax.axis_index("lev")
    level = (me * block).astype(F32)
    gather_messages(me, (p0, p1, p2, p3), order)
    wait_all(winds)
    rows = [*range(count - 1), lat_rows - 1]
    for i, row in enumerate(rows):
        theta, thick, mid, geopot = column_state(order, (i,), block, width, level, levels, ground[pl.ds(row, 1), :])
        theta_s[i] = theta
        thick_s[i] = thick
        now = (theta, mid, geopot)
        zonal_s[i] = zonal[i] - push(now, tuple(around(x) for x in now))
        for field, x in enumerate(now):
            states[i, field] = x
    early = copy_all(rows_back(theta_s, theta_out, count - 1) + rows_back(thick_s, thick_out, count - 1), sems, 6)
    wait_all(basis)

    @pl.when(flag[0] != 0)
    def _():
        picked = jnp.concatenate([table[pl.ds(0, count - 1), :], table[pl.ds(lat_rows - 1, 1), :]], axis=0)
        filter_rows(zonal_s, count, picked, tables, block)

    late = copy_all(rows_back(zonal_s, zonal_out, count - 1), sems, 10)
    wait_all(early + late)


def outer_merid_kernel(
    levels, flag, faces, south, halo_s, states, edge_states, table, merid_h, t0, t1, t2, t3, merid_in,
    merid_out, merid, merid_s, b0, b1, b2, b3, sems,
):
    del merid_in
    lat_rows, block, width = merid_h.shape
    outer = states.shape[0]
    winds = copy_all(ends_of(merid_h, merid, outer, 1), sems)
    tables = (b0, b1, b2, b3)
    basis = copy_all(list(zip((t0, t1, t2, t3), tables)), sems, 2)
    level = (lax.axis_index("lev") * block).astype(F32)
    theta, _, mid, geopot = column_state(south, (0,), block, width, level, levels, halo_s[pl.ds(2 * block, 1), :])
    before = (theta, mid, geopot)
    fields = lambda ref, i: tuple(ref[i, f] for f in range(3))
    top = lat_rows - 1
    steps = [(i, fields(states, i)) for i in range(outer - 1)] + [(outer - 1, fields(edge_states, 0))]
    wait_all(winds)
    for row, now in steps:
        merid_s[row] = merid[row] - faces[row] * push(now, before)
        before = now
    merid_s[outer] = merid[outer] - faces[top] * push(fields(states, outer - 1), fields(edge_states, 1))
    wait_all(basis)

    @pl.when(flag[0] != 0)
    def _():
        picked = jnp.concatenate([table[pl.ds(0, outer), :], table[pl.ds(top, 1), :]], axis=0)
        filter_rows(merid_s, outer + 1, picked, tables, block)

    wait_all(copy_all(rows_back(merid_s, merid_out, outer), sems, 6))


def exchanged(parts):
    peers = lax.axis_size("lev")
    return [parts[0]] + [
        lax.ppermute(parts[step], "lev", [(i, (i + step) % peers) for i in range(peers)]) for step in range(1, peers)
    ]


def body(
    zonal_wind, meridional_wind, thickness, potential_temp, surface_geo, polar_mask, cutoff, damping
):
    lat_rows, block, width = zonal_wind.shape
    lat_count = lax.axis_size("lat")
    peers = lax.axis_size("lev")
    levels = block * peers
    total_rows = lat_rows * lat_count
    first_row = lax.axis_index("lat") * lat_rows
    row_ids = (first_row + jnp.arange(lat_rows + 1, dtype=jnp.int32)).astype(F32)
    faces = jnp.sin(math.pi * row_ids / total_rows)
    centres = jnp.sin(math.pi * (row_ids[:-1] + 0.5) / total_rows)
    coef = jnp.stack([faces[:-1], faces[1:]]) * (0.5 * COURANT) / centres
    northward = [(i, i + 1) for i in range(lat_count - 1)]
    southward = [(i + 1, i) for i in range(lat_count - 1)]
    flag = jnp.any(polar_mask != 0).astype(jnp.int32).reshape(1)
    shape = lambda *dims: jax.ShapeDtypeStruct(dims, F32)
    hbm = pl.BlockSpec(memory_space=pltpu.HBM)
    rows_of = lambda n: pltpu.VMEM((n, block, width), F32)
    dma = lambda n: pltpu.SemaphoreType.DMA((n,))

    inner_each = lat_rows // peers - 1
    inner = inner_each * peers
    outer, first = peers, peers - 1
    data_rows = packed_rows(block, width)
    message_rows = data_rows + 16
    stay = lambda *arrays: [pltpu.with_memory_space_constraint(x, pltpu.HBM) for x in arrays]
    winds_and_state = stay(zonal_wind, meridional_wind, thickness, potential_temp)
    ground_h, zonal_h, merid_h = stay(surface_geo, zonal_wind, meridional_wind)

    *inner_sent, to_north, to_south = pl.pallas_call(
        lambda *refs: advect_inner_kernel(first, inner_each, peers, *refs),
        out_shape=[shape(inner_each, 2, data_rows, LANES)] * peers
        + [shape(2 * block + 8, width), shape(3 * block, width)],
        in_specs=[SMEM] + [hbm] * 5,
        out_specs=[VMEM] * (peers + 2),
        scratch_shapes=[rows_of(lat_rows)] * 4 + [pltpu.VMEM((lat_rows, width), F32), dma(5)],
        compiler_params=params(12),
        cost_estimate=cost(5),
        name="advect_inner",
    )(coef, *winds_and_state, ground_h)
    inner_columns = exchanged(inner_sent)
    halo_s = lax.ppermute(to_north, "lat", northward)
    halo_n = lax.ppermute(to_south, "lat", southward)
    outer_sent = pl.pallas_call(
        lambda *refs: advect_outer_kernel(peers, *refs),
        out_shape=[shape(1, 2, data_rows, LANES)] * peers,
        in_specs=[SMEM] + [hbm] * 4 + [VMEM] * 2,
        out_specs=[VMEM] * peers,
        scratch_shapes=[rows_of(peers + 2)] * 4 + [dma(8)],
        compiler_params=params(12),
        cost_estimate=cost(3),
        name="advect_outer",
    )(coef, *winds_and_state, halo_s, halo_n)
    outer_columns = exchanged(outer_sent)

    def remap(columns, each, name, after):
        lanes = tile_count(width) * LANES
        return pl.pallas_call(
            lambda *refs: remap_kernel(width, block, peers, *refs),
            out_shape=[shape(each, message_rows, LANES)] * peers,
            in_specs=[VMEM] * peers + [pl.BlockSpec(memory_space=pl.ANY)] * len(after),
            out_specs=[VMEM] * peers,
            scratch_shapes=[
                pltpu.VMEM((each, 2, levels, lanes), F32),
                pltpu.VMEM((each, levels, lanes), F32),
                pltpu.VMEM((each, tile_count(width), 8, LANES), F32),
                pltpu.VMEM((each, 8, lanes), F32),
            ],
            compiler_params=params(12),
            cost_estimate=cost(1 + 3 * each),
            name=name,
        )(*columns, *after)

    inner_remapped = remap(inner_columns, inner_each, "remap_inner", [])
    inner_messages = exchanged(inner_remapped)
    outer_remapped = remap(outer_columns, 1, "remap_outer", inner_messages[1:2])
    outer_messages = exchanged(outer_remapped)

    high, low, wave = fourier_tables(width)
    active = (jnp.asarray(wave)[None, :] >= cutoff[:, None]) & (polar_mask[:, None] != 0)
    table = jnp.where(active, damping - 1.0, 0.0)
    tables = stay(*(jnp.asarray(x) for x in (high, low, np.ascontiguousarray(high.T), np.ascontiguousarray(low.T))))
    basis_scratch = [pltpu.VMEM((width, width), BF16)] * 4
    field = shape(lat_rows, block, width)

    zonal_next, merid_next, thick_next, theta_next, edge_states = pl.pallas_call(
        lambda *refs: inner_final_kernel(levels, first, *refs),
        out_shape=[field] * 4 + [shape(2, 3, block, width)],
        in_specs=[SMEM] * 2 + [VMEM] * (peers + 2) + [hbm] * 6 + [pl.BlockSpec(memory_space=pl.ANY)],
        out_specs=[hbm] * 4 + [VMEM],
        scratch_shapes=[pltpu.VMEM((inner, message_rows, LANES), F32)]
        + [rows_of(inner)] * 6
        + [rows_of(3), *basis_scratch, dma(10)],
        compiler_params=params(20),
        cost_estimate=cost(8),
        name="final_inner",
    )(
        flag, faces, *inner_messages, surface_geo, table, zonal_h, merid_h, *tables, outer_remapped[0]
    )

    edge_states, *outer_messages = lax.optimization_barrier((edge_states, *outer_messages))
    step_of_last = (lax.axis_index("lev") + 1) % peers
    last_message = outer_messages[0]
    for step in range(1, peers):
        last_message = jnp.where(step_of_last == step, outer_messages[step], last_message)
    south = lax.ppermute(last_message, "lat", northward)

    zonal_next, thick_next, theta_next, states = pl.pallas_call(
        lambda *refs: outer_zonal_kernel(levels, *refs),
        out_shape=[field] * 3 + [shape(outer, 3, block, width)],
        in_specs=[SMEM] + [VMEM] * (peers + 2) + [hbm] * 8,
        out_specs=[hbm] * 3 + [VMEM],
        scratch_shapes=[pltpu.VMEM((outer, message_rows, LANES), F32)]
        + [rows_of(outer)] * 4
        + [*basis_scratch, dma(12)],
        input_output_aliases={peers + 8: 0, peers + 9: 1, peers + 10: 2},
        compiler_params=params(16),
        cost_estimate=cost(4),
        name="final_outer_zonal",
    )(
        flag, *outer_messages, surface_geo, table, zonal_h, *tables, zonal_next, thick_next, theta_next
    )
    merid_next = pl.pallas_call(
        lambda *refs: outer_merid_kernel(levels, *refs),
        out_shape=field,
        in_specs=[SMEM] * 2 + [VMEM] * 5 + [hbm] * 6,
        out_specs=hbm,
        scratch_shapes=[rows_of(outer + 1)] * 2 + [*basis_scratch, dma(8)],
        input_output_aliases={12: 0},
        compiler_params=params(16),
        cost_estimate=cost(3),
        name="final_outer_merid",
    )(flag, faces, south, halo_s, states, edge_states, table, merid_h, *tables, merid_next)
    return zonal_next, merid_next, thick_next, theta_next


def solution(mesh):
    field = P("lat", "lev", None)
    in_specs = (field, field, field, field, P("lat", None), P("lat"), P("lat"), P("lat", None))
    return jax.shard_map(body, mesh=mesh, in_specs=in_specs, out_specs=(field,) * 4, check_vma=False)
```

```python
import math

import jax
import jax.numpy as jnp
import numpy as np
from jax import lax
from jax.experimental import pallas as pl
from jax.experimental.pallas import tpu as pltpu
from jax.sharding import PartitionSpec as P

TOP_PRESSURE = 0.01
HYBRID_SCALE = 0.2
EXNER_POWER = 2.0 / 7.0
COURANT = 0.012
HIGHEST = lax.Precision.HIGHEST
F32 = jnp.float32
BF16 = jnp.bfloat16
VMEM = pl.BlockSpec(memory_space=pltpu.VMEM)
SMEM = pl.BlockSpec(memory_space=pltpu.SMEM)
LANES = 128


def params(mib):
    return pltpu.CompilerParams(vmem_limit_bytes=mib * 1024 * 1024)


def cost(microseconds):
    return pl.CostEstimate(
        flops=int(microseconds * 1.1e9), bytes_accessed=int(microseconds * 3.6e6), transcendentals=0
    )


def fourier_tables(count):
    middle = count // 2
    ids = np.arange(count)
    wave = np.where(ids <= middle, ids, ids - middle)
    angle = 2.0 * np.pi / count * (ids[:, None] * wave[None, :] % count)
    edge = (ids == 0) | (ids == middle)
    weight = np.where(edge, 1.0 / math.sqrt(count), math.sqrt(2.0 / count))
    basis = np.where((ids <= middle)[None, :], np.cos(angle), np.sin(angle)) * weight[None, :]
    basis = basis.astype(np.float32)
    high = basis.astype(jnp.bfloat16)
    low = (basis - high.astype(np.float32)).astype(jnp.bfloat16)
    return high, low, wave.astype(np.int32)


def packed_rows(rows, width):
    return rows * width // LANES


def store_packed(ref, index, value):
    rows, width = value.shape
    full = width // LANES
    for tile in range(full):
        ref[(*index, pl.ds(tile * rows, rows), slice(None))] = value[:, tile * LANES : (tile + 1) * LANES]
    if width % LANES:
        rest = value[:, full * LANES :]
        half = rows // 2
        ref[(*index, pl.ds(full * rows, half), slice(None))] = jnp.concatenate([rest[:half], rest[half:]], axis=1)


def load_tile(ref, index, rows, width, tile):
    full = width // LANES
    if tile < full:
        return ref[(*index, pl.ds(tile * rows, rows), slice(None))]
    half = rows // 2
    both = ref[(*index, pl.ds(full * rows, half), slice(None))]
    return jnp.concatenate([both[:, : LANES // 2], both[:, LANES // 2 :]], axis=0)


def tile_count(width):
    return -(-width // LANES)


def wrapped(me, step, peers):
    other = me + step
    return jnp.where(other >= peers, other - peers, other)


def advect_row(row, coef, zonal, merid, t, h, t_s, h_s, t_n, h_n, w_n):
    u = zonal * (0.5 * COURANT)
    w_n = w_n * coef[1, row]
    w_s = merid * coef[0, row]
    for x, x_s, x_n in ((t, t_s, t_n), (h, h_s, h_n)):
        flux = u * (x + jnp.roll(x, 1, axis=1))
        yield x - (jnp.roll(flux, -1, axis=1) - flux) - (w_n * (x_n + x) - w_s * (x + x_s))


def edges_kernel(merid, thick, theta, ground, to_north, to_south, thick_s, theta_s, merid_s, ground_s, sems):
    lat_rows, levels, _ = thick.shape
    top = lat_rows - 1
    copies = []
    for source, target in ((thick, thick_s), (theta, theta_s)):
        copies += [(source.at[pl.ds(0, 1)], target.at[pl.ds(0, 1)]), (source.at[pl.ds(top, 1)], target.at[pl.ds(1, 1)])]
    wait_all(copy_all([*copies, (merid.at[pl.ds(0, 1)], merid_s), (ground, ground_s)], sems))
    to_north[pl.ds(0, levels), :] = thick_s[1]
    to_north[pl.ds(levels, levels), :] = theta_s[1] * thick_s[1]
    to_north[pl.ds(2 * levels, 1), :] = ground_s[pl.ds(top, 1), :]
    to_south[pl.ds(0, levels), :] = thick_s[0]
    to_south[pl.ds(levels, levels), :] = theta_s[0] * thick_s[0]
    to_south[pl.ds(2 * levels, levels), :] = merid_s[0]


def advect_kernel(first, rows_each, peers, coef, halo, *refs):
    fields, outs, held, sems = refs[:4], refs[4 : 4 + peers], refs[4 + peers : -1], refs[-1]
    lat_rows, levels, _ = fields[0].shape
    top = lat_rows - 1
    me = lax.axis_index("lev")
    part = lambda i: halo[pl.ds(i * levels, levels), :]
    owned = [first + wrapped(me, step, peers) * rows_each for step in range(peers)]
    reach = ((0, rows_each), (0, rows_each + 1), (1, rows_each + 2), (1, rows_each + 2))
    starts = [[jnp.clip(row - before, 0, lat_rows - count) for before, count in reach] for row in owned]
    arriving = [
        copy_all(
            [
                (field.at[pl.ds(start, count)], target.at[step])
                for field, target, start, (_, count) in zip(fields, held, starts[step], reach)
            ],
            sems,
            4 * step,
        )
        for step in range(peers)
    ]
    for step in range(peers):
        wait_all(arriving[step])
        zonal, merid, thick, theta = (ref.at[step] for ref in held)
        z_at, w_at, t_at, _ = (owned[step] - start for start in starts[step])
        for place in range(rows_each):
            row = owned[step] + place
            at = t_at + place
            low, high = jnp.maximum(at - 1, 0), jnp.minimum(at + 1, rows_each + 1)
            t, t_s, t_n = thick[at], thick[low], thick[high]
            h, h_s, h_n = theta[at] * t, theta[low] * t_s, theta[high] * t_n
            w, w_n = merid[w_at + place], merid[jnp.minimum(w_at + place + 1, rows_each)]
            if first == 0 and place == 0:
                t_s = jnp.where(row == 0, part(0), t_s)
                h_s = jnp.where(row == 0, part(1), h_s)
            if first + peers * rows_each == lat_rows and place == rows_each - 1:
                t_n = jnp.where(row == top, part(0), t_n)
                h_n = jnp.where(row == top, part(1), h_n)
                w_n = jnp.where(row == top, part(2), w_n)
            fields_new = advect_row(row, coef, zonal[z_at + place], w, t, h, t_s, h_s, t_n, h_n, w_n)
            for field, new in enumerate(fields_new):
                store_packed(outs[step], (place, field), new)


def target_edges(surface, sigma):
    curve = sigma * sigma
    return TOP_PRESSURE + HYBRID_SCALE * (sigma - curve) + (surface - TOP_PRESSURE) * curve


def target_thickness(surface, first, levels):
    step = 1.0 / levels
    curve = (2.0 * first + 1.0) * (step * step)
    return HYBRID_SCALE * (step - curve) + (surface - TOP_PRESSURE) * curve


def exner(pressure):
    return jnp.exp(EXNER_POWER * jnp.log(pressure))


def split_dot(x, ones):
    a = x.astype(BF16)
    r = x - a.astype(F32)
    b = r.astype(BF16)
    c = (r - b.astype(F32)).astype(BF16)
    dot = lambda v: jnp.dot(v, ones, preferred_element_type=F32)
    return dot(a) + (dot(b) + dot(c))

def remap_kernel(width, block, peers, *refs):
    parts = refs[:peers]
    gathered, spread, base_rows, base_s = refs[-4:]
    outs = refs[-4 - peers : -4]
    me = lax.axis_index("lev")
    count = parts[0].shape[0]
    levels = peers * block
    level_r = lax.broadcasted_iota(jnp.int32, (levels, levels), 0)
    level_c = lax.broadcasted_iota(jnp.int32, (levels, levels), 1)
    running = (level_r <= level_c).astype(F32).astype(BF16)
    below = (
        lax.broadcasted_iota(jnp.int32, (8, levels), 1)
        >= block * (1 + lax.broadcasted_iota(jnp.int32, (8, levels), 0))
    ).astype(F32)
    full = width // LANES
    data_rows = packed_rows(block, width)
    half = block // 2
    sources = [wrapped(me, (peers - step) % peers, peers) for step in range(peers)]
    targets = [wrapped(me, step, peers) for step in range(peers)]
    for place in range(count):
        for step in range(peers):
            at = pl.ds(pl.multiple_of(sources[step] * block, block), block)
            for field in range(2):
                for tile in range(tile_count(width)):
                    cols = min(LANES, width - tile * LANES)
                    gathered[place, field, at, pl.ds(tile * LANES, cols)] = load_tile(
                        parts[step], (place, field), block, width, tile)
    for place in range(count):
        cols = width
        here = pl.ds(0, cols)
        thick = gathered[place, 0, :, here]
        surface_row = TOP_PRESSURE + jnp.sum(thick, axis=0, keepdims=True)
        thick = thick.T
        heat = gathered[place, 1, :, here].T
        upper = TOP_PRESSURE + split_dot(thick, running)
        theta = heat / thick
        offset = split_dot(heat, running) - theta * upper
        surface = upper[:, levels - 1 :]
        lane = lax.broadcasted_iota(jnp.int32, (cols, levels), 1)
        lane_f = lane.astype(F32)
        edge = target_edges(surface, (lane_f + 1.0) * (1.0 / levels))
        at = jnp.zeros((cols, levels), jnp.int32)
        jump = levels // 2
        while jump:
            probe = jnp.take_along_axis(upper, at + (jump - 1), axis=1, mode="promise_in_bounds")
            at = jnp.where(probe < edge, at + jump, at)
            jump //= 2
        pick = lambda table: jnp.take_along_axis(table, at, axis=1, mode="promise_in_bounds")
        heat_to = pick(offset) + pick(theta) * edge
        heat_from = jnp.where(lane == 0, 0.0, pltpu.roll(heat_to, 1, 1))
        theta_next = (heat_to - heat_from) / target_thickness(surface, lane_f, levels)
        exner_to = exner(edge)
        exner_from = jnp.where(lane == 0, TOP_PRESSURE**EXNER_POWER, pltpu.roll(exner_to, 1, 1))
        layer = theta_next * (exner_to - exner_from)
        bases = lax.dot_general(
            below, layer, (((1,), (1,)), ((), ())), precision=HIGHEST, preferred_element_type=F32
        )
        base_s[place, :, here] = bases
        base_s[place, pl.ds(7, 1), here] = surface_row
        spread[place, :, here] = theta_next.T
    for place in range(count):
        for tile in range(tile_count(width)):
            base_rows[place, tile] = base_s[place, :, pl.ds(tile * LANES, LANES)]
        for step in range(peers):
            out = outs[step]
            start = pl.multiple_of(targets[step] * block, block)
            for tile in range(tile_count(width)):
                cols = min(LANES, width - tile * LANES)
                here = pl.ds(tile * LANES, cols)
                if tile < full:
                    out[place, pl.ds(tile * block, block), :] = spread[place, pl.ds(start, block), here]
                else:
                    part = spread[place, pl.ds(start, block), here]
                    out[place, pl.ds(full * block, half), :] = jnp.concatenate([part[:half], part[half:]], axis=1)
                out[place, pl.ds(data_rows + tile, 1), pl.ds(0, cols)] = base_rows[place, tile, pl.ds(7, 1), pl.ds(0, cols)]
                out[place, pl.ds(data_rows + 8 + tile, 1), pl.ds(0, cols)] = base_rows[place, tile, pl.ds(targets[step], 1), pl.ds(0, cols)]


def below_sum(layer):
    rows, width = layer.shape
    groups = rows // 8
    carry = None
    pieces = []
    sub = lax.broadcasted_iota(jnp.int32, (8, width), 0)
    for g in reversed(range(groups)):
        x = layer[g * 8 : (g + 1) * 8]
        total = x
        for step in (1, 2, 4):
            total = total + jnp.where(sub < 8 - step, pltpu.roll(total, 8 - step, 0), 0.0)
        under = total - x
        if carry is not None:
            under = under + carry
            carry = carry + total[0:1]
        else:
            carry = total[0:1]
        pieces.append(under)
    return jnp.concatenate(pieces[::-1], axis=0)


def column_state(message, index, block, width, first_level, levels, ground):
    tiles = tile_count(width)
    data_rows = packed_rows(block, width)
    theta = jnp.concatenate([load_tile(message, index, block, width, t) for t in range(tiles)], axis=1)

    def line(first):
        return jnp.concatenate(
            [message[(*index, pl.ds(first + t, 1), pl.ds(0, min(LANES, width - t * LANES)))] for t in range(tiles)],
            axis=1,
        )

    surface = line(data_rows)
    base = line(data_rows + 8)
    sub = lax.broadcasted_iota(jnp.int32, (block, width), 0).astype(F32) + first_level
    thick = target_thickness(surface, sub, levels)
    top = exner(target_edges(surface, sub * (1.0 / levels)))
    bottom_edge = exner(target_edges(surface, (first_level + block) * (1.0 / levels)))
    sub_i = lax.broadcasted_iota(jnp.int32, (block, width), 0)
    bottom = jnp.where(sub_i == block - 1, bottom_edge, pltpu.roll(top, block - 1, 0))
    layer = theta * (bottom - top)
    geopot = (ground + base) + (below_sum(layer) + 0.5 * layer)
    return theta, thick, 0.5 * (top + bottom), geopot


def push(now, before):
    theta, exner_mid, geopot = now
    theta_b, exner_b, geopot_b = before
    return (geopot - geopot_b) + 0.5 * (theta + theta_b) * (exner_mid - exner_b)


def filtered(value, table, high, low, high_t, low_t, block):
    def product(x, b_high, b_low):
        x_high = x.astype(BF16)
        x_low = (x - x_high.astype(F32)).astype(BF16)
        dot = lambda a, b: jnp.dot(a, b, preferred_element_type=F32)
        return dot(x_high, b_high) + (dot(x_low, b_high) + dot(x_high, b_low))

    spectral = product(value, high, low)
    rows, width = value.shape
    spectral = (spectral.reshape(rows // block, block, width) * table[:, None, :]).reshape(rows, width)
    return value + product(spectral, high_t, low_t)


def gather_messages(me, parts, order):
    peers = len(parts)
    for step, part in enumerate(parts):
        owner = wrapped(me, (peers - step) % peers, peers)
        for place in range(part.shape[0]):
            order[owner * part.shape[0] + place] = part[place]


def copy_all(copies, sems, first=0):
    started = [pltpu.make_async_copy(source, target, sems.at[first + i]) for i, (source, target) in enumerate(copies)]
    for copy in started:
        copy.start()
    return started


def wait_all(copies):
    for copy in copies:
        copy.wait()


def filter_rows(ref, count, table, tables, block):
    width = ref.shape[-1]
    value = ref[pl.ds(0, count)].reshape(count * block, width)
    value = filtered(value, table, *(t[...] for t in tables), block)
    ref[pl.ds(0, count)] = value.reshape(count, block, width)


def around(x):
    return jnp.roll(x, 1, axis=1)


def upper_final_kernel(
    levels, first, flag, faces, p0, p1, p2, p3, ground, table, zonal, merid, b0, b1, b2, b3, after,
    zonal_out, merid_out, thick_out, theta_out, edge_state,
    order, zonal_s, merid_s, thick_s, theta_s, carried, sems,
):
    del after
    lat_rows, block, width = zonal.shape
    count = lat_rows - first
    rows = pl.ds(first, count)
    me = lax.axis_index("lev")
    level = (me * block).astype(F32)
    gather_messages(me, (p0, p1, p2, p3), order)
    carried[...] = jnp.zeros_like(carried)

    def one_row(i, _):
        row = first + i
        theta, thick, mid, geopot = column_state(order, (i,), block, width, level, levels, ground[pl.ds(row, 1), :])
        theta_s[i] = theta
        thick_s[i] = thick
        now = (theta, mid, geopot)
        zonal_s[i] = zonal[row] - push(now, tuple(around(x) for x in now))
        before = (carried[0], carried[1], carried[2])
        merid_s[jnp.maximum(i - 1, 0)] = merid[row] - faces[row] * push(now, before)
        for field, x in enumerate(now):
            carried[field] = x

        @pl.when(i == 0)
        def _():
            for field, x in enumerate(now):
                edge_state[field] = x

        return 0

    lax.fori_loop(0, count, one_row, 0)
    early = copy_all([(theta_s, theta_out.at[rows]), (thick_s, thick_out.at[rows])], sems)

    @pl.when(flag[0] != 0)
    def _():
        tables = (b0, b1, b2, b3)
        filter_rows(zonal_s, count, table[rows, :], tables, block)
        filter_rows(merid_s, count - 1, table[pl.ds(first + 1, count - 1), :], tables, block)

    late = copy_all(
        [
            (zonal_s, zonal_out.at[rows]),
            (merid_s.at[pl.ds(0, count - 1)], merid_out.at[pl.ds(first + 1, count - 1)]),
        ],
        sems,
        2,
    )
    wait_all(early + late)


def lower_final_kernel(
    levels, flag, faces, south, halo_s, edge_state, p0, p1, p2, p3, ground, table, zonal, merid, b0, b1, b2, b3,
    zonal_in, merid_in, thick_in, theta_in,
    zonal_out, merid_out, thick_out, theta_out,
    order, winds_s, thick_s, theta_s, sems,
):
    del zonal_in, merid_in, thick_in, theta_in
    count = order.shape[0]
    _, block, width = zonal.shape
    me = lax.axis_index("lev")
    level = (me * block).astype(F32)
    gather_messages(me, (p0, p1, p2, p3), order)
    state = lambda ref, i, line: column_state(ref, (i,), block, width, level, levels, line)
    theta, _, mid, geopot = state(south, 0, halo_s[pl.ds(2 * block, 1), :])
    before = (theta, mid, geopot)
    for row in range(count):
        theta, thick, mid, geopot = state(order, row, ground[pl.ds(row, 1), :])
        theta_s[row] = theta
        thick_s[row] = thick
        now = (theta, mid, geopot)
        winds_s[row] = zonal[row] - push(now, tuple(around(x) for x in now))
        winds_s[count + row] = merid[row] - faces[row] * push(now, before)
        before = now
    now = tuple(edge_state[field] for field in range(3))
    winds_s[2 * count] = merid[count] - faces[count] * push(now, before)
    rows = pl.ds(0, count)
    early = copy_all([(theta_s, theta_out.at[rows]), (thick_s, thick_out.at[rows])], sems)

    @pl.when(flag[0] != 0)
    def _():
        picked = jnp.concatenate([table[rows, :], table[pl.ds(0, count + 1), :]], axis=0)
        filter_rows(winds_s, 2 * count + 1, picked, (b0, b1, b2, b3), block)

    late = copy_all(
        [
            (winds_s.at[rows], zonal_out.at[rows]),
            (winds_s.at[pl.ds(count, count + 1)], merid_out.at[pl.ds(0, count + 1)]),
        ],
        sems,
        2,
    )
    wait_all(early + late)


def exchanged(parts):
    peers = lax.axis_size("lev")
    return [parts[0]] + [
        lax.ppermute(parts[step], "lev", [(i, (i + step) % peers) for i in range(peers)]) for step in range(1, peers)
    ]


def body(
    zonal_wind, meridional_wind, thickness, potential_temp, surface_geo, polar_mask, cutoff, damping
):
    lat_rows, block, width = zonal_wind.shape
    lat_count = lax.axis_size("lat")
    peers = lax.axis_size("lev")
    levels = block * peers
    total_rows = lat_rows * lat_count
    first_row = lax.axis_index("lat") * lat_rows
    row_ids = (first_row + jnp.arange(lat_rows + 1, dtype=jnp.int32)).astype(F32)
    faces = jnp.sin(math.pi * row_ids / total_rows)
    centres = jnp.sin(math.pi * (row_ids[:-1] + 0.5) / total_rows)
    coef = jnp.stack([faces[:-1], faces[1:]]) * (0.5 * COURANT) / centres
    northward = [(i, i + 1) for i in range(lat_count - 1)]
    southward = [(i + 1, i) for i in range(lat_count - 1)]
    flag = jnp.any(polar_mask != 0).astype(jnp.int32).reshape(1)
    shape = lambda *dims: jax.ShapeDtypeStruct(dims, F32)
    hbm = pl.BlockSpec(memory_space=pltpu.HBM)
    rows_of = lambda n: pltpu.VMEM((n, block, width), F32)
    dma = lambda n: pltpu.SemaphoreType.DMA((n,))

    lower_each = 1
    upper_each = lat_rows // peers - lower_each
    first = lower_each * peers
    upper = lat_rows - first
    data_rows = packed_rows(block, width)
    message_rows = data_rows + 16
    stay = lambda *arrays: [pltpu.with_memory_space_constraint(x, pltpu.HBM) for x in arrays]
    field = shape(lat_rows, block, width)

    fields = stay(zonal_wind, meridional_wind, thickness, potential_temp)
    to_north, to_south = pl.pallas_call(
        edges_kernel,
        out_shape=[shape(2 * block + 8, width), shape(3 * block, width)],
        in_specs=[hbm] * 4,
        out_specs=[VMEM] * 2,
        scratch_shapes=[rows_of(2), rows_of(2), rows_of(1), pltpu.VMEM((lat_rows, width), F32), dma(6)],
        compiler_params=params(8),
        cost_estimate=cost(1),
        name="edges",
    )(*fields[1:], *stay(surface_geo))
    halo_n = lax.ppermute(to_south, "lat", southward)
    halo_s = lax.ppermute(to_north, "lat", northward)

    def advect(start, each, halo, name):
        return pl.pallas_call(
            lambda *refs: advect_kernel(start, each, peers, *refs),
            out_shape=[shape(each, 2, data_rows, LANES)] * peers,
            in_specs=[SMEM, VMEM] + [hbm] * 4,
            out_specs=[VMEM] * peers,
            scratch_shapes=[
                pltpu.VMEM((peers, each + extra, block, width), F32) for extra in (0, 1, 2, 2)
            ]
            + [dma(4 * peers)],
            compiler_params=params(12),
            cost_estimate=cost(1 + 2 * each),
            name=name,
        )(coef, halo, *fields)

    upper_columns = exchanged(advect(first, upper_each, halo_n, "advect_upper"))
    lower_columns = exchanged(advect(0, lower_each, halo_s, "advect_lower"))

    def remap(columns, each, name, after):
        lanes = tile_count(width) * LANES
        return pl.pallas_call(
            lambda *refs: remap_kernel(width, block, peers, *refs),
            out_shape=[shape(each, message_rows, LANES)] * peers,
            in_specs=[VMEM] * peers + [pl.BlockSpec(memory_space=pl.ANY)] * len(after),
            out_specs=[VMEM] * peers,
            scratch_shapes=[
                pltpu.VMEM((each, 2, levels, lanes), F32),
                pltpu.VMEM((each, levels, lanes), F32),
                pltpu.VMEM((each, tile_count(width), 8, LANES), F32),
                pltpu.VMEM((each, 8, lanes), F32),
            ],
            compiler_params=params(12),
            cost_estimate=cost(1 + 3 * each),
            name=name,
        )(*columns, *after)

    upper_remapped = remap(upper_columns, upper_each, "remap_upper", lower_columns[:1])
    upper_messages = exchanged(upper_remapped)
    lower_remapped = remap(lower_columns, lower_each, "remap_lower", upper_messages[1:2])
    lower_messages = exchanged(lower_remapped)
    step_of_last = (lax.axis_index("lev") + 1) % peers
    _, *candidates = lax.optimization_barrier((lower_remapped[0], *upper_messages))
    last_message = candidates[0][-1:]
    for step in range(1, peers):
        last_message = jnp.where(step_of_last == step, candidates[step][-1:], last_message)
    south = lax.ppermute(last_message, "lat", northward)

    high, low, wave = fourier_tables(width)
    active = (jnp.asarray(wave)[None, :] >= cutoff[:, None]) & (polar_mask[:, None] != 0)
    table = jnp.where(active, damping - 1.0, 0.0)
    tables = [jnp.asarray(x) for x in (high, low, np.ascontiguousarray(high.T), np.ascontiguousarray(low.T))]

    *partial, edge_state = pl.pallas_call(
        lambda *refs: upper_final_kernel(levels, first, *refs),
        out_shape=[field] * 4 + [shape(3, block, width)],
        in_specs=[SMEM] * 2 + [VMEM] * (peers + 8) + [pl.BlockSpec(memory_space=pl.ANY)],
        out_specs=[hbm] * 4 + [VMEM],
        scratch_shapes=[pltpu.VMEM((upper, message_rows, LANES), F32)]
        + [rows_of(upper)] * 4
        + [rows_of(3), dma(4)],
        compiler_params=params(18),
        cost_estimate=cost(7),
        name="final_upper",
    )(
        flag, faces, *upper_messages, surface_geo, table, zonal_wind, meridional_wind, *tables, lower_remapped[0]
    )
    edge_state, *lower_messages = lax.optimization_barrier((edge_state, *lower_messages))
    return tuple(
        pl.pallas_call(
            lambda *refs: lower_final_kernel(levels, *refs),
            out_shape=[field] * 4,
            in_specs=[SMEM] * 2 + [VMEM] * (peers + 11) + [hbm] * 4,
            out_specs=[hbm] * 4,
            scratch_shapes=[pltpu.VMEM((first, message_rows, LANES), F32)]
            + [rows_of(2 * first + 1), rows_of(first), rows_of(first), dma(4)],
            input_output_aliases={peers + 13 + i: i for i in range(4)},
            compiler_params=params(16),
            cost_estimate=cost(6),
            name="final_lower",
        )(
            flag, faces, south, halo_s, edge_state, *lower_messages, surface_geo, table, zonal_wind, meridional_wind, *tables,
            *partial,
        )
    )


def solution(mesh):
    field = P("lat", "lev", None)
    in_specs = (field, field, field, field, P("lat", None), P("lat"), P("lat"), P("lat", None))
    return jax.shard_map(body, mesh=mesh, in_specs=in_specs, out_specs=(field,) * 4, check_vma=False)
```

```python
import math

import jax
import jax.numpy as jnp
import numpy as np
from jax import lax
from jax.experimental import pallas as pl
from jax.experimental.pallas import tpu as pltpu
from jax.sharding import PartitionSpec as P

TOP_PRESSURE = 0.01
HYBRID_SCALE = 0.2
EXNER_POWER = 2.0 / 7.0
COURANT = 0.012
HIGHEST = lax.Precision.HIGHEST
F32 = jnp.float32
BF16 = jnp.bfloat16
VMEM = pl.BlockSpec(memory_space=pltpu.VMEM)
SMEM = pl.BlockSpec(memory_space=pltpu.SMEM)
LANES = 128


def params(mib):
    return pltpu.CompilerParams(vmem_limit_bytes=mib * 1024 * 1024)


def cost(microseconds):
    return pl.CostEstimate(
        flops=int(microseconds * 1.1e9), bytes_accessed=int(microseconds * 3.6e6), transcendentals=0
    )


def fourier_tables(count):
    middle = count // 2
    ids = np.arange(count)
    wave = np.where(ids <= middle, ids, ids - middle)
    angle = 2.0 * np.pi / count * (ids[:, None] * wave[None, :] % count)
    edge = (ids == 0) | (ids == middle)
    weight = np.where(edge, 1.0 / math.sqrt(count), math.sqrt(2.0 / count))
    basis = np.where((ids <= middle)[None, :], np.cos(angle), np.sin(angle)) * weight[None, :]
    basis = basis.astype(np.float32)
    high = basis.astype(jnp.bfloat16)
    low = (basis - high.astype(np.float32)).astype(jnp.bfloat16)
    return high, low, wave.astype(np.int32)


def packed_rows(rows, width):
    return rows * width // LANES


def store_packed(ref, index, value):
    rows, width = value.shape
    full = width // LANES
    for tile in range(full):
        ref[(*index, pl.ds(tile * rows, rows), slice(None))] = value[:, tile * LANES : (tile + 1) * LANES]
    if width % LANES:
        rest = value[:, full * LANES :]
        half = rows // 2
        ref[(*index, pl.ds(full * rows, half), slice(None))] = jnp.concatenate([rest[:half], rest[half:]], axis=1)


def load_tile(ref, index, rows, width, tile):
    full = width // LANES
    if tile < full:
        return ref[(*index, pl.ds(tile * rows, rows), slice(None))]
    half = rows // 2
    both = ref[(*index, pl.ds(full * rows, half), slice(None))]
    return jnp.concatenate([both[:, : LANES // 2], both[:, LANES // 2 :]], axis=0)


def tile_count(width):
    return -(-width // LANES)


def wrapped(me, step, peers):
    other = me + step
    return jnp.where(other >= peers, other - peers, other)


def advect_row(row, coef, zonal, merid, t, h, t_s, h_s, t_n, h_n, w_n):
    u = zonal * (0.5 * COURANT)
    w_n = w_n * coef[1, row]
    w_s = merid * coef[0, row]
    for x, x_s, x_n in ((t, t_s, t_n), (h, h_s, h_n)):
        flux = u * (x + jnp.roll(x, 1, axis=1))
        yield x - (jnp.roll(flux, -1, axis=1) - flux) - (w_n * (x_n + x) - w_s * (x + x_s))


def edges_kernel(merid, thick, theta, ground, to_north, to_south, thick_s, theta_s, merid_s, ground_s, sems):
    lat_rows, levels, _ = thick.shape
    top = lat_rows - 1
    copies = []
    for source, target in ((thick, thick_s), (theta, theta_s)):
        copies += [(source.at[pl.ds(0, 1)], target.at[pl.ds(0, 1)]), (source.at[pl.ds(top, 1)], target.at[pl.ds(1, 1)])]
    wait_all(copy_all([*copies, (merid.at[pl.ds(0, 1)], merid_s), (ground, ground_s)], sems))
    to_north[pl.ds(0, levels), :] = thick_s[1]
    to_north[pl.ds(levels, levels), :] = theta_s[1] * thick_s[1]
    to_north[pl.ds(2 * levels, 1), :] = ground_s[pl.ds(top, 1), :]
    to_south[pl.ds(0, levels), :] = thick_s[0]
    to_south[pl.ds(levels, levels), :] = theta_s[0] * thick_s[0]
    to_south[pl.ds(2 * levels, levels), :] = merid_s[0]


def advect_kernel(first, rows_each, peers, coef, halo, *refs):
    fields, outs, held, sems = refs[:4], refs[4 : 4 + peers], refs[4 + peers : -1], refs[-1]
    lat_rows, levels, _ = fields[0].shape
    top = lat_rows - 1
    me = lax.axis_index("lev")
    part = lambda i: halo[pl.ds(i * levels, levels), :]
    owned = [first + wrapped(me, step, peers) * rows_each for step in range(peers)]
    reach = ((0, rows_each), (0, rows_each + 1), (1, rows_each + 2), (1, rows_each + 2))
    starts = [[jnp.clip(row - before, 0, lat_rows - count) for before, count in reach] for row in owned]
    arriving = [
        copy_all(
            [
                (field.at[pl.ds(start, count)], target.at[step])
                for field, target, start, (_, count) in zip(fields, held, starts[step], reach)
            ],
            sems,
            4 * step,
        )
        for step in range(peers)
    ]
    for step in range(peers):
        wait_all(arriving[step])
        zonal, merid, thick, theta = (ref.at[step] for ref in held)
        z_at, w_at, t_at, _ = (owned[step] - start for start in starts[step])
        for place in range(rows_each):
            row = owned[step] + place
            at = t_at + place
            low, high = jnp.maximum(at - 1, 0), jnp.minimum(at + 1, rows_each + 1)
            t, t_s, t_n = thick[at], thick[low], thick[high]
            h, h_s, h_n = theta[at] * t, theta[low] * t_s, theta[high] * t_n
            w, w_n = merid[w_at + place], merid[jnp.minimum(w_at + place + 1, rows_each)]
            if first == 0 and place == 0:
                t_s = jnp.where(row == 0, part(0), t_s)
                h_s = jnp.where(row == 0, part(1), h_s)
            if first + peers * rows_each == lat_rows and place == rows_each - 1:
                t_n = jnp.where(row == top, part(0), t_n)
                h_n = jnp.where(row == top, part(1), h_n)
                w_n = jnp.where(row == top, part(2), w_n)
            fields_new = advect_row(row, coef, zonal[z_at + place], w, t, h, t_s, h_s, t_n, h_n, w_n)
            for field, new in enumerate(fields_new):
                store_packed(outs[step], (place, field), new)


def target_edges(surface, sigma):
    curve = sigma * sigma
    return TOP_PRESSURE + HYBRID_SCALE * (sigma - curve) + (surface - TOP_PRESSURE) * curve


def target_thickness(surface, first, levels):
    step = 1.0 / levels
    curve = (2.0 * first + 1.0) * (step * step)
    return HYBRID_SCALE * (step - curve) + (surface - TOP_PRESSURE) * curve


def exner(pressure):
    return jnp.exp(EXNER_POWER * jnp.log(pressure))


def split_dot(x, ones):
    a = x.astype(BF16)
    r = x - a.astype(F32)
    b = r.astype(BF16)
    c = (r - b.astype(F32)).astype(BF16)
    dot = lambda v: jnp.dot(v, ones, preferred_element_type=F32)
    return dot(a) + (dot(b) + dot(c))

def remap_kernel(width, block, peers, *refs):
    parts = refs[:peers]
    gathered, spread, base_rows, base_s = refs[-4:]
    outs = refs[-4 - peers : -4]
    me = lax.axis_index("lev")
    count = parts[0].shape[0]
    levels = peers * block
    level_r = lax.broadcasted_iota(jnp.int32, (levels, levels), 0)
    level_c = lax.broadcasted_iota(jnp.int32, (levels, levels), 1)
    running = (level_r <= level_c).astype(F32).astype(BF16)
    below = (
        lax.broadcasted_iota(jnp.int32, (8, levels), 1)
        >= block * (1 + lax.broadcasted_iota(jnp.int32, (8, levels), 0))
    ).astype(F32)
    full = width // LANES
    data_rows = packed_rows(block, width)
    half = block // 2
    sources = [wrapped(me, (peers - step) % peers, peers) for step in range(peers)]
    targets = [wrapped(me, step, peers) for step in range(peers)]
    for place in range(count):
        for step in range(peers):
            at = pl.ds(pl.multiple_of(sources[step] * block, block), block)
            for field in range(2):
                for tile in range(tile_count(width)):
                    cols = min(LANES, width - tile * LANES)
                    gathered[place, field, at, pl.ds(tile * LANES, cols)] = load_tile(
                        parts[step], (place, field), block, width, tile)
    for place in range(count):
        cols = width
        here = pl.ds(0, cols)
        thick = gathered[place, 0, :, here]
        surface_row = TOP_PRESSURE + jnp.sum(thick, axis=0, keepdims=True)
        thick = thick.T
        heat = gathered[place, 1, :, here].T
        upper = TOP_PRESSURE + split_dot(thick, running)
        theta = heat / thick
        offset = split_dot(heat, running) - theta * upper
        surface = upper[:, levels - 1 :]
        lane = lax.broadcasted_iota(jnp.int32, (cols, levels), 1)
        lane_f = lane.astype(F32)
        edge = target_edges(surface, (lane_f + 1.0) * (1.0 / levels))
        at = jnp.zeros((cols, levels), jnp.int32)
        jump = levels // 2
        while jump:
            probe = jnp.take_along_axis(upper, at + (jump - 1), axis=1, mode="promise_in_bounds")
            at = jnp.where(probe < edge, at + jump, at)
            jump //= 2
        pick = lambda table: jnp.take_along_axis(table, at, axis=1, mode="promise_in_bounds")
        heat_to = pick(offset) + pick(theta) * edge
        heat_from = jnp.where(lane == 0, 0.0, pltpu.roll(heat_to, 1, 1))
        theta_next = (heat_to - heat_from) / target_thickness(surface, lane_f, levels)
        exner_to = exner(edge)
        exner_from = jnp.where(lane == 0, TOP_PRESSURE**EXNER_POWER, pltpu.roll(exner_to, 1, 1))
        layer = theta_next * (exner_to - exner_from)
        bases = lax.dot_general(
            below, layer, (((1,), (1,)), ((), ())), precision=HIGHEST, preferred_element_type=F32
        )
        base_s[place, :, here] = bases
        base_s[place, pl.ds(7, 1), here] = surface_row
        spread[place, :, here] = theta_next.T
    for place in range(count):
        for tile in range(tile_count(width)):
            base_rows[place, tile] = base_s[place, :, pl.ds(tile * LANES, LANES)]
        for step in range(peers):
            out = outs[step]
            start = pl.multiple_of(targets[step] * block, block)
            for tile in range(tile_count(width)):
                cols = min(LANES, width - tile * LANES)
                here = pl.ds(tile * LANES, cols)
                if tile < full:
                    out[place, pl.ds(tile * block, block), :] = spread[place, pl.ds(start, block), here]
                else:
                    part = spread[place, pl.ds(start, block), here]
                    out[place, pl.ds(full * block, half), :] = jnp.concatenate([part[:half], part[half:]], axis=1)
                out[place, pl.ds(data_rows + tile, 1), pl.ds(0, cols)] = base_rows[place, tile, pl.ds(7, 1), pl.ds(0, cols)]
                out[place, pl.ds(data_rows + 8 + tile, 1), pl.ds(0, cols)] = base_rows[place, tile, pl.ds(targets[step], 1), pl.ds(0, cols)]


def below_sum(layer):
    rows, width = layer.shape
    groups = rows // 8
    carry = None
    pieces = []
    sub = lax.broadcasted_iota(jnp.int32, (8, width), 0)
    for g in reversed(range(groups)):
        x = layer[g * 8 : (g + 1) * 8]
        total = x
        for step in (1, 2, 4):
            total = total + jnp.where(sub < 8 - step, pltpu.roll(total, 8 - step, 0), 0.0)
        under = total - x
        if carry is not None:
            under = under + carry
            carry = carry + total[0:1]
        else:
            carry = total[0:1]
        pieces.append(under)
    return jnp.concatenate(pieces[::-1], axis=0)


def column_state(message, index, block, width, first_level, levels, ground):
    tiles = tile_count(width)
    data_rows = packed_rows(block, width)
    theta = jnp.concatenate([load_tile(message, index, block, width, t) for t in range(tiles)], axis=1)

    def line(first):
        return jnp.concatenate(
            [message[(*index, pl.ds(first + t, 1), pl.ds(0, min(LANES, width - t * LANES)))] for t in range(tiles)],
            axis=1,
        )

    surface = line(data_rows)
    base = line(data_rows + 8)
    sub = lax.broadcasted_iota(jnp.int32, (block, width), 0).astype(F32) + first_level
    thick = target_thickness(surface, sub, levels)
    top = exner(target_edges(surface, sub * (1.0 / levels)))
    bottom_edge = exner(target_edges(surface, (first_level + block) * (1.0 / levels)))
    sub_i = lax.broadcasted_iota(jnp.int32, (block, width), 0)
    bottom = jnp.where(sub_i == block - 1, bottom_edge, pltpu.roll(top, block - 1, 0))
    layer = theta * (bottom - top)
    geopot = (ground + base) + (below_sum(layer) + 0.5 * layer)
    return theta, thick, 0.5 * (top + bottom), geopot


def push(now, before):
    theta, exner_mid, geopot = now
    theta_b, exner_b, geopot_b = before
    return (geopot - geopot_b) + 0.5 * (theta + theta_b) * (exner_mid - exner_b)


def filtered(value, table, high, low, high_t, low_t, block):
    def product(x, b_high, b_low):
        x_high = x.astype(BF16)
        x_low = (x - x_high.astype(F32)).astype(BF16)
        dot = lambda a, b: jnp.dot(a, b, preferred_element_type=F32)
        return dot(x_high, b_high) + (dot(x_low, b_high) + dot(x_high, b_low))

    spectral = product(value, high, low)
    rows, width = value.shape
    spectral = (spectral.reshape(rows // block, block, width) * table[:, None, :]).reshape(rows, width)
    return value + product(spectral, high_t, low_t)


def gather_messages(me, parts, order):
    peers = len(parts)
    for step, part in enumerate(parts):
        owner = wrapped(me, (peers - step) % peers, peers)
        for place in range(part.shape[0]):
            order[owner * part.shape[0] + place] = part[place]


def copy_all(copies, sems, first=0):
    started = [pltpu.make_async_copy(source, target, sems.at[first + i]) for i, (source, target) in enumerate(copies)]
    for copy in started:
        copy.start()
    return started


def wait_all(copies):
    for copy in copies:
        copy.wait()


def filter_rows(ref, count, table, tables, block):
    width = ref.shape[-1]
    value = ref[pl.ds(0, count)].reshape(count * block, width)
    value = filtered(value, table, *(t[...] for t in tables), block)
    ref[pl.ds(0, count)] = value.reshape(count, block, width)


def around(x):
    return jnp.roll(x, 1, axis=1)


def upper_final_kernel(
    levels, first, flag, faces, p0, p1, p2, p3, ground, table, zonal, merid, b0, b1, b2, b3, after,
    zonal_out, merid_out, thick_out, theta_out, edge_state,
    order, zonal_s, merid_s, thick_s, theta_s, carried, sems,
):
    del after
    lat_rows, block, width = zonal.shape
    count = lat_rows - first
    rows = pl.ds(first, count)
    me = lax.axis_index("lev")
    level = (me * block).astype(F32)
    gather_messages(me, (p0, p1, p2, p3), order)
    carried[...] = jnp.zeros_like(carried)

    def one_row(i, _):
        row = first + i
        theta, thick, mid, geopot = column_state(order, (i,), block, width, level, levels, ground[pl.ds(row, 1), :])
        theta_s[i] = theta
        thick_s[i] = thick
        now = (theta, mid, geopot)
        zonal_s[i] = zonal[row] - push(now, tuple(around(x) for x in now))
        before = (carried[0], carried[1], carried[2])
        merid_s[jnp.maximum(i - 1, 0)] = merid[row] - faces[row] * push(now, before)
        for field, x in enumerate(now):
            carried[field] = x

        @pl.when(i == 0)
        def _():
            for field, x in enumerate(now):
                edge_state[field] = x

        return 0

    lax.fori_loop(0, count, one_row, 0)
    early = copy_all([(theta_s, theta_out.at[rows]), (thick_s, thick_out.at[rows])], sems)

    @pl.when(flag[0] != 0)
    def _():
        tables = (b0, b1, b2, b3)
        filter_rows(zonal_s, count, table[rows, :], tables, block)
        filter_rows(merid_s, count - 1, table[pl.ds(first + 1, count - 1), :], tables, block)

    late = copy_all(
        [
            (zonal_s, zonal_out.at[rows]),
            (merid_s.at[pl.ds(0, count - 1)], merid_out.at[pl.ds(first + 1, count - 1)]),
        ],
        sems,
        2,
    )
    wait_all(early + late)


def lower_final_kernel(
    levels, flag, faces, south, halo_s, edge_state, p0, p1, p2, p3, ground, table, zonal, merid, b0, b1, b2, b3,
    zonal_in, merid_in, thick_in, theta_in,
    zonal_out, merid_out, thick_out, theta_out,
    order, winds_s, thick_s, theta_s, sems,
):
    del zonal_in, merid_in, thick_in, theta_in
    count = order.shape[0]
    _, block, width = zonal.shape
    me = lax.axis_index("lev")
    level = (me * block).astype(F32)
    gather_messages(me, (p0, p1, p2, p3), order)
    state = lambda ref, i, line: column_state(ref, (i,), block, width, level, levels, line)
    theta, _, mid, geopot = state(south, 0, halo_s[pl.ds(2 * block, 1), :])
    before = (theta, mid, geopot)
    for row in range(count):
        theta, thick, mid, geopot = state(order, row, ground[pl.ds(row, 1), :])
        theta_s[row] = theta
        thick_s[row] = thick
        now = (theta, mid, geopot)
        winds_s[row] = zonal[row] - push(now, tuple(around(x) for x in now))
        winds_s[count + row] = merid[row] - faces[row] * push(now, before)
        before = now
    now = tuple(edge_state[field] for field in range(3))
    winds_s[2 * count] = merid[count] - faces[count] * push(now, before)
    rows = pl.ds(0, count)
    early = copy_all([(theta_s, theta_out.at[rows]), (thick_s, thick_out.at[rows])], sems)

    @pl.when(flag[0] != 0)
    def _():
        picked = jnp.concatenate([table[rows, :], table[pl.ds(0, count + 1), :]], axis=0)
        filter_rows(winds_s, 2 * count + 1, picked, (b0, b1, b2, b3), block)

    late = copy_all(
        [
            (winds_s.at[rows], zonal_out.at[rows]),
            (winds_s.at[pl.ds(count, count + 1)], merid_out.at[pl.ds(0, count + 1)]),
        ],
        sems,
        2,
    )
    wait_all(early + late)


def exchanged(parts):
    peers = lax.axis_size("lev")
    return [parts[0]] + [
        lax.ppermute(parts[step], "lev", [(i, (i + step) % peers) for i in range(peers)]) for step in range(1, peers)
    ]


def body(
    zonal_wind, meridional_wind, thickness, potential_temp, surface_geo, polar_mask, cutoff, damping
):
    lat_rows, block, width = zonal_wind.shape
    lat_count = lax.axis_size("lat")
    peers = lax.axis_size("lev")
    levels = block * peers
    total_rows = lat_rows * lat_count
    first_row = lax.axis_index("lat") * lat_rows
    row_ids = (first_row + jnp.arange(lat_rows + 1, dtype=jnp.int32)).astype(F32)
    faces = jnp.sin(math.pi * row_ids / total_rows)
    centres = jnp.sin(math.pi * (row_ids[:-1] + 0.5) / total_rows)
    coef = jnp.stack([faces[:-1], faces[1:]]) * (0.5 * COURANT) / centres
    northward = [(i, i + 1) for i in range(lat_count - 1)]
    southward = [(i + 1, i) for i in range(lat_count - 1)]
    flag = jnp.any(polar_mask != 0).astype(jnp.int32).reshape(1)
    shape = lambda *dims: jax.ShapeDtypeStruct(dims, F32)
    hbm = pl.BlockSpec(memory_space=pltpu.HBM)
    rows_of = lambda n: pltpu.VMEM((n, block, width), F32)
    dma = lambda n: pltpu.SemaphoreType.DMA((n,))

    lower_each = 1
    upper_each = lat_rows // peers - lower_each
    first = lower_each * peers
    upper = lat_rows - first
    data_rows = packed_rows(block, width)
    message_rows = data_rows + 16
    stay = lambda *arrays: [pltpu.with_memory_space_constraint(x, pltpu.HBM) for x in arrays]
    field = shape(lat_rows, block, width)

    fields = stay(zonal_wind, meridional_wind, thickness, potential_temp)
    to_north, to_south = pl.pallas_call(
        edges_kernel,
        out_shape=[shape(2 * block + 8, width), shape(3 * block, width)],
        in_specs=[hbm] * 4,
        out_specs=[VMEM] * 2,
        scratch_shapes=[rows_of(2), rows_of(2), rows_of(1), pltpu.VMEM((lat_rows, width), F32), dma(6)],
        compiler_params=params(8),
        cost_estimate=cost(1),
        name="edges",
    )(*fields[1:], *stay(surface_geo))
    halo_n = lax.ppermute(to_south, "lat", southward)
    halo_s = lax.ppermute(to_north, "lat", northward)

    def advect(start, each, halo, name):
        return pl.pallas_call(
            lambda *refs: advect_kernel(start, each, peers, *refs),
            out_shape=[shape(each, 2, data_rows, LANES)] * peers,
            in_specs=[SMEM, VMEM] + [hbm] * 4,
            out_specs=[VMEM] * peers,
            scratch_shapes=[
                pltpu.VMEM((peers, each + extra, block, width), F32) for extra in (0, 1, 2, 2)
            ]
            + [dma(4 * peers)],
            compiler_params=params(12),
            cost_estimate=cost(1 + 2 * each),
            name=name,
        )(coef, halo, *fields)

    upper_columns = exchanged(advect(first, upper_each, halo_n, "advect_upper"))
    lower_sent = advect(0, lower_each, halo_s, "advect_lower")
    settled = lax.optimization_barrier((*upper_columns, *lower_sent))
    upper_columns, lower_sent = settled[:peers], settled[peers:]
    lower_columns = exchanged(lower_sent)

    def remap(columns, each, name, after):
        lanes = tile_count(width) * LANES
        return pl.pallas_call(
            lambda *refs: remap_kernel(width, block, peers, *refs),
            out_shape=[shape(each, message_rows, LANES)] * peers,
            in_specs=[VMEM] * peers + [pl.BlockSpec(memory_space=pl.ANY)] * len(after),
            out_specs=[VMEM] * peers,
            scratch_shapes=[
                pltpu.VMEM((each, 2, levels, lanes), F32),
                pltpu.VMEM((each, levels, lanes), F32),
                pltpu.VMEM((each, tile_count(width), 8, LANES), F32),
                pltpu.VMEM((each, 8, lanes), F32),
            ],
            compiler_params=params(12),
            cost_estimate=cost(1 + 3 * each),
            name=name,
        )(*columns, *after)

    upper_remapped = remap(upper_columns, upper_each, "remap_upper", lower_columns[:1])
    upper_messages = exchanged(upper_remapped)
    lower_remapped = remap(lower_columns, lower_each, "remap_lower", upper_messages[1:2])
    lower_messages = exchanged(lower_remapped)
    step_of_last = (lax.axis_index("lev") + 1) % peers
    _, *candidates = lax.optimization_barrier((lower_remapped[0], *upper_messages))
    last_message = candidates[0][-1:]
    for step in range(1, peers):
        last_message = jnp.where(step_of_last == step, candidates[step][-1:], last_message)
    south = lax.ppermute(last_message, "lat", northward)

    high, low, wave = fourier_tables(width)
    active = (jnp.asarray(wave)[None, :] >= cutoff[:, None]) & (polar_mask[:, None] != 0)
    table = jnp.where(active, damping - 1.0, 0.0)
    tables = [jnp.asarray(x) for x in (high, low, np.ascontiguousarray(high.T), np.ascontiguousarray(low.T))]

    *partial, edge_state = pl.pallas_call(
        lambda *refs: upper_final_kernel(levels, first, *refs),
        out_shape=[field] * 4 + [shape(3, block, width)],
        in_specs=[SMEM] * 2 + [VMEM] * (peers + 8) + [pl.BlockSpec(memory_space=pl.ANY)],
        out_specs=[hbm] * 4 + [VMEM],
        scratch_shapes=[pltpu.VMEM((upper, message_rows, LANES), F32)]
        + [rows_of(upper)] * 4
        + [rows_of(3), dma(4)],
        compiler_params=params(18),
        cost_estimate=cost(7),
        name="final_upper",
    )(
        flag, faces, *upper_messages, surface_geo, table, zonal_wind, meridional_wind, *tables, lower_remapped[0]
    )
    edge_state, *lower_messages = lax.optimization_barrier((edge_state, *lower_messages))
    return tuple(
        pl.pallas_call(
            lambda *refs: lower_final_kernel(levels, *refs),
            out_shape=[field] * 4,
            in_specs=[SMEM] * 2 + [VMEM] * (peers + 11) + [hbm] * 4,
            out_specs=[hbm] * 4,
            scratch_shapes=[pltpu.VMEM((first, message_rows, LANES), F32)]
            + [rows_of(2 * first + 1), rows_of(first), rows_of(first), dma(4)],
            input_output_aliases={peers + 13 + i: i for i in range(4)},
            compiler_params=params(16),
            cost_estimate=cost(6),
            name="final_lower",
        )(
            flag, faces, south, halo_s, edge_state, *lower_messages, surface_geo, table, zonal_wind, meridional_wind, *tables,
            *partial,
        )
    )


def solution(mesh):
    field = P("lat", "lev", None)
    in_specs = (field, field, field, field, P("lat", None), P("lat"), P("lat"), P("lat", None))
    return jax.shard_map(body, mesh=mesh, in_specs=in_specs, out_specs=(field,) * 4, check_vma=False)
```

```python
import math

import jax
import jax.numpy as jnp
import numpy as np
from jax import lax
from jax.experimental import pallas as pl
from jax.experimental.pallas import tpu as pltpu
from jax.sharding import PartitionSpec as P

TOP_PRESSURE = 0.01
HYBRID_SCALE = 0.2
EXNER_POWER = 2.0 / 7.0
COURANT = 0.012
HIGHEST = lax.Precision.HIGHEST
F32 = jnp.float32
BF16 = jnp.bfloat16
VMEM = pl.BlockSpec(memory_space=pltpu.VMEM)
SMEM = pl.BlockSpec(memory_space=pltpu.SMEM)
LANES = 128


def params(mib):
    return pltpu.CompilerParams(vmem_limit_bytes=mib * 1024 * 1024)


def cost(microseconds):
    return pl.CostEstimate(
        flops=int(microseconds * 1.1e9), bytes_accessed=int(microseconds * 3.6e6), transcendentals=0
    )


def fourier_tables(count):
    middle = count // 2
    ids = np.arange(count)
    wave = np.where(ids <= middle, ids, ids - middle)
    angle = 2.0 * np.pi / count * (ids[:, None] * wave[None, :] % count)
    edge = (ids == 0) | (ids == middle)
    weight = np.where(edge, 1.0 / math.sqrt(count), math.sqrt(2.0 / count))
    basis = np.where((ids <= middle)[None, :], np.cos(angle), np.sin(angle)) * weight[None, :]
    basis = basis.astype(np.float32)
    high = basis.astype(jnp.bfloat16)
    low = (basis - high.astype(np.float32)).astype(jnp.bfloat16)
    return high, low, wave.astype(np.int32)


def packed_rows(rows, width):
    return rows * width // LANES


def store_packed(ref, index, value):
    rows, width = value.shape
    full = width // LANES
    for tile in range(full):
        ref[(*index, pl.ds(tile * rows, rows), slice(None))] = value[:, tile * LANES : (tile + 1) * LANES]
    if width % LANES:
        rest = value[:, full * LANES :]
        half = rows // 2
        ref[(*index, pl.ds(full * rows, half), slice(None))] = jnp.concatenate([rest[:half], rest[half:]], axis=1)


def load_tile(ref, index, rows, width, tile):
    full = width // LANES
    if tile < full:
        return ref[(*index, pl.ds(tile * rows, rows), slice(None))]
    half = rows // 2
    both = ref[(*index, pl.ds(full * rows, half), slice(None))]
    return jnp.concatenate([both[:, : LANES // 2], both[:, LANES // 2 :]], axis=0)


def tile_count(width):
    return -(-width // LANES)


def wrapped(me, step, peers):
    other = me + step
    return jnp.where(other >= peers, other - peers, other)


def advect_row(row, coef, zonal, merid, t, h, t_s, h_s, t_n, h_n, w_n):
    u = zonal * (0.5 * COURANT)
    w_n = w_n * coef[1, row]
    w_s = merid * coef[0, row]
    for x, x_s, x_n in ((t, t_s, t_n), (h, h_s, h_n)):
        flux = u * (x + jnp.roll(x, 1, axis=1))
        yield x - (jnp.roll(flux, -1, axis=1) - flux) - (w_n * (x_n + x) - w_s * (x + x_s))


def edges_kernel(merid, thick, theta, ground, to_north, to_south, thick_s, theta_s, merid_s, ground_s, sems):
    lat_rows, levels, _ = thick.shape
    top = lat_rows - 1
    copies = []
    for source, target in ((thick, thick_s), (theta, theta_s)):
        copies += [(source.at[pl.ds(0, 1)], target.at[pl.ds(0, 1)]), (source.at[pl.ds(top, 1)], target.at[pl.ds(1, 1)])]
    wait_all(copy_all([*copies, (merid.at[pl.ds(0, 1)], merid_s), (ground, ground_s)], sems))
    to_north[pl.ds(0, levels), :] = thick_s[1]
    to_north[pl.ds(levels, levels), :] = theta_s[1] * thick_s[1]
    to_north[pl.ds(2 * levels, 1), :] = ground_s[pl.ds(top, 1), :]
    to_south[pl.ds(0, levels), :] = thick_s[0]
    to_south[pl.ds(levels, levels), :] = theta_s[0] * thick_s[0]
    to_south[pl.ds(2 * levels, levels), :] = merid_s[0]


def advect_kernel(first, rows_each, peers, coef, halo, *refs):
    fields, outs, held, sems = refs[:4], refs[4 : 4 + peers], refs[4 + peers : -1], refs[-1]
    lat_rows, levels, _ = fields[0].shape
    top = lat_rows - 1
    me = lax.axis_index("lev")
    part = lambda i: halo[pl.ds(i * levels, levels), :]
    owned = [first + wrapped(me, step, peers) * rows_each for step in range(peers)]
    reach = ((0, rows_each), (0, rows_each + 1), (1, rows_each + 2), (1, rows_each + 2))
    starts = [[jnp.clip(row - before, 0, lat_rows - count) for before, count in reach] for row in owned]
    arriving = [
        copy_all(
            [
                (field.at[pl.ds(start, count)], target.at[step])
                for field, target, start, (_, count) in zip(fields, held, starts[step], reach)
            ],
            sems,
            4 * step,
        )
        for step in range(peers)
    ]
    for step in range(peers):
        wait_all(arriving[step])
        zonal, merid, thick, theta = (ref.at[step] for ref in held)
        z_at, w_at, t_at, _ = (owned[step] - start for start in starts[step])
        for place in range(rows_each):
            row = owned[step] + place
            at = t_at + place
            low, high = jnp.maximum(at - 1, 0), jnp.minimum(at + 1, rows_each + 1)
            t, t_s, t_n = thick[at], thick[low], thick[high]
            h, h_s, h_n = theta[at] * t, theta[low] * t_s, theta[high] * t_n
            w, w_n = merid[w_at + place], merid[jnp.minimum(w_at + place + 1, rows_each)]
            if first == 0 and place == 0:
                t_s = jnp.where(row == 0, part(0), t_s)
                h_s = jnp.where(row == 0, part(1), h_s)
            if first + peers * rows_each == lat_rows and place == rows_each - 1:
                t_n = jnp.where(row == top, part(0), t_n)
                h_n = jnp.where(row == top, part(1), h_n)
                w_n = jnp.where(row == top, part(2), w_n)
            fields_new = advect_row(row, coef, zonal[z_at + place], w, t, h, t_s, h_s, t_n, h_n, w_n)
            for field, new in enumerate(fields_new):
                store_packed(outs[step], (place, field), new)


def target_edges(surface, sigma):
    curve = sigma * sigma
    return TOP_PRESSURE + HYBRID_SCALE * (sigma - curve) + (surface - TOP_PRESSURE) * curve


def target_thickness(surface, first, levels):
    step = 1.0 / levels
    curve = (2.0 * first + 1.0) * (step * step)
    return HYBRID_SCALE * (step - curve) + (surface - TOP_PRESSURE) * curve


def exner(pressure):
    return jnp.exp(EXNER_POWER * jnp.log(pressure))


def split_dot(x, ones):
    a = x.astype(BF16)
    r = x - a.astype(F32)
    b = r.astype(BF16)
    c = (r - b.astype(F32)).astype(BF16)
    dot = lambda v: jnp.dot(v, ones, preferred_element_type=F32)
    return dot(a) + (dot(b) + dot(c))

def remap_kernel(width, block, peers, *refs):
    parts = refs[:peers]
    gathered, spread, base_rows, base_s = refs[-4:]
    outs = refs[-4 - peers : -4]
    me = lax.axis_index("lev")
    count = parts[0].shape[0]
    levels = peers * block
    level_r = lax.broadcasted_iota(jnp.int32, (levels, levels), 0)
    level_c = lax.broadcasted_iota(jnp.int32, (levels, levels), 1)
    running = (level_r <= level_c).astype(F32).astype(BF16)
    below = (
        lax.broadcasted_iota(jnp.int32, (8, levels), 1)
        >= block * (1 + lax.broadcasted_iota(jnp.int32, (8, levels), 0))
    ).astype(F32)
    full = width // LANES
    data_rows = packed_rows(block, width)
    half = block // 2
    sources = [wrapped(me, (peers - step) % peers, peers) for step in range(peers)]
    targets = [wrapped(me, step, peers) for step in range(peers)]
    for place in range(count):
        for step in range(peers):
            at = pl.ds(pl.multiple_of(sources[step] * block, block), block)
            for field in range(2):
                for tile in range(tile_count(width)):
                    cols = min(LANES, width - tile * LANES)
                    gathered[place, field, at, pl.ds(tile * LANES, cols)] = load_tile(
                        parts[step], (place, field), block, width, tile)
    for place in range(count):
        cols = width
        here = pl.ds(0, cols)
        thick = gathered[place, 0, :, here]
        surface_row = TOP_PRESSURE + jnp.sum(thick, axis=0, keepdims=True)
        thick = thick.T
        heat = gathered[place, 1, :, here].T
        upper = TOP_PRESSURE + split_dot(thick, running)
        theta = heat / thick
        offset = split_dot(heat, running) - theta * upper
        surface = upper[:, levels - 1 :]
        lane = lax.broadcasted_iota(jnp.int32, (cols, levels), 1)
        lane_f = lane.astype(F32)
        edge = target_edges(surface, (lane_f + 1.0) * (1.0 / levels))
        at = jnp.zeros((cols, levels), jnp.int32)
        jump = levels // 2
        while jump:
            probe = jnp.take_along_axis(upper, at + (jump - 1), axis=1, mode="promise_in_bounds")
            at = jnp.where(probe < edge, at + jump, at)
            jump //= 2
        pick = lambda table: jnp.take_along_axis(table, at, axis=1, mode="promise_in_bounds")
        heat_to = pick(offset) + pick(theta) * edge
        heat_from = jnp.where(lane == 0, 0.0, pltpu.roll(heat_to, 1, 1))
        theta_next = (heat_to - heat_from) / target_thickness(surface, lane_f, levels)
        exner_to = exner(edge)
        exner_from = jnp.where(lane == 0, TOP_PRESSURE**EXNER_POWER, pltpu.roll(exner_to, 1, 1))
        layer = theta_next * (exner_to - exner_from)
        bases = lax.dot_general(
            below, layer, (((1,), (1,)), ((), ())), precision=HIGHEST, preferred_element_type=F32
        )
        base_s[place, :, here] = bases
        base_s[place, pl.ds(7, 1), here] = surface_row
        spread[place, :, here] = theta_next.T
    for place in range(count):
        for tile in range(tile_count(width)):
            base_rows[place, tile] = base_s[place, :, pl.ds(tile * LANES, LANES)]
        for step in range(peers):
            out = outs[step]
            start = pl.multiple_of(targets[step] * block, block)
            for tile in range(tile_count(width)):
                cols = min(LANES, width - tile * LANES)
                here = pl.ds(tile * LANES, cols)
                if tile < full:
                    out[place, pl.ds(tile * block, block), :] = spread[place, pl.ds(start, block), here]
                else:
                    part = spread[place, pl.ds(start, block), here]
                    out[place, pl.ds(full * block, half), :] = jnp.concatenate([part[:half], part[half:]], axis=1)
                out[place, pl.ds(data_rows + tile, 1), pl.ds(0, cols)] = base_rows[place, tile, pl.ds(7, 1), pl.ds(0, cols)]
                out[place, pl.ds(data_rows + 8 + tile, 1), pl.ds(0, cols)] = base_rows[place, tile, pl.ds(targets[step], 1), pl.ds(0, cols)]


def below_sum(layer):
    rows, width = layer.shape
    groups = rows // 8
    carry = None
    pieces = []
    sub = lax.broadcasted_iota(jnp.int32, (8, width), 0)
    for g in reversed(range(groups)):
        x = layer[g * 8 : (g + 1) * 8]
        total = x
        for step in (1, 2, 4):
            total = total + jnp.where(sub < 8 - step, pltpu.roll(total, 8 - step, 0), 0.0)
        under = total - x
        if carry is not None:
            under = under + carry
            carry = carry + total[0:1]
        else:
            carry = total[0:1]
        pieces.append(under)
    return jnp.concatenate(pieces[::-1], axis=0)


def column_state(message, index, block, width, first_level, levels, ground):
    tiles = tile_count(width)
    data_rows = packed_rows(block, width)
    theta = jnp.concatenate([load_tile(message, index, block, width, t) for t in range(tiles)], axis=1)

    def line(first):
        return jnp.concatenate(
            [message[(*index, pl.ds(first + t, 1), pl.ds(0, min(LANES, width - t * LANES)))] for t in range(tiles)],
            axis=1,
        )

    surface = line(data_rows)
    base = line(data_rows + 8)
    sub = lax.broadcasted_iota(jnp.int32, (block, width), 0).astype(F32) + first_level
    thick = target_thickness(surface, sub, levels)
    top = exner(target_edges(surface, sub * (1.0 / levels)))
    bottom_edge = exner(target_edges(surface, (first_level + block) * (1.0 / levels)))
    sub_i = lax.broadcasted_iota(jnp.int32, (block, width), 0)
    bottom = jnp.where(sub_i == block - 1, bottom_edge, pltpu.roll(top, block - 1, 0))
    layer = theta * (bottom - top)
    geopot = (ground + base) + (below_sum(layer) + 0.5 * layer)
    return theta, thick, 0.5 * (top + bottom), geopot


def push(now, before):
    theta, exner_mid, geopot = now
    theta_b, exner_b, geopot_b = before
    return (geopot - geopot_b) + 0.5 * (theta + theta_b) * (exner_mid - exner_b)


def filtered(value, table, high, low, high_t, low_t, block):
    def product(x, b_high, b_low):
        x_high = x.astype(BF16)
        x_low = (x - x_high.astype(F32)).astype(BF16)
        dot = lambda a, b: jnp.dot(a, b, preferred_element_type=F32)
        return dot(x_high, b_high) + (dot(x_low, b_high) + dot(x_high, b_low))

    spectral = product(value, high, low)
    rows, width = value.shape
    spectral = (spectral.reshape(rows // block, block, width) * table[:, None, :]).reshape(rows, width)
    return value + product(spectral, high_t, low_t)


def gather_messages(me, parts, order):
    peers = len(parts)
    for step, part in enumerate(parts):
        owner = wrapped(me, (peers - step) % peers, peers)
        for place in range(part.shape[0]):
            order[owner * part.shape[0] + place] = part[place]


def copy_all(copies, sems, first=0):
    started = [pltpu.make_async_copy(source, target, sems.at[first + i]) for i, (source, target) in enumerate(copies)]
    for copy in started:
        copy.start()
    return started


def wait_all(copies):
    for copy in copies:
        copy.wait()


def filter_rows(ref, count, table, tables, block):
    width = ref.shape[-1]
    value = ref[pl.ds(0, count)].reshape(count * block, width)
    value = filtered(value, table, *(t[...] for t in tables), block)
    ref[pl.ds(0, count)] = value.reshape(count, block, width)


def around(x):
    return jnp.roll(x, 1, axis=1)


def upper_final_kernel(
    levels, first, flag, faces, p0, p1, p2, p3, ground, table, zonal, merid, b0, b1, b2, b3, after,
    zonal_out, merid_out, thick_out, theta_out, edge_state,
    order, zonal_s, merid_s, thick_s, theta_s, carried, sems,
):
    del after
    lat_rows, block, width = zonal.shape
    count = lat_rows - first
    rows = pl.ds(first, count)
    me = lax.axis_index("lev")
    level = (me * block).astype(F32)
    gather_messages(me, (p0, p1, p2, p3), order)
    carried[...] = jnp.zeros_like(carried)

    def one_row(i, _):
        row = first + i
        theta, thick, mid, geopot = column_state(order, (i,), block, width, level, levels, ground[pl.ds(row, 1), :])
        theta_s[i] = theta
        thick_s[i] = thick
        now = (theta, mid, geopot)
        zonal_s[i] = zonal[row] - push(now, tuple(around(x) for x in now))
        before = (carried[0], carried[1], carried[2])
        merid_s[jnp.maximum(i - 1, 0)] = merid[row] - faces[row] * push(now, before)
        for field, x in enumerate(now):
            carried[field] = x

        @pl.when(i == 0)
        def _():
            for field, x in enumerate(now):
                edge_state[field] = x

        return 0

    lax.fori_loop(0, count, one_row, 0)
    early = copy_all([(theta_s, theta_out.at[rows]), (thick_s, thick_out.at[rows])], sems)

    @pl.when(flag[0] != 0)
    def _():
        tables = (b0, b1, b2, b3)
        filter_rows(zonal_s, count, table[rows, :], tables, block)
        filter_rows(merid_s, count - 1, table[pl.ds(first + 1, count - 1), :], tables, block)

    late = copy_all(
        [
            (zonal_s, zonal_out.at[rows]),
            (merid_s.at[pl.ds(0, count - 1)], merid_out.at[pl.ds(first + 1, count - 1)]),
        ],
        sems,
        2,
    )
    wait_all(early + late)


def lower_final_kernel(
    levels, flag, faces, south, halo_s, edge_state, p0, p1, p2, p3, ground, table, zonal, merid, b0, b1, b2, b3,
    zonal_in, merid_in, thick_in, theta_in,
    zonal_out, merid_out, thick_out, theta_out,
    order, winds_s, thick_s, theta_s, sems,
):
    del zonal_in, merid_in, thick_in, theta_in
    count = order.shape[0]
    _, block, width = zonal.shape
    me = lax.axis_index("lev")
    level = (me * block).astype(F32)
    gather_messages(me, (p0, p1, p2, p3), order)
    state = lambda ref, i, line: column_state(ref, (i,), block, width, level, levels, line)
    theta, _, mid, geopot = state(south, 0, halo_s[pl.ds(2 * block, 1), :])
    before = (theta, mid, geopot)
    for row in range(count):
        theta, thick, mid, geopot = state(order, row, ground[pl.ds(row, 1), :])
        theta_s[row] = theta
        thick_s[row] = thick
        now = (theta, mid, geopot)
        winds_s[row] = zonal[row] - push(now, tuple(around(x) for x in now))
        winds_s[count + row] = merid[row] - faces[row] * push(now, before)
        before = now
    now = tuple(edge_state[field] for field in range(3))
    winds_s[2 * count] = merid[count] - faces[count] * push(now, before)
    rows = pl.ds(0, count)
    early = copy_all([(theta_s, theta_out.at[rows]), (thick_s, thick_out.at[rows])], sems)

    @pl.when(flag[0] != 0)
    def _():
        picked = jnp.concatenate([table[rows, :], table[pl.ds(0, count + 1), :]], axis=0)
        filter_rows(winds_s, 2 * count + 1, picked, (b0, b1, b2, b3), block)

    late = copy_all(
        [
            (winds_s.at[rows], zonal_out.at[rows]),
            (winds_s.at[pl.ds(count, count + 1)], merid_out.at[pl.ds(0, count + 1)]),
        ],
        sems,
        2,
    )
    wait_all(early + late)


def exchanged(parts):
    peers = lax.axis_size("lev")
    return [parts[0]] + [
        lax.ppermute(parts[step], "lev", [(i, (i + step) % peers) for i in range(peers)]) for step in range(1, peers)
    ]


def body(
    zonal_wind, meridional_wind, thickness, potential_temp, surface_geo, polar_mask, cutoff, damping
):
    lat_rows, block, width = zonal_wind.shape
    lat_count = lax.axis_size("lat")
    peers = lax.axis_size("lev")
    levels = block * peers
    total_rows = lat_rows * lat_count
    first_row = lax.axis_index("lat") * lat_rows
    row_ids = (first_row + jnp.arange(lat_rows + 1, dtype=jnp.int32)).astype(F32)
    faces = jnp.sin(math.pi * row_ids / total_rows)
    centres = jnp.sin(math.pi * (row_ids[:-1] + 0.5) / total_rows)
    coef = jnp.stack([faces[:-1], faces[1:]]) * (0.5 * COURANT) / centres
    northward = [(i, i + 1) for i in range(lat_count - 1)]
    southward = [(i + 1, i) for i in range(lat_count - 1)]
    flag = jnp.any(polar_mask != 0).astype(jnp.int32).reshape(1)
    shape = lambda *dims: jax.ShapeDtypeStruct(dims, F32)
    hbm = pl.BlockSpec(memory_space=pltpu.HBM)
    rows_of = lambda n: pltpu.VMEM((n, block, width), F32)
    dma = lambda n: pltpu.SemaphoreType.DMA((n,))

    lower_each = 1
    upper_each = lat_rows // peers - lower_each
    first = lower_each * peers
    upper = lat_rows - first
    data_rows = packed_rows(block, width)
    message_rows = data_rows + 16
    stay = lambda *arrays: [pltpu.with_memory_space_constraint(x, pltpu.HBM) for x in arrays]
    field = shape(lat_rows, block, width)

    fields = stay(zonal_wind, meridional_wind, thickness, potential_temp)
    to_north, to_south = pl.pallas_call(
        edges_kernel,
        out_shape=[shape(2 * block + 8, width), shape(3 * block, width)],
        in_specs=[hbm] * 4,
        out_specs=[VMEM] * 2,
        scratch_shapes=[rows_of(2), rows_of(2), rows_of(1), pltpu.VMEM((lat_rows, width), F32), dma(6)],
        compiler_params=params(8),
        cost_estimate=cost(1),
        name="edges",
    )(*fields[1:], *stay(surface_geo))
    halo_n = lax.ppermute(to_south, "lat", southward)
    halo_s = lax.ppermute(to_north, "lat", northward)

    def advect(start, each, halo, name):
        return pl.pallas_call(
            lambda *refs: advect_kernel(start, each, peers, *refs),
            out_shape=[shape(each, 2, data_rows, LANES)] * peers,
            in_specs=[SMEM, VMEM] + [hbm] * 4,
            out_specs=[VMEM] * peers,
            scratch_shapes=[
                pltpu.VMEM((peers, each + extra, block, width), F32) for extra in (0, 1, 2, 2)
            ]
            + [dma(4 * peers)],
            compiler_params=params(12),
            cost_estimate=cost(1 + 2 * each),
            name=name,
        )(coef, halo, *fields)

    upper_columns = exchanged(advect(first, upper_each, halo_n, "advect_upper"))
    lower_sent = advect(0, lower_each, halo_s, "advect_lower")
    settled = lax.optimization_barrier((*upper_columns, *lower_sent))
    upper_columns, lower_sent = settled[:peers], settled[peers:]
    lower_columns = exchanged(lower_sent)

    def remap(columns, each, name, after):
        lanes = tile_count(width) * LANES
        return pl.pallas_call(
            lambda *refs: remap_kernel(width, block, peers, *refs),
            out_shape=[shape(each, message_rows, LANES)] * peers,
            in_specs=[VMEM] * peers + [pl.BlockSpec(memory_space=pl.ANY)] * len(after),
            out_specs=[VMEM] * peers,
            scratch_shapes=[
                pltpu.VMEM((each, 2, levels, lanes), F32),
                pltpu.VMEM((each, levels, lanes), F32),
                pltpu.VMEM((each, tile_count(width), 8, LANES), F32),
                pltpu.VMEM((each, 8, lanes), F32),
            ],
            compiler_params=params(12),
            cost_estimate=cost(3 * each - 2.8),
            name=name,
        )(*columns, *after)

    upper_remapped = remap(upper_columns, upper_each, "remap_upper", lower_columns[:1])
    upper_messages = exchanged(upper_remapped)
    lower_remapped = remap(lower_columns, lower_each, "remap_lower", upper_remapped[:1])
    lower_messages = exchanged(lower_remapped)
    step_of_last = (lax.axis_index("lev") + 1) % peers
    _, *candidates = lax.optimization_barrier((lower_remapped[0], *upper_messages))
    last_message = candidates[0][-1:]
    for step in range(1, peers):
        last_message = jnp.where(step_of_last == step, candidates[step][-1:], last_message)
    south = lax.ppermute(last_message, "lat", northward)

    high, low, wave = fourier_tables(width)
    active = (jnp.asarray(wave)[None, :] >= cutoff[:, None]) & (polar_mask[:, None] != 0)
    table = jnp.where(active, damping - 1.0, 0.0)
    tables = [jnp.asarray(x) for x in (high, low, np.ascontiguousarray(high.T), np.ascontiguousarray(low.T))]

    *partial, edge_state = pl.pallas_call(
        lambda *refs: upper_final_kernel(levels, first, *refs),
        out_shape=[field] * 4 + [shape(3, block, width)],
        in_specs=[SMEM] * 2 + [VMEM] * (peers + 8) + [pl.BlockSpec(memory_space=pl.ANY)],
        out_specs=[hbm] * 4 + [VMEM],
        scratch_shapes=[pltpu.VMEM((upper, message_rows, LANES), F32)]
        + [rows_of(upper)] * 4
        + [rows_of(3), dma(4)],
        compiler_params=params(18),
        cost_estimate=cost(7),
        name="final_upper",
    )(
        flag, faces, *upper_messages, surface_geo, table, zonal_wind, meridional_wind, *tables, lower_remapped[0]
    )
    edge_state, *lower_messages = lax.optimization_barrier((edge_state, *lower_messages))
    return tuple(
        pl.pallas_call(
            lambda *refs: lower_final_kernel(levels, *refs),
            out_shape=[field] * 4,
            in_specs=[SMEM] * 2 + [VMEM] * (peers + 11) + [hbm] * 4,
            out_specs=[hbm] * 4,
            scratch_shapes=[pltpu.VMEM((first, message_rows, LANES), F32)]
            + [rows_of(2 * first + 1), rows_of(first), rows_of(first), dma(4)],
            input_output_aliases={peers + 13 + i: i for i in range(4)},
            compiler_params=params(16),
            cost_estimate=cost(6),
            name="final_lower",
        )(
            flag, faces, south, halo_s, edge_state, *lower_messages, surface_geo, table, zonal_wind, meridional_wind, *tables,
            *partial,
        )
    )


def solution(mesh):
    field = P("lat", "lev", None)
    in_specs = (field, field, field, field, P("lat", None), P("lat"), P("lat"), P("lat", None))
    return jax.shard_map(body, mesh=mesh, in_specs=in_specs, out_specs=(field,) * 4, check_vma=False)
```

```python
import math

import jax
import jax.numpy as jnp
import numpy as np
from jax import lax
from jax.experimental import pallas as pl
from jax.experimental.pallas import tpu as pltpu
from jax.sharding import PartitionSpec as P

TOP_PRESSURE = 0.01
HYBRID_SCALE = 0.2
EXNER_POWER = 2.0 / 7.0
COURANT = 0.012
HIGHEST = lax.Precision.HIGHEST
F32 = jnp.float32
BF16 = jnp.bfloat16
VMEM = pl.BlockSpec(memory_space=pltpu.VMEM)
SMEM = pl.BlockSpec(memory_space=pltpu.SMEM)
LANES = 128


def params(mib):
    return pltpu.CompilerParams(vmem_limit_bytes=mib * 1024 * 1024)


def cost(microseconds):
    return pl.CostEstimate(
        flops=int(microseconds * 1.1e9), bytes_accessed=int(microseconds * 3.6e6), transcendentals=0
    )


def fourier_tables(count):
    middle = count // 2
    ids = np.arange(count)
    wave = np.where(ids <= middle, ids, ids - middle)
    angle = 2.0 * np.pi / count * (ids[:, None] * wave[None, :] % count)
    edge = (ids == 0) | (ids == middle)
    weight = np.where(edge, 1.0 / math.sqrt(count), math.sqrt(2.0 / count))
    basis = np.where((ids <= middle)[None, :], np.cos(angle), np.sin(angle)) * weight[None, :]
    basis = basis.astype(np.float32)
    high = basis.astype(jnp.bfloat16)
    low = (basis - high.astype(np.float32)).astype(jnp.bfloat16)
    return high, low, wave.astype(np.int32)


def packed_rows(rows, width):
    return rows * width // LANES


def store_packed(ref, index, value):
    rows, width = value.shape
    full = width // LANES
    for tile in range(full):
        ref[(*index, pl.ds(tile * rows, rows), slice(None))] = value[:, tile * LANES : (tile + 1) * LANES]
    if width % LANES:
        rest = value[:, full * LANES :]
        half = rows // 2
        ref[(*index, pl.ds(full * rows, half), slice(None))] = jnp.concatenate([rest[:half], rest[half:]], axis=1)


def load_tile(ref, index, rows, width, tile):
    full = width // LANES
    if tile < full:
        return ref[(*index, pl.ds(tile * rows, rows), slice(None))]
    half = rows // 2
    both = ref[(*index, pl.ds(full * rows, half), slice(None))]
    return jnp.concatenate([both[:, : LANES // 2], both[:, LANES // 2 :]], axis=0)


def tile_count(width):
    return -(-width // LANES)


def wrapped(me, step, peers):
    other = me + step
    return jnp.where(other >= peers, other - peers, other)


def advect_row(row, coef, zonal, merid, t, h, t_s, h_s, t_n, h_n, w_n):
    u = zonal * (0.5 * COURANT)
    w_n = w_n * coef[1, row]
    w_s = merid * coef[0, row]
    for x, x_s, x_n in ((t, t_s, t_n), (h, h_s, h_n)):
        flux = u * (x + jnp.roll(x, 1, axis=1))
        yield x - (jnp.roll(flux, -1, axis=1) - flux) - (w_n * (x_n + x) - w_s * (x + x_s))


def edges_kernel(merid, thick, theta, ground, to_north, to_south, thick_s, theta_s, merid_s, ground_s, sems):
    lat_rows, levels, _ = thick.shape
    top = lat_rows - 1
    copies = []
    for source, target in ((thick, thick_s), (theta, theta_s)):
        copies += [(source.at[pl.ds(0, 1)], target.at[pl.ds(0, 1)]), (source.at[pl.ds(top, 1)], target.at[pl.ds(1, 1)])]
    wait_all(copy_all([*copies, (merid.at[pl.ds(0, 1)], merid_s), (ground, ground_s)], sems))
    to_north[pl.ds(0, levels), :] = thick_s[1]
    to_north[pl.ds(levels, levels), :] = theta_s[1] * thick_s[1]
    to_north[pl.ds(2 * levels, 1), :] = ground_s[pl.ds(top, 1), :]
    to_south[pl.ds(0, levels), :] = thick_s[0]
    to_south[pl.ds(levels, levels), :] = theta_s[0] * thick_s[0]
    to_south[pl.ds(2 * levels, levels), :] = merid_s[0]


def advect_kernel(first, rows_each, peers, coef, halo, *refs):
    fields, outs, held, sems = refs[:4], refs[4 : 4 + peers], refs[4 + peers : -1], refs[-1]
    lat_rows, levels, _ = fields[0].shape
    top = lat_rows - 1
    me = lax.axis_index("lev")
    part = lambda i: halo[pl.ds(i * levels, levels), :]
    owned = [first + wrapped(me, step, peers) * rows_each for step in range(peers)]
    reach = ((0, rows_each), (0, rows_each + 1), (1, rows_each + 2), (1, rows_each + 2))
    starts = [[jnp.clip(row - before, 0, lat_rows - count) for before, count in reach] for row in owned]
    arriving = [
        copy_all(
            [
                (field.at[pl.ds(start, count)], target.at[step])
                for field, target, start, (_, count) in zip(fields, held, starts[step], reach)
            ],
            sems,
            4 * step,
        )
        for step in range(peers)
    ]
    for step in range(peers):
        wait_all(arriving[step])
        zonal, merid, thick, theta = (ref.at[step] for ref in held)
        z_at, w_at, t_at, _ = (owned[step] - start for start in starts[step])
        for place in range(rows_each):
            row = owned[step] + place
            at = t_at + place
            low, high = jnp.maximum(at - 1, 0), jnp.minimum(at + 1, rows_each + 1)
            t, t_s, t_n = thick[at], thick[low], thick[high]
            h, h_s, h_n = theta[at] * t, theta[low] * t_s, theta[high] * t_n
            w, w_n = merid[w_at + place], merid[jnp.minimum(w_at + place + 1, rows_each)]
            if first == 0 and place == 0:
                t_s = jnp.where(row == 0, part(0), t_s)
                h_s = jnp.where(row == 0, part(1), h_s)
            if first + peers * rows_each == lat_rows and place == rows_each - 1:
                t_n = jnp.where(row == top, part(0), t_n)
                h_n = jnp.where(row == top, part(1), h_n)
                w_n = jnp.where(row == top, part(2), w_n)
            fields_new = advect_row(row, coef, zonal[z_at + place], w, t, h, t_s, h_s, t_n, h_n, w_n)
            for field, new in enumerate(fields_new):
                store_packed(outs[step], (place, field), new)


def target_edges(surface, sigma):
    curve = sigma * sigma
    return TOP_PRESSURE + HYBRID_SCALE * (sigma - curve) + (surface - TOP_PRESSURE) * curve


def target_thickness(surface, first, levels):
    step = 1.0 / levels
    curve = (2.0 * first + 1.0) * (step * step)
    return HYBRID_SCALE * (step - curve) + (surface - TOP_PRESSURE) * curve


def exner(pressure):
    return jnp.exp(EXNER_POWER * jnp.log(pressure))


def split_dot(x, ones):
    a = x.astype(BF16)
    r = x - a.astype(F32)
    b = r.astype(BF16)
    c = (r - b.astype(F32)).astype(BF16)
    dot = lambda v: jnp.dot(v, ones, preferred_element_type=F32)
    return dot(a) + (dot(b) + dot(c))

def remap_kernel(width, block, peers, *refs):
    parts = refs[:peers]
    gathered, spread, base_rows, base_s = refs[-4:]
    outs = refs[-4 - peers : -4]
    me = lax.axis_index("lev")
    count = parts[0].shape[0]
    levels = peers * block
    level_r = lax.broadcasted_iota(jnp.int32, (levels, levels), 0)
    level_c = lax.broadcasted_iota(jnp.int32, (levels, levels), 1)
    running = (level_r <= level_c).astype(F32).astype(BF16)
    below = (
        lax.broadcasted_iota(jnp.int32, (8, levels), 1)
        >= block * (1 + lax.broadcasted_iota(jnp.int32, (8, levels), 0))
    ).astype(F32)
    full = width // LANES
    data_rows = packed_rows(block, width)
    half = block // 2
    sources = [wrapped(me, (peers - step) % peers, peers) for step in range(peers)]
    targets = [wrapped(me, step, peers) for step in range(peers)]
    for place in range(count):
        for step in range(peers):
            at = pl.ds(pl.multiple_of(sources[step] * block, block), block)
            for field in range(2):
                for tile in range(tile_count(width)):
                    cols = min(LANES, width - tile * LANES)
                    gathered[place, field, at, pl.ds(tile * LANES, cols)] = load_tile(
                        parts[step], (place, field), block, width, tile)
    for place in range(count):
        cols = width
        here = pl.ds(0, cols)
        thick = gathered[place, 0, :, here]
        surface_row = TOP_PRESSURE + jnp.sum(thick, axis=0, keepdims=True)
        thick = thick.T
        heat = gathered[place, 1, :, here].T
        upper = TOP_PRESSURE + split_dot(thick, running)
        theta = heat / thick
        offset = split_dot(heat, running) - theta * upper
        surface = upper[:, levels - 1 :]
        lane = lax.broadcasted_iota(jnp.int32, (cols, levels), 1)
        lane_f = lane.astype(F32)
        edge = target_edges(surface, (lane_f + 1.0) * (1.0 / levels))
        at = jnp.zeros((cols, levels), jnp.int32)
        jump = levels // 2
        while jump:
            probe = jnp.take_along_axis(upper, at + (jump - 1), axis=1, mode="promise_in_bounds")
            at = jnp.where(probe < edge, at + jump, at)
            jump //= 2
        pick = lambda table: jnp.take_along_axis(table, at, axis=1, mode="promise_in_bounds")
        heat_to = pick(offset) + pick(theta) * edge
        heat_from = jnp.where(lane == 0, 0.0, pltpu.roll(heat_to, 1, 1))
        theta_next = (heat_to - heat_from) / target_thickness(surface, lane_f, levels)
        exner_to = exner(edge)
        exner_from = jnp.where(lane == 0, TOP_PRESSURE**EXNER_POWER, pltpu.roll(exner_to, 1, 1))
        layer = theta_next * (exner_to - exner_from)
        bases = lax.dot_general(
            below, layer, (((1,), (1,)), ((), ())), precision=HIGHEST, preferred_element_type=F32
        )
        base_s[place, :, here] = bases
        base_s[place, pl.ds(7, 1), here] = surface_row
        spread[place, :, here] = theta_next.T
    for place in range(count):
        for tile in range(tile_count(width)):
            base_rows[place, tile] = base_s[place, :, pl.ds(tile * LANES, LANES)]
        for step in range(peers):
            out = outs[step]
            start = pl.multiple_of(targets[step] * block, block)
            for tile in range(tile_count(width)):
                cols = min(LANES, width - tile * LANES)
                here = pl.ds(tile * LANES, cols)
                if tile < full:
                    out[place, pl.ds(tile * block, block), :] = spread[place, pl.ds(start, block), here]
                else:
                    part = spread[place, pl.ds(start, block), here]
                    out[place, pl.ds(full * block, half), :] = jnp.concatenate([part[:half], part[half:]], axis=1)
                out[place, pl.ds(data_rows + tile, 1), pl.ds(0, cols)] = base_rows[place, tile, pl.ds(7, 1), pl.ds(0, cols)]
                out[place, pl.ds(data_rows + 8 + tile, 1), pl.ds(0, cols)] = base_rows[place, tile, pl.ds(targets[step], 1), pl.ds(0, cols)]


def below_sum(layer):
    rows, width = layer.shape
    groups = rows // 8
    carry = None
    pieces = []
    sub = lax.broadcasted_iota(jnp.int32, (8, width), 0)
    for g in reversed(range(groups)):
        x = layer[g * 8 : (g + 1) * 8]
        total = x
        for step in (1, 2, 4):
            total = total + jnp.where(sub < 8 - step, pltpu.roll(total, 8 - step, 0), 0.0)
        under = total - x
        if carry is not None:
            under = under + carry
            carry = carry + total[0:1]
        else:
            carry = total[0:1]
        pieces.append(under)
    return jnp.concatenate(pieces[::-1], axis=0)


def column_state(message, index, block, width, first_level, levels, ground):
    tiles = tile_count(width)
    data_rows = packed_rows(block, width)
    theta = jnp.concatenate([load_tile(message, index, block, width, t) for t in range(tiles)], axis=1)

    def line(first):
        return jnp.concatenate(
            [message[(*index, pl.ds(first + t, 1), pl.ds(0, min(LANES, width - t * LANES)))] for t in range(tiles)],
            axis=1,
        )

    surface = line(data_rows)
    base = line(data_rows + 8)
    sub = lax.broadcasted_iota(jnp.int32, (block, width), 0).astype(F32) + first_level
    thick = target_thickness(surface, sub, levels)
    top = exner(target_edges(surface, sub * (1.0 / levels)))
    bottom_edge = exner(target_edges(surface, (first_level + block) * (1.0 / levels)))
    sub_i = lax.broadcasted_iota(jnp.int32, (block, width), 0)
    bottom = jnp.where(sub_i == block - 1, bottom_edge, pltpu.roll(top, block - 1, 0))
    layer = theta * (bottom - top)
    geopot = (ground + base) + (below_sum(layer) + 0.5 * layer)
    return theta, thick, 0.5 * (top + bottom), geopot


def push(now, before):
    theta, exner_mid, geopot = now
    theta_b, exner_b, geopot_b = before
    return (geopot - geopot_b) + 0.5 * (theta + theta_b) * (exner_mid - exner_b)


def filtered(value, table, high, low, high_t, low_t, block):
    def product(x, b_high, b_low):
        x_high = x.astype(BF16)
        x_low = (x - x_high.astype(F32)).astype(BF16)
        dot = lambda a, b: jnp.dot(a, b, preferred_element_type=F32)
        return dot(x_high, b_high) + (dot(x_low, b_high) + dot(x_high, b_low))

    spectral = product(value, high, low)
    rows, width = value.shape
    spectral = (spectral.reshape(rows // block, block, width) * table[:, None, :]).reshape(rows, width)
    return value + product(spectral, high_t, low_t)


def gather_messages(me, parts, order):
    peers = len(parts)
    for step, part in enumerate(parts):
        owner = wrapped(me, (peers - step) % peers, peers)
        for place in range(part.shape[0]):
            order[owner * part.shape[0] + place] = part[place]


def copy_all(copies, sems, first=0):
    started = [pltpu.make_async_copy(source, target, sems.at[first + i]) for i, (source, target) in enumerate(copies)]
    for copy in started:
        copy.start()
    return started


def wait_all(copies):
    for copy in copies:
        copy.wait()


def filter_rows(ref, count, table, tables, block):
    width = ref.shape[-1]
    value = ref[pl.ds(0, count)].reshape(count * block, width)
    value = filtered(value, table, *(t[...] for t in tables), block)
    ref[pl.ds(0, count)] = value.reshape(count, block, width)


def around(x):
    return jnp.roll(x, 1, axis=1)


def upper_final_kernel(
    levels, first, flag, faces, p0, p1, p2, p3, ground, table, zonal, merid, b0, b1, b2, b3, after,
    zonal_out, merid_out, thick_out, theta_out, edge_state,
    order, zonal_s, merid_s, thick_s, theta_s, carried, sems,
):
    del after
    lat_rows, block, width = zonal.shape
    count = lat_rows - first
    rows = pl.ds(first, count)
    me = lax.axis_index("lev")
    level = (me * block).astype(F32)
    gather_messages(me, (p0, p1, p2, p3), order)
    carried[...] = jnp.zeros_like(carried)

    def one_row(i, _):
        row = first + i
        theta, thick, mid, geopot = column_state(order, (i,), block, width, level, levels, ground[pl.ds(row, 1), :])
        theta_s[i] = theta
        thick_s[i] = thick
        now = (theta, mid, geopot)
        zonal_s[i] = zonal[row] - push(now, tuple(around(x) for x in now))
        before = (carried[0], carried[1], carried[2])
        merid_s[jnp.maximum(i - 1, 0)] = merid[row] - faces[row] * push(now, before)
        for field, x in enumerate(now):
            carried[field] = x

        @pl.when(i == 0)
        def _():
            for field, x in enumerate(now):
                edge_state[field] = x

        return 0

    lax.fori_loop(0, count, one_row, 0)
    early = copy_all([(theta_s, theta_out.at[rows]), (thick_s, thick_out.at[rows])], sems)

    @pl.when(flag[0] != 0)
    def _():
        tables = (b0, b1, b2, b3)
        filter_rows(zonal_s, count, table[rows, :], tables, block)

    early += copy_all([(zonal_s, zonal_out.at[rows])], sems, 2)

    @pl.when(flag[0] != 0)
    def _():
        tables = (b0, b1, b2, b3)
        filter_rows(merid_s, count - 1, table[pl.ds(first + 1, count - 1), :], tables, block)

    late = copy_all([(merid_s.at[pl.ds(0, count - 1)], merid_out.at[pl.ds(first + 1, count - 1)])], sems, 3)
    wait_all(early + late)


def lower_final_kernel(
    levels, flag, faces, south, halo_s, edge_state, p0, p1, p2, p3, ground, table, zonal, merid, b0, b1, b2, b3,
    zonal_in, merid_in, thick_in, theta_in,
    zonal_out, merid_out, thick_out, theta_out,
    order, winds_s, thick_s, theta_s, sems,
):
    del zonal_in, merid_in, thick_in, theta_in
    count = order.shape[0]
    _, block, width = zonal.shape
    me = lax.axis_index("lev")
    level = (me * block).astype(F32)
    gather_messages(me, (p0, p1, p2, p3), order)
    state = lambda ref, i, line: column_state(ref, (i,), block, width, level, levels, line)
    theta, _, mid, geopot = state(south, 0, halo_s[pl.ds(2 * block, 1), :])
    before = (theta, mid, geopot)
    for row in range(count):
        theta, thick, mid, geopot = state(order, row, ground[pl.ds(row, 1), :])
        theta_s[row] = theta
        thick_s[row] = thick
        now = (theta, mid, geopot)
        winds_s[row] = zonal[row] - push(now, tuple(around(x) for x in now))
        winds_s[count + row] = merid[row] - faces[row] * push(now, before)
        before = now
    now = tuple(edge_state[field] for field in range(3))
    winds_s[2 * count] = merid[count] - faces[count] * push(now, before)
    rows = pl.ds(0, count)
    early = copy_all([(theta_s, theta_out.at[rows]), (thick_s, thick_out.at[rows])], sems)

    @pl.when(flag[0] != 0)
    def _():
        picked = jnp.concatenate([table[rows, :], table[pl.ds(0, count + 1), :]], axis=0)
        filter_rows(winds_s, 2 * count + 1, picked, (b0, b1, b2, b3), block)

    late = copy_all(
        [
            (winds_s.at[rows], zonal_out.at[rows]),
            (winds_s.at[pl.ds(count, count + 1)], merid_out.at[pl.ds(0, count + 1)]),
        ],
        sems,
        2,
    )
    wait_all(early + late)


def exchanged(parts):
    peers = lax.axis_size("lev")
    return [parts[0]] + [
        lax.ppermute(parts[step], "lev", [(i, (i + step) % peers) for i in range(peers)]) for step in range(1, peers)
    ]


def body(
    zonal_wind, meridional_wind, thickness, potential_temp, surface_geo, polar_mask, cutoff, damping
):
    lat_rows, block, width = zonal_wind.shape
    lat_count = lax.axis_size("lat")
    peers = lax.axis_size("lev")
    levels = block * peers
    total_rows = lat_rows * lat_count
    first_row = lax.axis_index("lat") * lat_rows
    row_ids = (first_row + jnp.arange(lat_rows + 1, dtype=jnp.int32)).astype(F32)
    faces = jnp.sin(math.pi * row_ids / total_rows)
    centres = jnp.sin(math.pi * (row_ids[:-1] + 0.5) / total_rows)
    coef = jnp.stack([faces[:-1], faces[1:]]) * (0.5 * COURANT) / centres
    northward = [(i, i + 1) for i in range(lat_count - 1)]
    southward = [(i + 1, i) for i in range(lat_count - 1)]
    flag = jnp.any(polar_mask != 0).astype(jnp.int32).reshape(1)
    shape = lambda *dims: jax.ShapeDtypeStruct(dims, F32)
    hbm = pl.BlockSpec(memory_space=pltpu.HBM)
    rows_of = lambda n: pltpu.VMEM((n, block, width), F32)
    dma = lambda n: pltpu.SemaphoreType.DMA((n,))

    lower_each = 1
    upper_each = lat_rows // peers - lower_each
    first = lower_each * peers
    upper = lat_rows - first
    data_rows = packed_rows(block, width)
    message_rows = data_rows + 16
    stay = lambda *arrays: [pltpu.with_memory_space_constraint(x, pltpu.HBM) for x in arrays]
    field = shape(lat_rows, block, width)

    fields = stay(zonal_wind, meridional_wind, thickness, potential_temp)
    to_north, to_south = pl.pallas_call(
        edges_kernel,
        out_shape=[shape(2 * block + 8, width), shape(3 * block, width)],
        in_specs=[hbm] * 4,
        out_specs=[VMEM] * 2,
        scratch_shapes=[rows_of(2), rows_of(2), rows_of(1), pltpu.VMEM((lat_rows, width), F32), dma(6)],
        compiler_params=params(8),
        cost_estimate=cost(1),
        name="edges",
    )(*fields[1:], *stay(surface_geo))
    halo_n = lax.ppermute(to_south, "lat", southward)
    halo_s = lax.ppermute(to_north, "lat", northward)

    def advect(start, each, halo, name):
        return pl.pallas_call(
            lambda *refs: advect_kernel(start, each, peers, *refs),
            out_shape=[shape(each, 2, data_rows, LANES)] * peers,
            in_specs=[SMEM, VMEM] + [hbm] * 4,
            out_specs=[VMEM] * peers,
            scratch_shapes=[
                pltpu.VMEM((peers, each + extra, block, width), F32) for extra in (0, 1, 2, 2)
            ]
            + [dma(4 * peers)],
            compiler_params=params(12),
            cost_estimate=cost(1 + 2 * each),
            name=name,
        )(coef, halo, *fields)

    upper_columns = exchanged(advect(first, upper_each, halo_n, "advect_upper"))
    lower_sent = advect(0, lower_each, halo_s, "advect_lower")
    upper_columns[1], *lower_sent = lax.optimization_barrier((upper_columns[1], *lower_sent))
    lower_columns = exchanged(lower_sent)

    def remap(columns, each, name, after):
        lanes = tile_count(width) * LANES
        return pl.pallas_call(
            lambda *refs: remap_kernel(width, block, peers, *refs),
            out_shape=[shape(each, message_rows, LANES)] * peers,
            in_specs=[VMEM] * peers + [pl.BlockSpec(memory_space=pl.ANY)] * len(after),
            out_specs=[VMEM] * peers,
            scratch_shapes=[
                pltpu.VMEM((each, 2, levels, lanes), F32),
                pltpu.VMEM((each, levels, lanes), F32),
                pltpu.VMEM((each, tile_count(width), 8, LANES), F32),
                pltpu.VMEM((each, 8, lanes), F32),
            ],
            compiler_params=params(12),
            cost_estimate=cost(3 * each - 2.8),
            name=name,
        )(*columns, *after)

    upper_remapped = remap(upper_columns, upper_each, "remap_upper", lower_columns[:1])
    upper_messages = exchanged(upper_remapped)
    lower_remapped = remap(lower_columns, lower_each, "remap_lower", upper_remapped[:1])
    lower_messages = exchanged(lower_remapped)
    step_of_last = (lax.axis_index("lev") + 1) % peers
    _, *candidates = lax.optimization_barrier((lower_remapped[0], *upper_messages))
    last_message = candidates[0][-1:]
    for step in range(1, peers):
        last_message = jnp.where(step_of_last == step, candidates[step][-1:], last_message)
    south = lax.ppermute(last_message, "lat", northward)

    high, low, wave = fourier_tables(width)
    active = (jnp.asarray(wave)[None, :] >= cutoff[:, None]) & (polar_mask[:, None] != 0)
    table = jnp.where(active, damping - 1.0, 0.0)
    tables = [jnp.asarray(x) for x in (high, low, np.ascontiguousarray(high.T), np.ascontiguousarray(low.T))]

    *partial, edge_state = pl.pallas_call(
        lambda *refs: upper_final_kernel(levels, first, *refs),
        out_shape=[field] * 4 + [shape(3, block, width)],
        in_specs=[SMEM] * 2 + [VMEM] * (peers + 8) + [pl.BlockSpec(memory_space=pl.ANY)],
        out_specs=[hbm] * 4 + [VMEM],
        scratch_shapes=[pltpu.VMEM((upper, message_rows, LANES), F32)]
        + [rows_of(upper)] * 4
        + [rows_of(3), dma(4)],
        compiler_params=params(18),
        cost_estimate=cost(7),
        name="final_upper",
    )(
        flag, faces, *upper_messages, surface_geo, table, zonal_wind, meridional_wind, *tables, lower_remapped[0]
    )
    edge_state, *lower_messages = lax.optimization_barrier((edge_state, *lower_messages))
    return tuple(
        pl.pallas_call(
            lambda *refs: lower_final_kernel(levels, *refs),
            out_shape=[field] * 4,
            in_specs=[SMEM] * 2 + [VMEM] * (peers + 11) + [hbm] * 4,
            out_specs=[hbm] * 4,
            scratch_shapes=[pltpu.VMEM((first, message_rows, LANES), F32)]
            + [rows_of(2 * first + 1), rows_of(first), rows_of(first), dma(4)],
            input_output_aliases={peers + 13 + i: i for i in range(4)},
            compiler_params=params(16),
            cost_estimate=cost(6),
            name="final_lower",
        )(
            flag, faces, south, halo_s, edge_state, *lower_messages, surface_geo, table, zonal_wind, meridional_wind, *tables,
            *partial,
        )
    )


def solution(mesh):
    field = P("lat", "lev", None)
    in_specs = (field, field, field, field, P("lat", None), P("lat"), P("lat"), P("lat", None))
    return jax.shard_map(body, mesh=mesh, in_specs=in_specs, out_specs=(field,) * 4, check_vma=False)
```

```python
import math

import jax
import jax.numpy as jnp
import numpy as np
from jax import lax
from jax.experimental import pallas as pl
from jax.experimental.pallas import tpu as pltpu
from jax.sharding import PartitionSpec as P

TOP_PRESSURE = 0.01
HYBRID_SCALE = 0.2
EXNER_POWER = 2.0 / 7.0
COURANT = 0.012
HIGHEST = lax.Precision.HIGHEST
F32 = jnp.float32
BF16 = jnp.bfloat16
VMEM = pl.BlockSpec(memory_space=pltpu.VMEM)
SMEM = pl.BlockSpec(memory_space=pltpu.SMEM)
LANES = 128


def params(mib):
    return pltpu.CompilerParams(vmem_limit_bytes=mib * 1024 * 1024)


def cost(microseconds):
    return pl.CostEstimate(
        flops=int(microseconds * 1.1e9), bytes_accessed=int(microseconds * 3.6e6), transcendentals=0
    )


def fourier_tables(count):
    middle = count // 2
    ids = np.arange(count)
    wave = np.where(ids <= middle, ids, ids - middle)
    angle = 2.0 * np.pi / count * (ids[:, None] * wave[None, :] % count)
    edge = (ids == 0) | (ids == middle)
    weight = np.where(edge, 1.0 / math.sqrt(count), math.sqrt(2.0 / count))
    basis = np.where((ids <= middle)[None, :], np.cos(angle), np.sin(angle)) * weight[None, :]
    basis = basis.astype(np.float32)
    high = basis.astype(jnp.bfloat16)
    low = (basis - high.astype(np.float32)).astype(jnp.bfloat16)
    return high, low, wave.astype(np.int32)


def packed_rows(rows, width):
    return rows * width // LANES


def store_packed(ref, index, value):
    rows, width = value.shape
    full = width // LANES
    for tile in range(full):
        ref[(*index, pl.ds(tile * rows, rows), slice(None))] = value[:, tile * LANES : (tile + 1) * LANES]
    if width % LANES:
        rest = value[:, full * LANES :]
        half = rows // 2
        ref[(*index, pl.ds(full * rows, half), slice(None))] = jnp.concatenate([rest[:half], rest[half:]], axis=1)


def load_tile(ref, index, rows, width, tile):
    full = width // LANES
    if tile < full:
        return ref[(*index, pl.ds(tile * rows, rows), slice(None))]
    half = rows // 2
    both = ref[(*index, pl.ds(full * rows, half), slice(None))]
    return jnp.concatenate([both[:, : LANES // 2], both[:, LANES // 2 :]], axis=0)


def tile_count(width):
    return -(-width // LANES)


def wrapped(me, step, peers):
    other = me + step
    return jnp.where(other >= peers, other - peers, other)


def advect_row(row, coef, zonal, merid, t, h, t_s, h_s, t_n, h_n, w_n):
    u = zonal * (0.5 * COURANT)
    w_n = w_n * coef[1, row]
    w_s = merid * coef[0, row]
    for x, x_s, x_n in ((t, t_s, t_n), (h, h_s, h_n)):
        flux = u * (x + jnp.roll(x, 1, axis=1))
        yield x - (jnp.roll(flux, -1, axis=1) - flux) - (w_n * (x_n + x) - w_s * (x + x_s))


def edges_kernel(merid, thick, theta, ground, to_north, to_south, thick_s, theta_s, merid_s, ground_s, sems):
    lat_rows, levels, _ = thick.shape
    top = lat_rows - 1
    copies = []
    for source, target in ((thick, thick_s), (theta, theta_s)):
        copies += [(source.at[pl.ds(0, 1)], target.at[pl.ds(0, 1)]), (source.at[pl.ds(top, 1)], target.at[pl.ds(1, 1)])]
    wait_all(copy_all([*copies, (merid.at[pl.ds(0, 1)], merid_s), (ground, ground_s)], sems))
    to_north[pl.ds(0, levels), :] = thick_s[1]
    to_north[pl.ds(levels, levels), :] = theta_s[1] * thick_s[1]
    to_north[pl.ds(2 * levels, 1), :] = ground_s[pl.ds(top, 1), :]
    to_south[pl.ds(0, levels), :] = thick_s[0]
    to_south[pl.ds(levels, levels), :] = theta_s[0] * thick_s[0]
    to_south[pl.ds(2 * levels, levels), :] = merid_s[0]


def advect_kernel(first, rows_each, peers, coef, halo, *refs):
    fields, outs, held, sems = refs[:4], refs[4 : 4 + peers], refs[4 + peers : -1], refs[-1]
    lat_rows, levels, _ = fields[0].shape
    top = lat_rows - 1
    me = lax.axis_index("lev")
    part = lambda i: halo[pl.ds(i * levels, levels), :]
    owned = [first + wrapped(me, step, peers) * rows_each for step in range(peers)]
    reach = ((0, rows_each), (0, rows_each + 1), (1, rows_each + 2), (1, rows_each + 2))
    starts = [[jnp.clip(row - before, 0, lat_rows - count) for before, count in reach] for row in owned]
    arriving = [
        copy_all(
            [
                (field.at[pl.ds(start, count)], target.at[step])
                for field, target, start, (_, count) in zip(fields, held, starts[step], reach)
            ],
            sems,
            4 * step,
        )
        for step in range(peers)
    ]
    for step in range(peers):
        wait_all(arriving[step])
        zonal, merid, thick, theta = (ref.at[step] for ref in held)
        z_at, w_at, t_at, _ = (owned[step] - start for start in starts[step])
        for place in range(rows_each):
            row = owned[step] + place
            at = t_at + place
            low, high = jnp.maximum(at - 1, 0), jnp.minimum(at + 1, rows_each + 1)
            t, t_s, t_n = thick[at], thick[low], thick[high]
            h, h_s, h_n = theta[at] * t, theta[low] * t_s, theta[high] * t_n
            w, w_n = merid[w_at + place], merid[jnp.minimum(w_at + place + 1, rows_each)]
            if first == 0 and place == 0:
                t_s = jnp.where(row == 0, part(0), t_s)
                h_s = jnp.where(row == 0, part(1), h_s)
            if first + peers * rows_each == lat_rows and place == rows_each - 1:
                t_n = jnp.where(row == top, part(0), t_n)
                h_n = jnp.where(row == top, part(1), h_n)
                w_n = jnp.where(row == top, part(2), w_n)
            fields_new = advect_row(row, coef, zonal[z_at + place], w, t, h, t_s, h_s, t_n, h_n, w_n)
            for field, new in enumerate(fields_new):
                store_packed(outs[step], (place, field), new)


def target_edges(surface, sigma):
    curve = sigma * sigma
    return TOP_PRESSURE + HYBRID_SCALE * (sigma - curve) + (surface - TOP_PRESSURE) * curve


def target_thickness(surface, first, levels):
    step = 1.0 / levels
    curve = (2.0 * first + 1.0) * (step * step)
    return HYBRID_SCALE * (step - curve) + (surface - TOP_PRESSURE) * curve


def exner(pressure):
    return jnp.exp(EXNER_POWER * jnp.log(pressure))


def split_dot(x, ones):
    a = x.astype(BF16)
    r = x - a.astype(F32)
    b = r.astype(BF16)
    c = (r - b.astype(F32)).astype(BF16)
    dot = lambda v: jnp.dot(v, ones, preferred_element_type=F32)
    return dot(a) + (dot(b) + dot(c))

def remap_kernel(width, block, peers, *refs):
    parts = refs[:peers]
    gathered, spread, base_rows, base_s = refs[-4:]
    outs = refs[-4 - peers : -4]
    me = lax.axis_index("lev")
    count = parts[0].shape[0]
    levels = peers * block
    level_r = lax.broadcasted_iota(jnp.int32, (levels, levels), 0)
    level_c = lax.broadcasted_iota(jnp.int32, (levels, levels), 1)
    running = (level_r <= level_c).astype(F32).astype(BF16)
    below = (
        lax.broadcasted_iota(jnp.int32, (8, levels), 1)
        >= block * (1 + lax.broadcasted_iota(jnp.int32, (8, levels), 0))
    ).astype(F32)
    full = width // LANES
    data_rows = packed_rows(block, width)
    half = block // 2
    sources = [wrapped(me, (peers - step) % peers, peers) for step in range(peers)]
    targets = [wrapped(me, step, peers) for step in range(peers)]
    for place in range(count):
        for step in range(peers):
            at = pl.ds(pl.multiple_of(sources[step] * block, block), block)
            for field in range(2):
                for tile in range(tile_count(width)):
                    cols = min(LANES, width - tile * LANES)
                    gathered[place, field, at, pl.ds(tile * LANES, cols)] = load_tile(
                        parts[step], (place, field), block, width, tile)
    for place in range(count):
        cols = width
        here = pl.ds(0, cols)
        thick = gathered[place, 0, :, here]
        surface_row = TOP_PRESSURE + jnp.sum(thick, axis=0, keepdims=True)
        thick = thick.T
        heat = gathered[place, 1, :, here].T
        upper = TOP_PRESSURE + split_dot(thick, running)
        theta = heat / thick
        offset = split_dot(heat, running) - theta * upper
        surface = upper[:, levels - 1 :]
        lane = lax.broadcasted_iota(jnp.int32, (cols, levels), 1)
        lane_f = lane.astype(F32)
        edge = target_edges(surface, (lane_f + 1.0) * (1.0 / levels))
        at = jnp.zeros((cols, levels), jnp.int32)
        jump = levels // 2
        while jump:
            probe = jnp.take_along_axis(upper, at + (jump - 1), axis=1, mode="promise_in_bounds")
            at = jnp.where(probe < edge, at + jump, at)
            jump //= 2
        pick = lambda table: jnp.take_along_axis(table, at, axis=1, mode="promise_in_bounds")
        heat_to = pick(offset) + pick(theta) * edge
        heat_from = jnp.where(lane == 0, 0.0, pltpu.roll(heat_to, 1, 1))
        theta_next = (heat_to - heat_from) / target_thickness(surface, lane_f, levels)
        exner_to = exner(edge)
        exner_from = jnp.where(lane == 0, TOP_PRESSURE**EXNER_POWER, pltpu.roll(exner_to, 1, 1))
        layer = theta_next * (exner_to - exner_from)
        bases = lax.dot_general(
            below, layer, (((1,), (1,)), ((), ())), precision=HIGHEST, preferred_element_type=F32
        )
        base_s[place, :, here] = bases
        base_s[place, pl.ds(7, 1), here] = surface_row
        spread[place, :, here] = theta_next.T
    for place in range(count):
        for tile in range(tile_count(width)):
            base_rows[place, tile] = base_s[place, :, pl.ds(tile * LANES, LANES)]
        for step in range(peers):
            out = outs[step]
            start = pl.multiple_of(targets[step] * block, block)
            for tile in range(tile_count(width)):
                cols = min(LANES, width - tile * LANES)
                here = pl.ds(tile * LANES, cols)
                if tile < full:
                    out[place, pl.ds(tile * block, block), :] = spread[place, pl.ds(start, block), here]
                else:
                    part = spread[place, pl.ds(start, block), here]
                    out[place, pl.ds(full * block, half), :] = jnp.concatenate([part[:half], part[half:]], axis=1)
                out[place, pl.ds(data_rows + tile, 1), pl.ds(0, cols)] = base_rows[place, tile, pl.ds(7, 1), pl.ds(0, cols)]
                out[place, pl.ds(data_rows + 8 + tile, 1), pl.ds(0, cols)] = base_rows[place, tile, pl.ds(targets[step], 1), pl.ds(0, cols)]


def below_sum(layer):
    rows, width = layer.shape
    groups = rows // 8
    carry = None
    pieces = []
    sub = lax.broadcasted_iota(jnp.int32, (8, width), 0)
    for g in reversed(range(groups)):
        x = layer[g * 8 : (g + 1) * 8]
        total = x
        for step in (1, 2, 4):
            total = total + jnp.where(sub < 8 - step, pltpu.roll(total, 8 - step, 0), 0.0)
        under = total - x
        if carry is not None:
            under = under + carry
            carry = carry + total[0:1]
        else:
            carry = total[0:1]
        pieces.append(under)
    return jnp.concatenate(pieces[::-1], axis=0)


def column_state(message, index, block, width, first_level, levels, ground):
    tiles = tile_count(width)
    data_rows = packed_rows(block, width)
    theta = jnp.concatenate([load_tile(message, index, block, width, t) for t in range(tiles)], axis=1)

    def line(first):
        return jnp.concatenate(
            [message[(*index, pl.ds(first + t, 1), pl.ds(0, min(LANES, width - t * LANES)))] for t in range(tiles)],
            axis=1,
        )

    surface = line(data_rows)
    base = line(data_rows + 8)
    sub = lax.broadcasted_iota(jnp.int32, (block, width), 0).astype(F32) + first_level
    thick = target_thickness(surface, sub, levels)
    top = exner(target_edges(surface, sub * (1.0 / levels)))
    bottom_edge = exner(target_edges(surface, (first_level + block) * (1.0 / levels)))
    sub_i = lax.broadcasted_iota(jnp.int32, (block, width), 0)
    bottom = jnp.where(sub_i == block - 1, bottom_edge, pltpu.roll(top, block - 1, 0))
    layer = theta * (bottom - top)
    geopot = (ground + base) + (below_sum(layer) + 0.5 * layer)
    return theta, thick, 0.5 * (top + bottom), geopot


def push(now, before):
    theta, exner_mid, geopot = now
    theta_b, exner_b, geopot_b = before
    return (geopot - geopot_b) + 0.5 * (theta + theta_b) * (exner_mid - exner_b)


def filtered(value, table, high, low, high_t, low_t, block):
    def product(x, b_high, b_low):
        x_high = x.astype(BF16)
        x_low = (x - x_high.astype(F32)).astype(BF16)
        dot = lambda a, b: jnp.dot(a, b, preferred_element_type=F32)
        return dot(x_high, b_high) + (dot(x_low, b_high) + dot(x_high, b_low))

    spectral = product(value, high, low)
    rows, width = value.shape
    spectral = (spectral.reshape(rows // block, block, width) * table[:, None, :]).reshape(rows, width)
    return value + product(spectral, high_t, low_t)


def gather_messages(me, parts, order):
    peers = len(parts)
    for step, part in enumerate(parts):
        owner = wrapped(me, (peers - step) % peers, peers)
        for place in range(part.shape[0]):
            order[owner * part.shape[0] + place] = part[place]


def copy_all(copies, sems, first=0):
    started = [pltpu.make_async_copy(source, target, sems.at[first + i]) for i, (source, target) in enumerate(copies)]
    for copy in started:
        copy.start()
    return started


def wait_all(copies):
    for copy in copies:
        copy.wait()


def filter_rows(ref, count, table, tables, block):
    width = ref.shape[-1]
    value = ref[pl.ds(0, count)].reshape(count * block, width)
    value = filtered(value, table, *(t[...] for t in tables), block)
    ref[pl.ds(0, count)] = value.reshape(count, block, width)


def around(x):
    return jnp.roll(x, 1, axis=1)


def upper_final_kernel(
    levels, first, flag, faces, p0, p1, p2, p3, ground, table, zonal, merid, b0, b1, b2, b3, after,
    zonal_out, merid_out, thick_out, theta_out, edge_state,
    order, zonal_s, merid_s, thick_s, theta_s, carried, sems,
):
    del after
    lat_rows, block, width = zonal.shape
    count = lat_rows - first
    rows = pl.ds(first, count)
    me = lax.axis_index("lev")
    level = (me * block).astype(F32)
    gather_messages(me, (p0, p1, p2, p3), order)
    carried[...] = jnp.zeros_like(carried)

    def one_row(i, _):
        row = first + i
        theta, thick, mid, geopot = column_state(order, (i,), block, width, level, levels, ground[pl.ds(row, 1), :])
        theta_s[i] = theta
        thick_s[i] = thick
        now = (theta, mid, geopot)
        zonal_s[i] = zonal[row] - push(now, tuple(around(x) for x in now))
        before = (carried[0], carried[1], carried[2])
        merid_s[jnp.maximum(i - 1, 0)] = merid[row] - faces[row] * push(now, before)
        for field, x in enumerate(now):
            carried[field] = x

        @pl.when(i == 0)
        def _():
            for field, x in enumerate(now):
                edge_state[field] = x

        return 0

    lax.fori_loop(0, count, one_row, 0)
    early = copy_all([(theta_s, theta_out.at[rows]), (thick_s, thick_out.at[rows])], sems)

    @pl.when(flag[0] != 0)
    def _():
        tables = (b0, b1, b2, b3)
        filter_rows(zonal_s, count, table[rows, :], tables, block)

    early += copy_all([(zonal_s, zonal_out.at[rows])], sems, 2)

    @pl.when(flag[0] != 0)
    def _():
        tables = (b0, b1, b2, b3)
        filter_rows(merid_s, count - 1, table[pl.ds(first + 1, count - 1), :], tables, block)

    late = copy_all([(merid_s.at[pl.ds(0, count - 1)], merid_out.at[pl.ds(first + 1, count - 1)])], sems, 3)
    wait_all(early + late)


def lower_final_kernel(
    levels, flag, faces, south, halo_s, edge_state, p0, p1, p2, p3, ground, table, zonal, merid, b0, b1, b2, b3,
    zonal_in, merid_in, thick_in, theta_in,
    zonal_out, merid_out, thick_out, theta_out,
    order, winds_s, thick_s, theta_s, sems,
):
    del zonal_in, merid_in, thick_in, theta_in
    count = order.shape[0]
    _, block, width = zonal.shape
    me = lax.axis_index("lev")
    level = (me * block).astype(F32)
    gather_messages(me, (p0, p1, p2, p3), order)
    state = lambda ref, i, line: column_state(ref, (i,), block, width, level, levels, line)
    theta, _, mid, geopot = state(south, 0, halo_s[pl.ds(2 * block, 1), :])
    before = (theta, mid, geopot)
    for row in range(count):
        theta, thick, mid, geopot = state(order, row, ground[pl.ds(row, 1), :])
        theta_s[row] = theta
        thick_s[row] = thick
        now = (theta, mid, geopot)
        winds_s[row] = zonal[row] - push(now, tuple(around(x) for x in now))
        winds_s[count + row] = merid[row] - faces[row] * push(now, before)
        before = now
    now = tuple(edge_state[field] for field in range(3))
    winds_s[2 * count] = merid[count] - faces[count] * push(now, before)
    rows = pl.ds(0, count)
    early = copy_all([(theta_s, theta_out.at[rows]), (thick_s, thick_out.at[rows])], sems)

    @pl.when(flag[0] != 0)
    def _():
        picked = jnp.concatenate([table[rows, :], table[pl.ds(0, count + 1), :]], axis=0)
        filter_rows(winds_s, 2 * count + 1, picked, (b0, b1, b2, b3), block)

    late = copy_all(
        [
            (winds_s.at[rows], zonal_out.at[rows]),
            (winds_s.at[pl.ds(count, count + 1)], merid_out.at[pl.ds(0, count + 1)]),
        ],
        sems,
        2,
    )
    wait_all(early + late)


def exchanged(parts):
    peers = lax.axis_size("lev")
    return [parts[0]] + [
        lax.ppermute(parts[step], "lev", [(i, (i + step) % peers) for i in range(peers)]) for step in range(1, peers)
    ]


def body(
    zonal_wind, meridional_wind, thickness, potential_temp, surface_geo, polar_mask, cutoff, damping
):
    lat_rows, block, width = zonal_wind.shape
    lat_count = lax.axis_size("lat")
    peers = lax.axis_size("lev")
    levels = block * peers
    total_rows = lat_rows * lat_count
    first_row = lax.axis_index("lat") * lat_rows
    row_ids = (first_row + jnp.arange(lat_rows + 1, dtype=jnp.int32)).astype(F32)
    faces = jnp.sin(math.pi * row_ids / total_rows)
    centres = jnp.sin(math.pi * (row_ids[:-1] + 0.5) / total_rows)
    coef = jnp.stack([faces[:-1], faces[1:]]) * (0.5 * COURANT) / centres
    northward = [(i, i + 1) for i in range(lat_count - 1)]
    southward = [(i + 1, i) for i in range(lat_count - 1)]
    flag = jnp.any(polar_mask != 0).astype(jnp.int32).reshape(1)
    shape = lambda *dims: jax.ShapeDtypeStruct(dims, F32)
    hbm = pl.BlockSpec(memory_space=pltpu.HBM)
    rows_of = lambda n: pltpu.VMEM((n, block, width), F32)
    dma = lambda n: pltpu.SemaphoreType.DMA((n,))

    lower_each = 1
    upper_each = lat_rows // peers - lower_each
    first = lower_each * peers
    upper = lat_rows - first
    data_rows = packed_rows(block, width)
    message_rows = data_rows + 16
    stay = lambda *arrays: [pltpu.with_memory_space_constraint(x, pltpu.HBM) for x in arrays]
    field = shape(lat_rows, block, width)

    fields = stay(zonal_wind, meridional_wind, thickness, potential_temp)
    to_north, to_south = pl.pallas_call(
        edges_kernel,
        out_shape=[shape(2 * block + 8, width), shape(3 * block, width)],
        in_specs=[hbm] * 4,
        out_specs=[VMEM] * 2,
        scratch_shapes=[rows_of(2), rows_of(2), rows_of(1), pltpu.VMEM((lat_rows, width), F32), dma(6)],
        compiler_params=params(8),
        cost_estimate=cost(1),
        name="edges",
    )(*fields[1:], *stay(surface_geo))
    halo_n = lax.ppermute(to_south, "lat", southward)
    halo_s = lax.ppermute(to_north, "lat", northward)

    def advect(start, each, halo, name):
        return pl.pallas_call(
            lambda *refs: advect_kernel(start, each, peers, *refs),
            out_shape=[shape(each, 2, data_rows, LANES)] * peers,
            in_specs=[SMEM, VMEM] + [hbm] * 4,
            out_specs=[VMEM] * peers,
            scratch_shapes=[
                pltpu.VMEM((peers, each + extra, block, width), F32) for extra in (0, 1, 2, 2)
            ]
            + [dma(4 * peers)],
            compiler_params=params(12),
            cost_estimate=cost(1 + 2 * each),
            name=name,
        )(coef, halo, *fields)

    upper_columns = exchanged(advect(first, upper_each, halo_n, "advect_upper"))
    lower_sent = advect(0, lower_each, halo_s, "advect_lower")
    far = peers // 2
    upper_columns[far], *lower_sent = lax.optimization_barrier((upper_columns[far], *lower_sent))
    lower_columns = exchanged(lower_sent)

    def remap(columns, each, name, after):
        lanes = tile_count(width) * LANES
        return pl.pallas_call(
            lambda *refs: remap_kernel(width, block, peers, *refs),
            out_shape=[shape(each, message_rows, LANES)] * peers,
            in_specs=[VMEM] * peers + [pl.BlockSpec(memory_space=pl.ANY)] * len(after),
            out_specs=[VMEM] * peers,
            scratch_shapes=[
                pltpu.VMEM((each, 2, levels, lanes), F32),
                pltpu.VMEM((each, levels, lanes), F32),
                pltpu.VMEM((each, tile_count(width), 8, LANES), F32),
                pltpu.VMEM((each, 8, lanes), F32),
            ],
            compiler_params=params(12),
            cost_estimate=cost(3 * each - 2.8),
            name=name,
        )(*columns, *after)

    upper_remapped = remap(upper_columns, upper_each, "remap_upper", lower_columns[:1])
    upper_messages = exchanged(upper_remapped)
    lower_remapped = remap(lower_columns, lower_each, "remap_lower", upper_remapped[:1])
    lower_messages = exchanged(lower_remapped)
    step_of_last = (lax.axis_index("lev") + 1) % peers
    _, *candidates = lax.optimization_barrier((lower_remapped[0], *upper_messages))
    last_message = candidates[0][-1:]
    for step in range(1, peers):
        last_message = jnp.where(step_of_last == step, candidates[step][-1:], last_message)
    south = lax.ppermute(last_message, "lat", northward)

    high, low, wave = fourier_tables(width)
    active = (jnp.asarray(wave)[None, :] >= cutoff[:, None]) & (polar_mask[:, None] != 0)
    table = jnp.where(active, damping - 1.0, 0.0)
    tables = [jnp.asarray(x) for x in (high, low, np.ascontiguousarray(high.T), np.ascontiguousarray(low.T))]

    *partial, edge_state = pl.pallas_call(
        lambda *refs: upper_final_kernel(levels, first, *refs),
        out_shape=[field] * 4 + [shape(3, block, width)],
        in_specs=[SMEM] * 2 + [VMEM] * (peers + 8) + [pl.BlockSpec(memory_space=pl.ANY)],
        out_specs=[hbm] * 4 + [VMEM],
        scratch_shapes=[pltpu.VMEM((upper, message_rows, LANES), F32)]
        + [rows_of(upper)] * 4
        + [rows_of(3), dma(4)],
        compiler_params=params(18),
        cost_estimate=cost(7),
        name="final_upper",
    )(
        flag, faces, *upper_messages, surface_geo, table, zonal_wind, meridional_wind, *tables, lower_remapped[0]
    )
    edge_state, *lower_messages = lax.optimization_barrier((edge_state, *lower_messages))
    return tuple(
        pl.pallas_call(
            lambda *refs: lower_final_kernel(levels, *refs),
            out_shape=[field] * 4,
            in_specs=[SMEM] * 2 + [VMEM] * (peers + 11) + [hbm] * 4,
            out_specs=[hbm] * 4,
            scratch_shapes=[pltpu.VMEM((first, message_rows, LANES), F32)]
            + [rows_of(2 * first + 1), rows_of(first), rows_of(first), dma(4)],
            input_output_aliases={peers + 13 + i: i for i in range(4)},
            compiler_params=params(16),
            cost_estimate=cost(6),
            name="final_lower",
        )(
            flag, faces, south, halo_s, edge_state, *lower_messages, surface_geo, table, zonal_wind, meridional_wind, *tables,
            *partial,
        )
    )


def solution(mesh):
    field = P("lat", "lev", None)
    in_specs = (field, field, field, field, P("lat", None), P("lat"), P("lat"), P("lat", None))
    return jax.shard_map(body, mesh=mesh, in_specs=in_specs, out_specs=(field,) * 4, check_vma=False)
```

```python
import math

import jax
import jax.numpy as jnp
import numpy as np
from jax import lax
from jax.experimental import pallas as pl
from jax.experimental.pallas import tpu as pltpu
from jax.sharding import PartitionSpec as P

TOP_PRESSURE = 0.01
HYBRID_SCALE = 0.2
EXNER_POWER = 2.0 / 7.0
COURANT = 0.012
HIGHEST = lax.Precision.HIGHEST
F32 = jnp.float32
BF16 = jnp.bfloat16
VMEM = pl.BlockSpec(memory_space=pltpu.VMEM)
SMEM = pl.BlockSpec(memory_space=pltpu.SMEM)
LANES = 128


def params(mib):
    return pltpu.CompilerParams(vmem_limit_bytes=mib * 1024 * 1024)


def cost(microseconds):
    return pl.CostEstimate(
        flops=int(microseconds * 1.1e9), bytes_accessed=int(microseconds * 3.6e6), transcendentals=0
    )


def fourier_tables(count):
    middle = count // 2
    ids = np.arange(count)
    wave = np.where(ids <= middle, ids, ids - middle)
    angle = 2.0 * np.pi / count * (ids[:, None] * wave[None, :] % count)
    edge = (ids == 0) | (ids == middle)
    weight = np.where(edge, 1.0 / math.sqrt(count), math.sqrt(2.0 / count))
    basis = np.where((ids <= middle)[None, :], np.cos(angle), np.sin(angle)) * weight[None, :]
    basis = basis.astype(np.float32)
    high = basis.astype(jnp.bfloat16)
    low = (basis - high.astype(np.float32)).astype(jnp.bfloat16)
    return high, low, wave.astype(np.int32)


def packed_rows(rows, width):
    return rows * width // LANES


def store_packed(ref, index, value):
    rows, width = value.shape
    full = width // LANES
    for tile in range(full):
        ref[(*index, pl.ds(tile * rows, rows), slice(None))] = value[:, tile * LANES : (tile + 1) * LANES]
    if width % LANES:
        rest = value[:, full * LANES :]
        half = rows // 2
        ref[(*index, pl.ds(full * rows, half), slice(None))] = jnp.concatenate([rest[:half], rest[half:]], axis=1)


def load_tile(ref, index, rows, width, tile):
    full = width // LANES
    if tile < full:
        return ref[(*index, pl.ds(tile * rows, rows), slice(None))]
    half = rows // 2
    both = ref[(*index, pl.ds(full * rows, half), slice(None))]
    return jnp.concatenate([both[:, : LANES // 2], both[:, LANES // 2 :]], axis=0)


def tile_count(width):
    return -(-width // LANES)


def wrapped(me, step, peers):
    other = me + step
    return jnp.where(other >= peers, other - peers, other)


def advect_row(row, coef, zonal, merid, t, h, t_s, h_s, t_n, h_n, w_n):
    u = zonal * (0.5 * COURANT)
    w_n = w_n * coef[1, row]
    w_s = merid * coef[0, row]
    for x, x_s, x_n in ((t, t_s, t_n), (h, h_s, h_n)):
        flux = u * (x + jnp.roll(x, 1, axis=1))
        yield x - (jnp.roll(flux, -1, axis=1) - flux) - (w_n * (x_n + x) - w_s * (x + x_s))


def edges_kernel(merid, thick, theta, ground, to_north, to_south, thick_s, theta_s, merid_s, ground_s, sems):
    lat_rows, levels, _ = thick.shape
    top = lat_rows - 1
    copies = []
    for source, target in ((thick, thick_s), (theta, theta_s)):
        copies += [(source.at[pl.ds(0, 1)], target.at[pl.ds(0, 1)]), (source.at[pl.ds(top, 1)], target.at[pl.ds(1, 1)])]
    wait_all(copy_all([*copies, (merid.at[pl.ds(0, 1)], merid_s), (ground, ground_s)], sems))
    to_north[pl.ds(0, levels), :] = thick_s[1]
    to_north[pl.ds(levels, levels), :] = theta_s[1] * thick_s[1]
    to_north[pl.ds(2 * levels, 1), :] = ground_s[pl.ds(top, 1), :]
    to_south[pl.ds(0, levels), :] = thick_s[0]
    to_south[pl.ds(levels, levels), :] = theta_s[0] * thick_s[0]
    to_south[pl.ds(2 * levels, levels), :] = merid_s[0]


def advect_kernel(first, rows_each, peers, coef, halo, *refs):
    fields, outs, held, sems = refs[:4], refs[4 : 4 + peers], refs[4 + peers : -1], refs[-1]
    lat_rows, levels, _ = fields[0].shape
    top = lat_rows - 1
    me = lax.axis_index("lev")
    part = lambda i: halo[pl.ds(i * levels, levels), :]
    owned = [first + wrapped(me, step, peers) * rows_each for step in range(peers)]
    reach = ((0, rows_each), (0, rows_each + 1), (1, rows_each + 2), (1, rows_each + 2))
    starts = [[jnp.clip(row - before, 0, lat_rows - count) for before, count in reach] for row in owned]
    arriving = [
        copy_all(
            [
                (field.at[pl.ds(start, count)], target.at[step])
                for field, target, start, (_, count) in zip(fields, held, starts[step], reach)
            ],
            sems,
            4 * step,
        )
        for step in range(peers)
    ]
    for step in range(peers):
        wait_all(arriving[step])
        zonal, merid, thick, theta = (ref.at[step] for ref in held)
        z_at, w_at, t_at, _ = (owned[step] - start for start in starts[step])
        for place in range(rows_each):
            row = owned[step] + place
            at = t_at + place
            low, high = jnp.maximum(at - 1, 0), jnp.minimum(at + 1, rows_each + 1)
            t, t_s, t_n = thick[at], thick[low], thick[high]
            h, h_s, h_n = theta[at] * t, theta[low] * t_s, theta[high] * t_n
            w, w_n = merid[w_at + place], merid[jnp.minimum(w_at + place + 1, rows_each)]
            if first == 0 and place == 0:
                t_s = jnp.where(row == 0, part(0), t_s)
                h_s = jnp.where(row == 0, part(1), h_s)
            if first + peers * rows_each == lat_rows and place == rows_each - 1:
                t_n = jnp.where(row == top, part(0), t_n)
                h_n = jnp.where(row == top, part(1), h_n)
                w_n = jnp.where(row == top, part(2), w_n)
            fields_new = advect_row(row, coef, zonal[z_at + place], w, t, h, t_s, h_s, t_n, h_n, w_n)
            for field, new in enumerate(fields_new):
                store_packed(outs[step], (place, field), new)


def target_edges(surface, sigma):
    curve = sigma * sigma
    return TOP_PRESSURE + HYBRID_SCALE * (sigma - curve) + (surface - TOP_PRESSURE) * curve


def target_thickness(surface, first, levels):
    step = 1.0 / levels
    curve = (2.0 * first + 1.0) * (step * step)
    return HYBRID_SCALE * (step - curve) + (surface - TOP_PRESSURE) * curve


def exner(pressure):
    return jnp.exp(EXNER_POWER * jnp.log(pressure))


def split_dot(x, ones):
    a = x.astype(BF16)
    r = x - a.astype(F32)
    b = r.astype(BF16)
    c = (r - b.astype(F32)).astype(BF16)
    dot = lambda v: jnp.dot(v, ones, preferred_element_type=F32)
    return dot(a) + (dot(b) + dot(c))

def remap_kernel(width, block, peers, *refs):
    parts = refs[:peers]
    gathered, spread, base_rows, base_s = refs[-4:]
    outs = refs[-4 - peers : -4]
    me = lax.axis_index("lev")
    count = parts[0].shape[0]
    levels = peers * block
    level_r = lax.broadcasted_iota(jnp.int32, (levels, levels), 0)
    level_c = lax.broadcasted_iota(jnp.int32, (levels, levels), 1)
    running = (level_r <= level_c).astype(F32).astype(BF16)
    below = (
        lax.broadcasted_iota(jnp.int32, (8, levels), 1)
        >= block * (1 + lax.broadcasted_iota(jnp.int32, (8, levels), 0))
    ).astype(F32)
    full = width // LANES
    data_rows = packed_rows(block, width)
    half = block // 2
    sources = [wrapped(me, (peers - step) % peers, peers) for step in range(peers)]
    targets = [wrapped(me, step, peers) for step in range(peers)]
    for place in range(count):
        for step in range(peers):
            at = pl.ds(pl.multiple_of(sources[step] * block, block), block)
            for field in range(2):
                for tile in range(tile_count(width)):
                    cols = min(LANES, width - tile * LANES)
                    gathered[place, field, at, pl.ds(tile * LANES, cols)] = load_tile(
                        parts[step], (place, field), block, width, tile)
    for place in range(count):
        cols = width
        here = pl.ds(0, cols)
        thick = gathered[place, 0, :, here]
        surface_row = TOP_PRESSURE + jnp.sum(thick, axis=0, keepdims=True)
        thick = thick.T
        heat = gathered[place, 1, :, here].T
        upper = TOP_PRESSURE + split_dot(thick, running)
        theta = heat / thick
        offset = split_dot(heat, running) - theta * upper
        surface = upper[:, levels - 1 :]
        lane = lax.broadcasted_iota(jnp.int32, (cols, levels), 1)
        lane_f = lane.astype(F32)
        edge = target_edges(surface, (lane_f + 1.0) * (1.0 / levels))
        at = jnp.zeros((cols, levels), jnp.int32)
        jump = levels // 2
        while jump:
            probe = jnp.take_along_axis(upper, at + (jump - 1), axis=1, mode="promise_in_bounds")
            at = jnp.where(probe < edge, at + jump, at)
            jump //= 2
        pick = lambda table: jnp.take_along_axis(table, at, axis=1, mode="promise_in_bounds")
        heat_to = pick(offset) + pick(theta) * edge
        heat_from = jnp.where(lane == 0, 0.0, pltpu.roll(heat_to, 1, 1))
        theta_next = (heat_to - heat_from) / target_thickness(surface, lane_f, levels)
        exner_to = exner(edge)
        exner_from = jnp.where(lane == 0, TOP_PRESSURE**EXNER_POWER, pltpu.roll(exner_to, 1, 1))
        layer = theta_next * (exner_to - exner_from)
        bases = lax.dot_general(
            below, layer, (((1,), (1,)), ((), ())), precision=HIGHEST, preferred_element_type=F32
        )
        base_s[place, :, here] = bases
        base_s[place, pl.ds(7, 1), here] = surface_row
        spread[place, :, here] = theta_next.T
    for place in range(count):
        for tile in range(tile_count(width)):
            base_rows[place, tile] = base_s[place, :, pl.ds(tile * LANES, LANES)]
        for step in range(peers):
            out = outs[step]
            start = pl.multiple_of(targets[step] * block, block)
            for tile in range(tile_count(width)):
                cols = min(LANES, width - tile * LANES)
                here = pl.ds(tile * LANES, cols)
                if tile < full:
                    out[place, pl.ds(tile * block, block), :] = spread[place, pl.ds(start, block), here]
                else:
                    part = spread[place, pl.ds(start, block), here]
                    out[place, pl.ds(full * block, half), :] = jnp.concatenate([part[:half], part[half:]], axis=1)
                out[place, pl.ds(data_rows + tile, 1), pl.ds(0, cols)] = base_rows[place, tile, pl.ds(7, 1), pl.ds(0, cols)]
                out[place, pl.ds(data_rows + 8 + tile, 1), pl.ds(0, cols)] = base_rows[place, tile, pl.ds(targets[step], 1), pl.ds(0, cols)]


def below_sum(layer):
    rows, width = layer.shape
    groups = rows // 8
    carry = None
    pieces = []
    sub = lax.broadcasted_iota(jnp.int32, (8, width), 0)
    for g in reversed(range(groups)):
        x = layer[g * 8 : (g + 1) * 8]
        total = x
        for step in (1, 2, 4):
            total = total + jnp.where(sub < 8 - step, pltpu.roll(total, 8 - step, 0), 0.0)
        under = total - x
        if carry is not None:
            under = under + carry
            carry = carry + total[0:1]
        else:
            carry = total[0:1]
        pieces.append(under)
    return jnp.concatenate(pieces[::-1], axis=0)


def column_state(message, index, block, width, first_level, levels, ground):
    tiles = tile_count(width)
    data_rows = packed_rows(block, width)
    theta = jnp.concatenate([load_tile(message, index, block, width, t) for t in range(tiles)], axis=1)

    def line(first):
        return jnp.concatenate(
            [message[(*index, pl.ds(first + t, 1), pl.ds(0, min(LANES, width - t * LANES)))] for t in range(tiles)],
            axis=1,
        )

    surface = line(data_rows)
    base = line(data_rows + 8)
    sub = lax.broadcasted_iota(jnp.int32, (block, width), 0).astype(F32) + first_level
    thick = target_thickness(surface, sub, levels)
    top = exner(target_edges(surface, sub * (1.0 / levels)))
    bottom_edge = exner(target_edges(surface, (first_level + block) * (1.0 / levels)))
    sub_i = lax.broadcasted_iota(jnp.int32, (block, width), 0)
    bottom = jnp.where(sub_i == block - 1, bottom_edge, pltpu.roll(top, block - 1, 0))
    layer = theta * (bottom - top)
    geopot = (ground + base) + (below_sum(layer) + 0.5 * layer)
    return theta, thick, 0.5 * (top + bottom), geopot


def push(now, before):
    theta, exner_mid, geopot = now
    theta_b, exner_b, geopot_b = before
    return (geopot - geopot_b) + 0.5 * (theta + theta_b) * (exner_mid - exner_b)


def filtered(value, table, basis, basis_t, split, block):
    rows, width = value.shape
    span = tile_count(width) * LANES

    def product(x, stacked):
        high = x.astype(BF16)
        low = (x - high.astype(F32)).astype(BF16)
        for i, part in enumerate((high, low, high)):
            split[pl.ds(0, rows), pl.ds(i * span, width)] = part
        return jnp.dot(split[pl.ds(0, rows), :], stacked[...], preferred_element_type=F32)

    spectral = product(value, basis)
    spectral = (spectral.reshape(rows // block, block, width) * table[:, None, :]).reshape(rows, width)
    return value + product(spectral, basis_t)


def clear_gaps(split, width):
    span = tile_count(width) * LANES
    last = width // LANES * LANES
    for i in range(split.shape[1] // span):
        split[:, pl.ds(i * span + last, span - last)] = jnp.zeros((split.shape[0], span - last), BF16)


def stacked_tables(high, low):
    rows, width = high.shape
    gap = np.zeros((tile_count(rows) * LANES - rows, width), high.dtype)
    return jnp.asarray(np.concatenate([high, gap, high, gap, low, gap]))


def gather_messages(me, parts, order):
    peers = len(parts)
    for step, part in enumerate(parts):
        owner = wrapped(me, (peers - step) % peers, peers)
        for place in range(part.shape[0]):
            order[owner * part.shape[0] + place] = part[place]


def copy_all(copies, sems, first=0):
    started = [pltpu.make_async_copy(source, target, sems.at[first + i]) for i, (source, target) in enumerate(copies)]
    for copy in started:
        copy.start()
    return started


def wait_all(copies):
    for copy in copies:
        copy.wait()


def filter_rows(ref, count, table, tables, block):
    width = ref.shape[-1]
    value = ref[pl.ds(0, count)].reshape(count * block, width)
    value = filtered(value, table, *tables, block)
    ref[pl.ds(0, count)] = value.reshape(count, block, width)


def around(x):
    return jnp.roll(x, 1, axis=1)


def upper_final_kernel(
    levels, first, flag, faces, p0, p1, p2, p3, ground, table, zonal, merid, basis, basis_t, after,
    zonal_out, merid_out, thick_out, theta_out, edge_state,
    order, zonal_s, merid_s, thick_s, theta_s, carried, split, sems,
):
    del after
    lat_rows, block, width = zonal.shape
    count = lat_rows - first
    rows = pl.ds(first, count)
    me = lax.axis_index("lev")
    level = (me * block).astype(F32)
    gather_messages(me, (p0, p1, p2, p3), order)
    carried[...] = jnp.zeros_like(carried)

    def one_row(i, _):
        row = first + i
        theta, thick, mid, geopot = column_state(order, (i,), block, width, level, levels, ground[pl.ds(row, 1), :])
        theta_s[i] = theta
        thick_s[i] = thick
        now = (theta, mid, geopot)
        zonal_s[i] = zonal[row] - push(now, tuple(around(x) for x in now))
        before = (carried[0], carried[1], carried[2])
        merid_s[jnp.maximum(i - 1, 0)] = merid[row] - faces[row] * push(now, before)
        for field, x in enumerate(now):
            carried[field] = x

        @pl.when(i == 0)
        def _():
            for field, x in enumerate(now):
                edge_state[field] = x

        return 0

    lax.fori_loop(0, count, one_row, 0)
    early = copy_all([(theta_s, theta_out.at[rows]), (thick_s, thick_out.at[rows])], sems)

    @pl.when(flag[0] != 0)
    def _():
        tables = (basis, basis_t, split)
        clear_gaps(split, width)
        filter_rows(zonal_s, count, table[rows, :], tables, block)

    early += copy_all([(zonal_s, zonal_out.at[rows])], sems, 2)

    @pl.when(flag[0] != 0)
    def _():
        tables = (basis, basis_t, split)
        filter_rows(merid_s, count - 1, table[pl.ds(first + 1, count - 1), :], tables, block)

    late = copy_all([(merid_s.at[pl.ds(0, count - 1)], merid_out.at[pl.ds(first + 1, count - 1)])], sems, 3)
    wait_all(early + late)


def lower_final_kernel(
    levels, flag, faces, south, halo_s, edge_state, p0, p1, p2, p3, ground, table, zonal, merid, basis, basis_t,
    zonal_in, merid_in, thick_in, theta_in,
    zonal_out, merid_out, thick_out, theta_out,
    order, winds_s, thick_s, theta_s, split, sems,
):
    del zonal_in, merid_in, thick_in, theta_in
    count = order.shape[0]
    _, block, width = zonal.shape
    me = lax.axis_index("lev")
    level = (me * block).astype(F32)
    gather_messages(me, (p0, p1, p2, p3), order)
    state = lambda ref, i, line: column_state(ref, (i,), block, width, level, levels, line)
    theta, _, mid, geopot = state(south, 0, halo_s[pl.ds(2 * block, 1), :])
    before = (theta, mid, geopot)
    for row in range(count):
        theta, thick, mid, geopot = state(order, row, ground[pl.ds(row, 1), :])
        theta_s[row] = theta
        thick_s[row] = thick
        now = (theta, mid, geopot)
        winds_s[row] = zonal[row] - push(now, tuple(around(x) for x in now))
        winds_s[count + row] = merid[row] - faces[row] * push(now, before)
        before = now
    now = tuple(edge_state[field] for field in range(3))
    winds_s[2 * count] = merid[count] - faces[count] * push(now, before)
    rows = pl.ds(0, count)
    early = copy_all([(theta_s, theta_out.at[rows]), (thick_s, thick_out.at[rows])], sems)

    @pl.when(flag[0] != 0)
    def _():
        picked = jnp.concatenate([table[rows, :], table[pl.ds(0, count + 1), :]], axis=0)
        clear_gaps(split, width)
        filter_rows(winds_s, 2 * count + 1, picked, (basis, basis_t, split), block)

    late = copy_all(
        [
            (winds_s.at[rows], zonal_out.at[rows]),
            (winds_s.at[pl.ds(count, count + 1)], merid_out.at[pl.ds(0, count + 1)]),
        ],
        sems,
        2,
    )
    wait_all(early + late)


def exchanged(parts):
    peers = lax.axis_size("lev")
    return [parts[0]] + [
        lax.ppermute(parts[step], "lev", [(i, (i + step) % peers) for i in range(peers)]) for step in range(1, peers)
    ]


def body(
    zonal_wind, meridional_wind, thickness, potential_temp, surface_geo, polar_mask, cutoff, damping
):
    lat_rows, block, width = zonal_wind.shape
    lat_count = lax.axis_size("lat")
    peers = lax.axis_size("lev")
    levels = block * peers
    total_rows = lat_rows * lat_count
    first_row = lax.axis_index("lat") * lat_rows
    row_ids = (first_row + jnp.arange(lat_rows + 1, dtype=jnp.int32)).astype(F32)
    faces = jnp.sin(math.pi * row_ids / total_rows)
    centres = jnp.sin(math.pi * (row_ids[:-1] + 0.5) / total_rows)
    coef = jnp.stack([faces[:-1], faces[1:]]) * (0.5 * COURANT) / centres
    northward = [(i, i + 1) for i in range(lat_count - 1)]
    southward = [(i + 1, i) for i in range(lat_count - 1)]
    flag = jnp.any(polar_mask != 0).astype(jnp.int32).reshape(1)
    shape = lambda *dims: jax.ShapeDtypeStruct(dims, F32)
    hbm = pl.BlockSpec(memory_space=pltpu.HBM)
    rows_of = lambda n: pltpu.VMEM((n, block, width), F32)
    dma = lambda n: pltpu.SemaphoreType.DMA((n,))

    lower_each = 1
    upper_each = lat_rows // peers - lower_each
    first = lower_each * peers
    upper = lat_rows - first
    data_rows = packed_rows(block, width)
    message_rows = data_rows + 16
    stay = lambda *arrays: [pltpu.with_memory_space_constraint(x, pltpu.HBM) for x in arrays]
    field = shape(lat_rows, block, width)

    fields = stay(zonal_wind, meridional_wind, thickness, potential_temp)
    to_north, to_south = pl.pallas_call(
        edges_kernel,
        out_shape=[shape(2 * block + 8, width), shape(3 * block, width)],
        in_specs=[hbm] * 4,
        out_specs=[VMEM] * 2,
        scratch_shapes=[rows_of(2), rows_of(2), rows_of(1), pltpu.VMEM((lat_rows, width), F32), dma(6)],
        compiler_params=params(8),
        cost_estimate=cost(1),
        name="edges",
    )(*fields[1:], *stay(surface_geo))
    halo_n = lax.ppermute(to_south, "lat", southward)
    halo_s = lax.ppermute(to_north, "lat", northward)

    def advect(start, each, halo, name):
        return pl.pallas_call(
            lambda *refs: advect_kernel(start, each, peers, *refs),
            out_shape=[shape(each, 2, data_rows, LANES)] * peers,
            in_specs=[SMEM, VMEM] + [hbm] * 4,
            out_specs=[VMEM] * peers,
            scratch_shapes=[
                pltpu.VMEM((peers, each + extra, block, width), F32) for extra in (0, 1, 2, 2)
            ]
            + [dma(4 * peers)],
            compiler_params=params(12),
            cost_estimate=cost(1 + 2 * each),
            name=name,
        )(coef, halo, *fields)

    upper_columns = exchanged(advect(first, upper_each, halo_n, "advect_upper"))
    lower_sent = advect(0, lower_each, halo_s, "advect_lower")
    upper_columns[1], *lower_sent = lax.optimization_barrier((upper_columns[1], *lower_sent))
    lower_columns = exchanged(lower_sent)

    def remap(columns, each, name, after):
        lanes = tile_count(width) * LANES
        return pl.pallas_call(
            lambda *refs: remap_kernel(width, block, peers, *refs),
            out_shape=[shape(each, message_rows, LANES)] * peers,
            in_specs=[VMEM] * peers + [pl.BlockSpec(memory_space=pl.ANY)] * len(after),
            out_specs=[VMEM] * peers,
            scratch_shapes=[
                pltpu.VMEM((each, 2, levels, lanes), F32),
                pltpu.VMEM((each, levels, lanes), F32),
                pltpu.VMEM((each, tile_count(width), 8, LANES), F32),
                pltpu.VMEM((each, 8, lanes), F32),
            ],
            compiler_params=params(12),
            cost_estimate=cost(3 * each - 2.8),
            name=name,
        )(*columns, *after)

    upper_remapped = remap(upper_columns, upper_each, "remap_upper", lower_columns[:1])
    upper_messages = exchanged(upper_remapped)
    lower_remapped = remap(lower_columns, lower_each, "remap_lower", upper_remapped[:1])
    lower_messages = exchanged(lower_remapped)
    step_of_last = (lax.axis_index("lev") + 1) % peers
    _, *candidates = lax.optimization_barrier((lower_remapped[0], *upper_messages))
    last_message = candidates[0][-1:]
    for step in range(1, peers):
        last_message = jnp.where(step_of_last == step, candidates[step][-1:], last_message)
    south = lax.ppermute(last_message, "lat", northward)

    high, low, wave = fourier_tables(width)
    active = (jnp.asarray(wave)[None, :] >= cutoff[:, None]) & (polar_mask[:, None] != 0)
    table = jnp.where(active, damping - 1.0, 0.0)
    tables = [stacked_tables(high, low), stacked_tables(high.T, low.T)]
    split_of = lambda rows: pltpu.VMEM((rows * block, 3 * tile_count(width) * LANES), BF16)

    *partial, edge_state = pl.pallas_call(
        lambda *refs: upper_final_kernel(levels, first, *refs),
        out_shape=[field] * 4 + [shape(3, block, width)],
        in_specs=[SMEM] * 2 + [VMEM] * (peers + 6) + [pl.BlockSpec(memory_space=pl.ANY)],
        out_specs=[hbm] * 4 + [VMEM],
        scratch_shapes=[pltpu.VMEM((upper, message_rows, LANES), F32)]
        + [rows_of(upper)] * 4
        + [rows_of(3), split_of(upper), dma(4)],
        compiler_params=params(18),
        cost_estimate=cost(7),
        name="final_upper",
    )(
        flag, faces, *upper_messages, surface_geo, table, zonal_wind, meridional_wind, *tables, lower_remapped[0]
    )
    edge_state, *lower_messages = lax.optimization_barrier((edge_state, *lower_messages))
    return tuple(
        pl.pallas_call(
            lambda *refs: lower_final_kernel(levels, *refs),
            out_shape=[field] * 4,
            in_specs=[SMEM] * 2 + [VMEM] * (peers + 9) + [hbm] * 4,
            out_specs=[hbm] * 4,
            scratch_shapes=[pltpu.VMEM((first, message_rows, LANES), F32)]
            + [rows_of(2 * first + 1), rows_of(first), rows_of(first), split_of(2 * first + 1), dma(4)],
            input_output_aliases={peers + 11 + i: i for i in range(4)},
            compiler_params=params(16),
            cost_estimate=cost(6),
            name="final_lower",
        )(
            flag, faces, south, halo_s, edge_state, *lower_messages, surface_geo, table, zonal_wind, meridional_wind, *tables,
            *partial,
        )
    )


def solution(mesh):
    field = P("lat", "lev", None)
    in_specs = (field, field, field, field, P("lat", None), P("lat"), P("lat"), P("lat", None))
    return jax.shard_map(body, mesh=mesh, in_specs=in_specs, out_specs=(field,) * 4, check_vma=False)
```

```python
import math

import jax
import jax.numpy as jnp
import numpy as np
from jax import lax
from jax.experimental import pallas as pl
from jax.experimental.pallas import tpu as pltpu
from jax.sharding import PartitionSpec as P

TOP_PRESSURE = 0.01
HYBRID_SCALE = 0.2
EXNER_POWER = 2.0 / 7.0
COURANT = 0.012
HIGHEST = lax.Precision.HIGHEST
F32 = jnp.float32
BF16 = jnp.bfloat16
VMEM = pl.BlockSpec(memory_space=pltpu.VMEM)
SMEM = pl.BlockSpec(memory_space=pltpu.SMEM)
LANES = 128


def params(mib):
    return pltpu.CompilerParams(vmem_limit_bytes=mib * 1024 * 1024)


def cost(microseconds):
    return pl.CostEstimate(
        flops=int(microseconds * 1.1e9), bytes_accessed=int(microseconds * 3.6e6), transcendentals=0
    )


def fourier_tables(count):
    middle = count // 2
    ids = np.arange(count)
    wave = np.where(ids <= middle, ids, ids - middle)
    angle = 2.0 * np.pi / count * (ids[:, None] * wave[None, :] % count)
    edge = (ids == 0) | (ids == middle)
    weight = np.where(edge, 1.0 / math.sqrt(count), math.sqrt(2.0 / count))
    basis = np.where((ids <= middle)[None, :], np.cos(angle), np.sin(angle)) * weight[None, :]
    basis = basis.astype(np.float32)
    high = basis.astype(jnp.bfloat16)
    low = (basis - high.astype(np.float32)).astype(jnp.bfloat16)
    return high, low, wave.astype(np.int32)


def packed_rows(rows, width):
    return rows * width // LANES


def store_packed(ref, index, value):
    rows, width = value.shape
    full = width // LANES
    for tile in range(full):
        ref[(*index, pl.ds(tile * rows, rows), slice(None))] = value[:, tile * LANES : (tile + 1) * LANES]
    if width % LANES:
        rest = value[:, full * LANES :]
        half = rows // 2
        ref[(*index, pl.ds(full * rows, half), slice(None))] = jnp.concatenate([rest[:half], rest[half:]], axis=1)


def load_tile(ref, index, rows, width, tile):
    full = width // LANES
    if tile < full:
        return ref[(*index, pl.ds(tile * rows, rows), slice(None))]
    half = rows // 2
    both = ref[(*index, pl.ds(full * rows, half), slice(None))]
    return jnp.concatenate([both[:, : LANES // 2], both[:, LANES // 2 :]], axis=0)


def tile_count(width):
    return -(-width // LANES)


def wrapped(me, step, peers):
    other = me + step
    return jnp.where(other >= peers, other - peers, other)


def advect_row(row, coef, zonal, merid, t, h, t_s, h_s, t_n, h_n, w_n):
    u = zonal * (0.5 * COURANT)
    w_n = w_n * coef[1, row]
    w_s = merid * coef[0, row]
    for x, x_s, x_n in ((t, t_s, t_n), (h, h_s, h_n)):
        flux = u * (x + jnp.roll(x, 1, axis=1))
        yield x - (jnp.roll(flux, -1, axis=1) - flux) - (w_n * (x_n + x) - w_s * (x + x_s))


def edges_kernel(merid, thick, theta, ground, to_north, to_south, thick_s, theta_s, merid_s, ground_s, sems):
    lat_rows, levels, _ = thick.shape
    top = lat_rows - 1
    copies = []
    for source, target in ((thick, thick_s), (theta, theta_s)):
        copies += [(source.at[pl.ds(0, 1)], target.at[pl.ds(0, 1)]), (source.at[pl.ds(top, 1)], target.at[pl.ds(1, 1)])]
    wait_all(copy_all([*copies, (merid.at[pl.ds(0, 1)], merid_s), (ground, ground_s)], sems))
    to_north[pl.ds(0, levels), :] = thick_s[1]
    to_north[pl.ds(levels, levels), :] = theta_s[1] * thick_s[1]
    to_north[pl.ds(2 * levels, 1), :] = ground_s[pl.ds(top, 1), :]
    to_south[pl.ds(0, levels), :] = thick_s[0]
    to_south[pl.ds(levels, levels), :] = theta_s[0] * thick_s[0]
    to_south[pl.ds(2 * levels, levels), :] = merid_s[0]


def advect_kernel(first, rows_each, peers, coef, halo, *refs):
    fields, outs, held, sems = refs[:4], refs[4 : 4 + peers], refs[4 + peers : -1], refs[-1]
    lat_rows, levels, _ = fields[0].shape
    top = lat_rows - 1
    me = lax.axis_index("lev")
    part = lambda i: halo[pl.ds(i * levels, levels), :]
    owned = [first + wrapped(me, step, peers) * rows_each for step in range(peers)]
    reach = ((0, rows_each), (0, rows_each + 1), (1, rows_each + 2), (1, rows_each + 2))
    starts = [[jnp.clip(row - before, 0, lat_rows - count) for before, count in reach] for row in owned]
    arriving = [
        copy_all(
            [
                (field.at[pl.ds(start, count)], target.at[step])
                for field, target, start, (_, count) in zip(fields, held, starts[step], reach)
            ],
            sems,
            4 * step,
        )
        for step in range(peers)
    ]
    for step in range(peers):
        wait_all(arriving[step])
        zonal, merid, thick, theta = (ref.at[step] for ref in held)
        z_at, w_at, t_at, _ = (owned[step] - start for start in starts[step])
        for place in range(rows_each):
            row = owned[step] + place
            at = t_at + place
            low, high = jnp.maximum(at - 1, 0), jnp.minimum(at + 1, rows_each + 1)
            t, t_s, t_n = thick[at], thick[low], thick[high]
            h, h_s, h_n = theta[at] * t, theta[low] * t_s, theta[high] * t_n
            w, w_n = merid[w_at + place], merid[jnp.minimum(w_at + place + 1, rows_each)]
            if first == 0 and place == 0:
                t_s = jnp.where(row == 0, part(0), t_s)
                h_s = jnp.where(row == 0, part(1), h_s)
            if first + peers * rows_each == lat_rows and place == rows_each - 1:
                t_n = jnp.where(row == top, part(0), t_n)
                h_n = jnp.where(row == top, part(1), h_n)
                w_n = jnp.where(row == top, part(2), w_n)
            fields_new = advect_row(row, coef, zonal[z_at + place], w, t, h, t_s, h_s, t_n, h_n, w_n)
            for field, new in enumerate(fields_new):
                store_packed(outs[step], (place, field), new)


def target_edges(surface, sigma):
    curve = sigma * sigma
    return TOP_PRESSURE + HYBRID_SCALE * (sigma - curve) + (surface - TOP_PRESSURE) * curve


def target_thickness(surface, first, levels):
    step = 1.0 / levels
    curve = (2.0 * first + 1.0) * (step * step)
    return HYBRID_SCALE * (step - curve) + (surface - TOP_PRESSURE) * curve


def exner(pressure):
    return jnp.exp(EXNER_POWER * jnp.log(pressure))


def split_dot(x, ones):
    a = x.astype(BF16)
    r = x - a.astype(F32)
    b = r.astype(BF16)
    c = (r - b.astype(F32)).astype(BF16)
    dot = lambda v: jnp.dot(v, ones, preferred_element_type=F32)
    return dot(a) + (dot(b) + dot(c))

def remap_kernel(width, block, peers, *refs):
    parts = refs[:peers]
    gathered, spread, base_rows, base_s = refs[-4:]
    outs = refs[-4 - peers : -4]
    me = lax.axis_index("lev")
    count = parts[0].shape[0]
    levels = peers * block
    level_r = lax.broadcasted_iota(jnp.int32, (levels, levels), 0)
    level_c = lax.broadcasted_iota(jnp.int32, (levels, levels), 1)
    running = (level_r <= level_c).astype(F32).astype(BF16)
    below = (
        lax.broadcasted_iota(jnp.int32, (8, levels), 1)
        >= block * (1 + lax.broadcasted_iota(jnp.int32, (8, levels), 0))
    ).astype(F32)
    full = width // LANES
    data_rows = packed_rows(block, width)
    half = block // 2
    sources = [wrapped(me, (peers - step) % peers, peers) for step in range(peers)]
    targets = [wrapped(me, step, peers) for step in range(peers)]
    for place in range(count):
        for step in range(peers):
            at = pl.ds(pl.multiple_of(sources[step] * block, block), block)
            for field in range(2):
                for tile in range(tile_count(width)):
                    cols = min(LANES, width - tile * LANES)
                    gathered[place, field, at, pl.ds(tile * LANES, cols)] = load_tile(
                        parts[step], (place, field), block, width, tile)
    for place in range(count):
        cols = width
        here = pl.ds(0, cols)
        thick = gathered[place, 0, :, here]
        surface_row = TOP_PRESSURE + jnp.sum(thick, axis=0, keepdims=True)
        thick = thick.T
        heat = gathered[place, 1, :, here].T
        upper = TOP_PRESSURE + split_dot(thick, running)
        theta = heat / thick
        offset = split_dot(heat, running) - theta * upper
        surface = upper[:, levels - 1 :]
        lane = lax.broadcasted_iota(jnp.int32, (cols, levels), 1)
        lane_f = lane.astype(F32)
        edge = target_edges(surface, (lane_f + 1.0) * (1.0 / levels))
        at = jnp.zeros((cols, levels), jnp.int32)
        jump = levels // 2
        while jump:
            probe = jnp.take_along_axis(upper, at + (jump - 1), axis=1, mode="promise_in_bounds")
            at = jnp.where(probe < edge, at + jump, at)
            jump //= 2
        pick = lambda table: jnp.take_along_axis(table, at, axis=1, mode="promise_in_bounds")
        heat_to = pick(offset) + pick(theta) * edge
        heat_from = jnp.where(lane == 0, 0.0, pltpu.roll(heat_to, 1, 1))
        theta_next = (heat_to - heat_from) / target_thickness(surface, lane_f, levels)
        exner_to = exner(edge)
        exner_from = jnp.where(lane == 0, TOP_PRESSURE**EXNER_POWER, pltpu.roll(exner_to, 1, 1))
        layer = theta_next * (exner_to - exner_from)
        bases = lax.dot_general(
            below, layer, (((1,), (1,)), ((), ())), precision=HIGHEST, preferred_element_type=F32
        )
        base_s[place, :, here] = bases
        base_s[place, pl.ds(7, 1), here] = surface_row
        spread[place, :, here] = theta_next.T
    for place in range(count):
        for tile in range(tile_count(width)):
            base_rows[place, tile] = base_s[place, :, pl.ds(tile * LANES, LANES)]
        for step in range(peers):
            out = outs[step]
            start = pl.multiple_of(targets[step] * block, block)
            for tile in range(tile_count(width)):
                cols = min(LANES, width - tile * LANES)
                here = pl.ds(tile * LANES, cols)
                if tile < full:
                    out[place, pl.ds(tile * block, block), :] = spread[place, pl.ds(start, block), here]
                else:
                    part = spread[place, pl.ds(start, block), here]
                    out[place, pl.ds(full * block, half), :] = jnp.concatenate([part[:half], part[half:]], axis=1)
                out[place, pl.ds(data_rows + tile, 1), pl.ds(0, cols)] = base_rows[place, tile, pl.ds(7, 1), pl.ds(0, cols)]
                out[place, pl.ds(data_rows + 8 + tile, 1), pl.ds(0, cols)] = base_rows[place, tile, pl.ds(targets[step], 1), pl.ds(0, cols)]


def below_sum(layer):
    rows, width = layer.shape
    groups = rows // 8
    carry = None
    pieces = []
    sub = lax.broadcasted_iota(jnp.int32, (8, width), 0)
    for g in reversed(range(groups)):
        x = layer[g * 8 : (g + 1) * 8]
        total = x
        for step in (1, 2, 4):
            total = total + jnp.where(sub < 8 - step, pltpu.roll(total, 8 - step, 0), 0.0)
        under = total - x
        if carry is not None:
            under = under + carry
            carry = carry + total[0:1]
        else:
            carry = total[0:1]
        pieces.append(under)
    return jnp.concatenate(pieces[::-1], axis=0)


def column_state(message, index, block, width, first_level, levels, ground):
    tiles = tile_count(width)
    data_rows = packed_rows(block, width)
    theta = jnp.concatenate([load_tile(message, index, block, width, t) for t in range(tiles)], axis=1)

    def line(first):
        return jnp.concatenate(
            [message[(*index, pl.ds(first + t, 1), pl.ds(0, min(LANES, width - t * LANES)))] for t in range(tiles)],
            axis=1,
        )

    surface = line(data_rows)
    base = line(data_rows + 8)
    sub = lax.broadcasted_iota(jnp.int32, (block, width), 0).astype(F32) + first_level
    thick = target_thickness(surface, sub, levels)
    top = exner(target_edges(surface, sub * (1.0 / levels)))
    bottom_edge = exner(target_edges(surface, (first_level + block) * (1.0 / levels)))
    sub_i = lax.broadcasted_iota(jnp.int32, (block, width), 0)
    bottom = jnp.where(sub_i == block - 1, bottom_edge, pltpu.roll(top, block - 1, 0))
    layer = theta * (bottom - top)
    geopot = (ground + base) + (below_sum(layer) + 0.5 * layer)
    return theta, thick, 0.5 * (top + bottom), geopot


def push(now, before):
    theta, exner_mid, geopot = now
    theta_b, exner_b, geopot_b = before
    return (geopot - geopot_b) + 0.5 * (theta + theta_b) * (exner_mid - exner_b)


def filtered(value, table, basis, basis_t, split, block):
    rows, width = value.shape
    span = tile_count(width) * LANES

    def product(x, stacked):
        high = x.astype(BF16)
        low = (x - high.astype(F32)).astype(BF16)
        for i, part in enumerate((high, low, high)):
            split[pl.ds(0, rows), pl.ds(i * span, width)] = part
        return jnp.dot(split[pl.ds(0, rows), :], stacked[...], preferred_element_type=F32)

    spectral = product(value, basis)
    spectral = (spectral.reshape(rows // block, block, width) * table[:, None, :]).reshape(rows, width)
    return value + product(spectral, basis_t)


def clear_gaps(split, width):
    span = tile_count(width) * LANES
    last = width // LANES * LANES
    for i in range(split.shape[1] // span):
        split[:, pl.ds(i * span + last, span - last)] = jnp.zeros((split.shape[0], span - last), BF16)


def stacked_tables(high, low):
    rows, width = high.shape
    gap = np.zeros((tile_count(rows) * LANES - rows, width), high.dtype)
    return jnp.asarray(np.concatenate([high, gap, high, gap, low, gap]))


def gather_messages(me, parts, order):
    peers = len(parts)
    for step, part in enumerate(parts):
        owner = wrapped(me, (peers - step) % peers, peers)
        for place in range(part.shape[0]):
            order[owner * part.shape[0] + place] = part[place]


def copy_all(copies, sems, first=0):
    started = [pltpu.make_async_copy(source, target, sems.at[first + i]) for i, (source, target) in enumerate(copies)]
    for copy in started:
        copy.start()
    return started


def wait_all(copies):
    for copy in copies:
        copy.wait()


def filter_rows(ref, count, table, tables, block):
    width = ref.shape[-1]
    value = ref[pl.ds(0, count)].reshape(count * block, width)
    value = filtered(value, table, *tables, block)
    ref[pl.ds(0, count)] = value.reshape(count, block, width)


def around(x):
    return jnp.roll(x, 1, axis=1)


def upper_final_kernel(
    levels, first, flag, faces, p0, p1, p2, p3, ground, table, zonal, merid, basis, basis_t, after,
    zonal_out, merid_out, thick_out, theta_out, edge_state,
    order, zonal_s, merid_s, thick_s, theta_s, carried, split, sems,
):
    del after
    lat_rows, block, width = zonal.shape
    count = lat_rows - first
    rows = pl.ds(first, count)
    me = lax.axis_index("lev")
    level = (me * block).astype(F32)
    gather_messages(me, (p0, p1, p2, p3), order)
    carried[...] = jnp.zeros_like(carried)

    def one_row(i, _):
        row = first + i
        theta, thick, mid, geopot = column_state(order, (i,), block, width, level, levels, ground[pl.ds(row, 1), :])
        theta_s[i] = theta
        thick_s[i] = thick
        now = (theta, mid, geopot)
        zonal_s[i] = zonal[row] - push(now, tuple(around(x) for x in now))
        before = (carried[0], carried[1], carried[2])
        merid_s[jnp.maximum(i - 1, 0)] = merid[row] - faces[row] * push(now, before)
        for field, x in enumerate(now):
            carried[field] = x

        @pl.when(i == 0)
        def _():
            for field, x in enumerate(now):
                edge_state[field] = x

        return 0

    lax.fori_loop(0, count, one_row, 0)
    early = copy_all([(theta_s, theta_out.at[rows]), (thick_s, thick_out.at[rows])], sems)

    @pl.when(flag[0] != 0)
    def _():
        tables = (basis, basis_t, split)
        clear_gaps(split, width)
        filter_rows(zonal_s, count, table[rows, :], tables, block)

    early += copy_all([(zonal_s, zonal_out.at[rows])], sems, 2)

    @pl.when(flag[0] != 0)
    def _():
        tables = (basis, basis_t, split)
        filter_rows(merid_s, count - 1, table[pl.ds(first + 1, count - 1), :], tables, block)

    late = copy_all([(merid_s.at[pl.ds(0, count - 1)], merid_out.at[pl.ds(first + 1, count - 1)])], sems, 3)
    wait_all(early + late)


def lower_final_kernel(
    levels, flag, faces, south, halo_s, edge_state, p0, p1, p2, p3, ground, table, zonal, merid, basis, basis_t,
    zonal_in, merid_in, thick_in, theta_in,
    zonal_out, merid_out, thick_out, theta_out,
    order, winds_s, thick_s, theta_s, split, sems,
):
    del zonal_in, merid_in, thick_in, theta_in
    count = order.shape[0]
    _, block, width = zonal.shape
    me = lax.axis_index("lev")
    level = (me * block).astype(F32)
    gather_messages(me, (p0, p1, p2, p3), order)
    state = lambda ref, i, line: column_state(ref, (i,), block, width, level, levels, line)
    theta, _, mid, geopot = state(south, 0, halo_s[pl.ds(2 * block, 1), :])
    before = (theta, mid, geopot)
    for row in range(count):
        theta, thick, mid, geopot = state(order, row, ground[pl.ds(row, 1), :])
        theta_s[row] = theta
        thick_s[row] = thick
        now = (theta, mid, geopot)
        winds_s[row] = zonal[row] - push(now, tuple(around(x) for x in now))
        winds_s[count + row] = merid[row] - faces[row] * push(now, before)
        before = now
    now = tuple(edge_state[field] for field in range(3))
    winds_s[2 * count] = merid[count] - faces[count] * push(now, before)
    rows = pl.ds(0, count)
    early = copy_all([(theta_s, theta_out.at[rows]), (thick_s, thick_out.at[rows])], sems)

    @pl.when(flag[0] != 0)
    def _():
        picked = jnp.concatenate([table[rows, :], table[pl.ds(0, count + 1), :]], axis=0)
        clear_gaps(split, width)
        filter_rows(winds_s, 2 * count + 1, picked, (basis, basis_t, split), block)

    late = copy_all(
        [
            (winds_s.at[rows], zonal_out.at[rows]),
            (winds_s.at[pl.ds(count, count + 1)], merid_out.at[pl.ds(0, count + 1)]),
        ],
        sems,
        2,
    )
    wait_all(early + late)


def exchanged(parts):
    peers = lax.axis_size("lev")
    return [parts[0]] + [
        lax.ppermute(parts[step], "lev", [(i, (i + step) % peers) for i in range(peers)]) for step in range(1, peers)
    ]


def body(
    zonal_wind, meridional_wind, thickness, potential_temp, surface_geo, polar_mask, cutoff, damping
):
    lat_rows, block, width = zonal_wind.shape
    lat_count = lax.axis_size("lat")
    peers = lax.axis_size("lev")
    levels = block * peers
    total_rows = lat_rows * lat_count
    first_row = lax.axis_index("lat") * lat_rows
    row_ids = (first_row + jnp.arange(lat_rows + 1, dtype=jnp.int32)).astype(F32)
    faces = jnp.sin(math.pi * row_ids / total_rows)
    centres = jnp.sin(math.pi * (row_ids[:-1] + 0.5) / total_rows)
    coef = jnp.stack([faces[:-1], faces[1:]]) * (0.5 * COURANT) / centres
    northward = [(i, i + 1) for i in range(lat_count - 1)]
    southward = [(i + 1, i) for i in range(lat_count - 1)]
    shape = lambda *dims: jax.ShapeDtypeStruct(dims, F32)
    hbm = pl.BlockSpec(memory_space=pltpu.HBM)
    rows_of = lambda n: pltpu.VMEM((n, block, width), F32)
    dma = lambda n: pltpu.SemaphoreType.DMA((n,))

    lower_each = 1
    upper_each = lat_rows // peers - lower_each
    first = lower_each * peers
    upper = lat_rows - first
    data_rows = packed_rows(block, width)
    message_rows = data_rows + 16
    stay = lambda *arrays: [pltpu.with_memory_space_constraint(x, pltpu.HBM) for x in arrays]
    field = shape(lat_rows, block, width)

    fields = stay(zonal_wind, meridional_wind, thickness, potential_temp)
    to_north, to_south = pl.pallas_call(
        edges_kernel,
        out_shape=[shape(2 * block + 8, width), shape(3 * block, width)],
        in_specs=[hbm] * 4,
        out_specs=[VMEM] * 2,
        scratch_shapes=[rows_of(2), rows_of(2), rows_of(1), pltpu.VMEM((lat_rows, width), F32), dma(6)],
        compiler_params=params(8),
        cost_estimate=cost(1),
        name="edges",
    )(*fields[1:], *stay(surface_geo))
    halo_n = lax.ppermute(to_south, "lat", southward)

    def advect(start, each, halo, name):
        return pl.pallas_call(
            lambda *refs: advect_kernel(start, each, peers, *refs),
            out_shape=[shape(each, 2, data_rows, LANES)] * peers,
            in_specs=[SMEM, VMEM] + [hbm] * 4,
            out_specs=[VMEM] * peers,
            scratch_shapes=[
                pltpu.VMEM((peers, each + extra, block, width), F32) for extra in (0, 1, 2, 2)
            ]
            + [dma(4 * peers)],
            compiler_params=params(12),
            cost_estimate=cost(1 + 2 * each),
            name=name,
        )(coef, halo, *fields)

    upper_sent = advect(first, upper_each, halo_n, "advect_upper")
    to_north, *upper_sent = lax.optimization_barrier((to_north, *upper_sent))
    upper_columns = exchanged(upper_sent)
    halo_s = lax.ppermute(to_north, "lat", northward)
    lower_sent = advect(0, lower_each, halo_s, "advect_lower")
    upper_columns[1], polar_mask, *lower_sent = lax.optimization_barrier((upper_columns[1], polar_mask, *lower_sent))
    flag = jnp.any(polar_mask != 0).astype(jnp.int32).reshape(1)
    lower_columns = exchanged(lower_sent)

    def remap(columns, each, name, after):
        lanes = tile_count(width) * LANES
        return pl.pallas_call(
            lambda *refs: remap_kernel(width, block, peers, *refs),
            out_shape=[shape(each, message_rows, LANES)] * peers,
            in_specs=[VMEM] * peers + [pl.BlockSpec(memory_space=pl.ANY)] * len(after),
            out_specs=[VMEM] * peers,
            scratch_shapes=[
                pltpu.VMEM((each, 2, levels, lanes), F32),
                pltpu.VMEM((each, levels, lanes), F32),
                pltpu.VMEM((each, tile_count(width), 8, LANES), F32),
                pltpu.VMEM((each, 8, lanes), F32),
            ],
            compiler_params=params(12),
            cost_estimate=cost(3 * each - 2.8),
            name=name,
        )(*columns, *after)

    upper_remapped = remap(upper_columns, upper_each, "remap_upper", lower_columns[:1])
    upper_messages = exchanged(upper_remapped)
    lower_remapped = remap(lower_columns, lower_each, "remap_lower", upper_remapped[:1])
    lower_messages = exchanged(lower_remapped)
    step_of_last = (lax.axis_index("lev") + 1) % peers
    _, *candidates = lax.optimization_barrier((lower_remapped[0], *upper_messages))
    last_message = candidates[0][-1:]
    for step in range(1, peers):
        last_message = jnp.where(step_of_last == step, candidates[step][-1:], last_message)
    south = lax.ppermute(last_message, "lat", northward)

    high, low, wave = fourier_tables(width)
    active = (jnp.asarray(wave)[None, :] >= cutoff[:, None]) & (polar_mask[:, None] != 0)
    table = jnp.where(active, damping - 1.0, 0.0)
    tables = [stacked_tables(high, low), stacked_tables(high.T, low.T)]
    split_of = lambda rows: pltpu.VMEM((rows * block, 3 * tile_count(width) * LANES), BF16)

    *partial, edge_state = pl.pallas_call(
        lambda *refs: upper_final_kernel(levels, first, *refs),
        out_shape=[field] * 4 + [shape(3, block, width)],
        in_specs=[SMEM] * 2 + [VMEM] * (peers + 6) + [pl.BlockSpec(memory_space=pl.ANY)],
        out_specs=[hbm] * 4 + [VMEM],
        scratch_shapes=[pltpu.VMEM((upper, message_rows, LANES), F32)]
        + [rows_of(upper)] * 4
        + [rows_of(3), split_of(upper), dma(4)],
        compiler_params=params(18),
        cost_estimate=cost(7),
        name="final_upper",
    )(
        flag, faces, *upper_messages, surface_geo, table, zonal_wind, meridional_wind, *tables, lower_remapped[0]
    )
    edge_state, *lower_messages = lax.optimization_barrier((edge_state, *lower_messages))
    return tuple(
        pl.pallas_call(
            lambda *refs: lower_final_kernel(levels, *refs),
            out_shape=[field] * 4,
            in_specs=[SMEM] * 2 + [VMEM] * (peers + 9) + [hbm] * 4,
            out_specs=[hbm] * 4,
            scratch_shapes=[pltpu.VMEM((first, message_rows, LANES), F32)]
            + [rows_of(2 * first + 1), rows_of(first), rows_of(first), split_of(2 * first + 1), dma(4)],
            input_output_aliases={peers + 11 + i: i for i in range(4)},
            compiler_params=params(16),
            cost_estimate=cost(6),
            name="final_lower",
        )(
            flag, faces, south, halo_s, edge_state, *lower_messages, surface_geo, table, zonal_wind, meridional_wind, *tables,
            *partial,
        )
    )


def solution(mesh):
    field = P("lat", "lev", None)
    in_specs = (field, field, field, field, P("lat", None), P("lat"), P("lat"), P("lat", None))
    return jax.shard_map(body, mesh=mesh, in_specs=in_specs, out_specs=(field,) * 4, check_vma=False)
```

```python
import math

import jax
import jax.numpy as jnp
import numpy as np
from jax import lax
from jax.experimental import pallas as pl
from jax.experimental.pallas import tpu as pltpu
from jax.sharding import PartitionSpec as P

TOP_PRESSURE = 0.01
HYBRID_SCALE = 0.2
EXNER_POWER = 2.0 / 7.0
COURANT = 0.012
HIGHEST = lax.Precision.HIGHEST
F32 = jnp.float32
BF16 = jnp.bfloat16
VMEM = pl.BlockSpec(memory_space=pltpu.VMEM)
SMEM = pl.BlockSpec(memory_space=pltpu.SMEM)
LANES = 128


def params(mib):
    return pltpu.CompilerParams(vmem_limit_bytes=mib * 1024 * 1024)


def cost(microseconds):
    return pl.CostEstimate(
        flops=int(microseconds * 1.1e9), bytes_accessed=int(microseconds * 3.6e6), transcendentals=0
    )


def fourier_tables(count):
    middle = count // 2
    ids = np.arange(count)
    wave = np.where(ids <= middle, ids, ids - middle)
    angle = 2.0 * np.pi / count * (ids[:, None] * wave[None, :] % count)
    edge = (ids == 0) | (ids == middle)
    weight = np.where(edge, 1.0 / math.sqrt(count), math.sqrt(2.0 / count))
    basis = np.where((ids <= middle)[None, :], np.cos(angle), np.sin(angle)) * weight[None, :]
    basis = basis.astype(np.float32)
    high = basis.astype(jnp.bfloat16)
    low = (basis - high.astype(np.float32)).astype(jnp.bfloat16)
    return high, low, wave.astype(np.int32)


def packed_rows(rows, width):
    return rows * width // LANES


def store_packed(ref, index, value):
    rows, width = value.shape
    full = width // LANES
    for tile in range(full):
        ref[(*index, pl.ds(tile * rows, rows), slice(None))] = value[:, tile * LANES : (tile + 1) * LANES]
    if width % LANES:
        rest = value[:, full * LANES :]
        half = rows // 2
        ref[(*index, pl.ds(full * rows, half), slice(None))] = jnp.concatenate([rest[:half], rest[half:]], axis=1)


def load_tile(ref, index, rows, width, tile):
    full = width // LANES
    if tile < full:
        return ref[(*index, pl.ds(tile * rows, rows), slice(None))]
    half = rows // 2
    both = ref[(*index, pl.ds(full * rows, half), slice(None))]
    return jnp.concatenate([both[:, : LANES // 2], both[:, LANES // 2 :]], axis=0)


def tile_count(width):
    return -(-width // LANES)


def wrapped(me, step, peers):
    other = me + step
    return jnp.where(other >= peers, other - peers, other)


def advect_row(row, coef, zonal, merid, t, h, t_s, h_s, t_n, h_n, w_n):
    u = zonal * (0.5 * COURANT)
    w_n = w_n * coef[1, row]
    w_s = merid * coef[0, row]
    for x, x_s, x_n in ((t, t_s, t_n), (h, h_s, h_n)):
        flux = u * (x + jnp.roll(x, 1, axis=1))
        yield x - (jnp.roll(flux, -1, axis=1) - flux) - (w_n * (x_n + x) - w_s * (x + x_s))


def south_edge_kernel(merid, thick, theta, to_south, thick_s, theta_s, sems):
    levels = thick.shape[1]
    first = pl.ds(0, 1)
    copies = [(thick.at[first], thick_s), (theta.at[first], theta_s)]
    wait_all(copy_all([*copies, (merid.at[0], to_south.at[pl.ds(2 * levels, levels)])], sems))
    to_south[pl.ds(0, levels), :] = thick_s[0]
    to_south[pl.ds(levels, levels), :] = theta_s[0] * thick_s[0]


def north_edge_kernel(thick, theta, ground, after, to_north, thick_s, theta_s, ground_s, sems):
    del after
    lat_rows, levels, _ = thick.shape
    last = pl.ds(lat_rows - 1, 1)
    wait_all(copy_all([(thick.at[last], thick_s), (theta.at[last], theta_s), (ground, ground_s)], sems))
    to_north[pl.ds(0, levels), :] = thick_s[0]
    to_north[pl.ds(levels, levels), :] = theta_s[0] * thick_s[0]
    to_north[pl.ds(2 * levels, 1), :] = ground_s[pl.ds(lat_rows - 1, 1), :]


def advect_kernel(first, rows_each, peers, coef, halo, *refs):
    fields, outs, held, sems = refs[:4], refs[4 : 4 + peers], refs[4 + peers : -1], refs[-1]
    lat_rows, levels, _ = fields[0].shape
    top = lat_rows - 1
    me = lax.axis_index("lev")
    part = lambda i: halo[pl.ds(i * levels, levels), :]
    owned = [first + wrapped(me, step, peers) * rows_each for step in range(peers)]
    reach = ((0, rows_each), (0, rows_each + 1), (1, rows_each + 2), (1, rows_each + 2))
    starts = [[jnp.clip(row - before, 0, lat_rows - count) for before, count in reach] for row in owned]
    arriving = [
        copy_all(
            [
                (field.at[pl.ds(start, count)], target.at[step])
                for field, target, start, (_, count) in zip(fields, held, starts[step], reach)
            ],
            sems,
            4 * step,
        )
        for step in range(peers)
    ]
    for step in range(peers):
        wait_all(arriving[step])
        zonal, merid, thick, theta = (ref.at[step] for ref in held)
        z_at, w_at, t_at, _ = (owned[step] - start for start in starts[step])
        for place in range(rows_each):
            row = owned[step] + place
            at = t_at + place
            low, high = jnp.maximum(at - 1, 0), jnp.minimum(at + 1, rows_each + 1)
            t, t_s, t_n = thick[at], thick[low], thick[high]
            h, h_s, h_n = theta[at] * t, theta[low] * t_s, theta[high] * t_n
            w, w_n = merid[w_at + place], merid[jnp.minimum(w_at + place + 1, rows_each)]
            if first == 0 and place == 0:
                t_s = jnp.where(row == 0, part(0), t_s)
                h_s = jnp.where(row == 0, part(1), h_s)
            if first + peers * rows_each == lat_rows and place == rows_each - 1:
                t_n = jnp.where(row == top, part(0), t_n)
                h_n = jnp.where(row == top, part(1), h_n)
                w_n = jnp.where(row == top, part(2), w_n)
            fields_new = advect_row(row, coef, zonal[z_at + place], w, t, h, t_s, h_s, t_n, h_n, w_n)
            for field, new in enumerate(fields_new):
                store_packed(outs[step], (place, field), new)


def target_edges(surface, sigma):
    curve = sigma * sigma
    return TOP_PRESSURE + HYBRID_SCALE * (sigma - curve) + (surface - TOP_PRESSURE) * curve


def target_thickness(surface, first, levels):
    step = 1.0 / levels
    curve = (2.0 * first + 1.0) * (step * step)
    return HYBRID_SCALE * (step - curve) + (surface - TOP_PRESSURE) * curve


def exner(pressure):
    return jnp.exp(EXNER_POWER * jnp.log(pressure))


def split_dot(x, ones):
    a = x.astype(BF16)
    r = x - a.astype(F32)
    b = r.astype(BF16)
    c = (r - b.astype(F32)).astype(BF16)
    dot = lambda v: jnp.dot(v, ones, preferred_element_type=F32)
    return dot(a) + (dot(b) + dot(c))

def remap_kernel(width, block, peers, *refs):
    parts = refs[:peers]
    gathered, spread, base_rows, base_s = refs[-4:]
    outs = refs[-4 - peers : -4]
    me = lax.axis_index("lev")
    count = parts[0].shape[0]
    levels = peers * block
    level_r = lax.broadcasted_iota(jnp.int32, (levels, levels), 0)
    level_c = lax.broadcasted_iota(jnp.int32, (levels, levels), 1)
    running = (level_r <= level_c).astype(F32).astype(BF16)
    below = (
        lax.broadcasted_iota(jnp.int32, (8, levels), 1)
        >= block * (1 + lax.broadcasted_iota(jnp.int32, (8, levels), 0))
    ).astype(F32)
    full = width // LANES
    data_rows = packed_rows(block, width)
    half = block // 2
    sources = [wrapped(me, (peers - step) % peers, peers) for step in range(peers)]
    targets = [wrapped(me, step, peers) for step in range(peers)]
    for place in range(count):
        for step in range(peers):
            at = pl.ds(pl.multiple_of(sources[step] * block, block), block)
            for field in range(2):
                for tile in range(tile_count(width)):
                    cols = min(LANES, width - tile * LANES)
                    gathered[place, field, at, pl.ds(tile * LANES, cols)] = load_tile(
                        parts[step], (place, field), block, width, tile)
    for place in range(count):
        cols = width
        here = pl.ds(0, cols)
        thick = gathered[place, 0, :, here]
        surface_row = TOP_PRESSURE + jnp.sum(thick, axis=0, keepdims=True)
        thick = thick.T
        heat = gathered[place, 1, :, here].T
        upper = TOP_PRESSURE + split_dot(thick, running)
        theta = heat / thick
        offset = split_dot(heat, running) - theta * upper
        surface = upper[:, levels - 1 :]
        lane = lax.broadcasted_iota(jnp.int32, (cols, levels), 1)
        lane_f = lane.astype(F32)
        edge = target_edges(surface, (lane_f + 1.0) * (1.0 / levels))
        at = jnp.zeros((cols, levels), jnp.int32)
        jump = levels // 2
        while jump:
            probe = jnp.take_along_axis(upper, at + (jump - 1), axis=1, mode="promise_in_bounds")
            at = jnp.where(probe < edge, at + jump, at)
            jump //= 2
        pick = lambda table: jnp.take_along_axis(table, at, axis=1, mode="promise_in_bounds")
        heat_to = pick(offset) + pick(theta) * edge
        heat_from = jnp.where(lane == 0, 0.0, pltpu.roll(heat_to, 1, 1))
        theta_next = (heat_to - heat_from) / target_thickness(surface, lane_f, levels)
        exner_to = exner(edge)
        exner_from = jnp.where(lane == 0, TOP_PRESSURE**EXNER_POWER, pltpu.roll(exner_to, 1, 1))
        layer = theta_next * (exner_to - exner_from)
        bases = lax.dot_general(
            below, layer, (((1,), (1,)), ((), ())), precision=HIGHEST, preferred_element_type=F32
        )
        base_s[place, :, here] = bases
        base_s[place, pl.ds(7, 1), here] = surface_row
        spread[place, :, here] = theta_next.T
    for place in range(count):
        for tile in range(tile_count(width)):
            base_rows[place, tile] = base_s[place, :, pl.ds(tile * LANES, LANES)]
        for step in range(peers):
            out = outs[step]
            start = pl.multiple_of(targets[step] * block, block)
            for tile in range(tile_count(width)):
                cols = min(LANES, width - tile * LANES)
                here = pl.ds(tile * LANES, cols)
                if tile < full:
                    out[place, pl.ds(tile * block, block), :] = spread[place, pl.ds(start, block), here]
                else:
                    part = spread[place, pl.ds(start, block), here]
                    out[place, pl.ds(full * block, half), :] = jnp.concatenate([part[:half], part[half:]], axis=1)
                out[place, pl.ds(data_rows + tile, 1), pl.ds(0, cols)] = base_rows[place, tile, pl.ds(7, 1), pl.ds(0, cols)]
                out[place, pl.ds(data_rows + 8 + tile, 1), pl.ds(0, cols)] = base_rows[place, tile, pl.ds(targets[step], 1), pl.ds(0, cols)]


def below_sum(layer):
    rows, width = layer.shape
    groups = rows // 8
    carry = None
    pieces = []
    sub = lax.broadcasted_iota(jnp.int32, (8, width), 0)
    for g in reversed(range(groups)):
        x = layer[g * 8 : (g + 1) * 8]
        total = x
        for step in (1, 2, 4):
            total = total + jnp.where(sub < 8 - step, pltpu.roll(total, 8 - step, 0), 0.0)
        under = total - x
        if carry is not None:
            under = under + carry
            carry = carry + total[0:1]
        else:
            carry = total[0:1]
        pieces.append(under)
    return jnp.concatenate(pieces[::-1], axis=0)


def column_state(message, index, block, width, first_level, levels, ground):
    tiles = tile_count(width)
    data_rows = packed_rows(block, width)
    theta = jnp.concatenate([load_tile(message, index, block, width, t) for t in range(tiles)], axis=1)

    def line(first):
        return jnp.concatenate(
            [message[(*index, pl.ds(first + t, 1), pl.ds(0, min(LANES, width - t * LANES)))] for t in range(tiles)],
            axis=1,
        )

    surface = line(data_rows)
    base = line(data_rows + 8)
    sub = lax.broadcasted_iota(jnp.int32, (block, width), 0).astype(F32) + first_level
    thick = target_thickness(surface, sub, levels)
    top = exner(target_edges(surface, sub * (1.0 / levels)))
    bottom_edge = exner(target_edges(surface, (first_level + block) * (1.0 / levels)))
    sub_i = lax.broadcasted_iota(jnp.int32, (block, width), 0)
    bottom = jnp.where(sub_i == block - 1, bottom_edge, pltpu.roll(top, block - 1, 0))
    layer = theta * (bottom - top)
    geopot = (ground + base) + (below_sum(layer) + 0.5 * layer)
    return theta, thick, 0.5 * (top + bottom), geopot


def push(now, before):
    theta, exner_mid, geopot = now
    theta_b, exner_b, geopot_b = before
    return (geopot - geopot_b) + 0.5 * (theta + theta_b) * (exner_mid - exner_b)


def filtered(value, table, basis, basis_t, split, block):
    rows, width = value.shape
    span = tile_count(width) * LANES

    def product(x, stacked):
        high = x.astype(BF16)
        low = (x - high.astype(F32)).astype(BF16)
        for i, part in enumerate((high, low, high)):
            split[pl.ds(0, rows), pl.ds(i * span, width)] = part
        return jnp.dot(split[pl.ds(0, rows), :], stacked[...], preferred_element_type=F32)

    spectral = product(value, basis)
    spectral = (spectral.reshape(rows // block, block, width) * table[:, None, :]).reshape(rows, width)
    return value + product(spectral, basis_t)


def filtered_by_parts(value, table, basis, basis_t, block):
    rows, width = value.shape
    span = tile_count(width) * LANES

    def product(x, stacked):
        x_high = x.astype(BF16)
        x_low = (x - x_high.astype(F32)).astype(BF16)
        high, low = stacked[pl.ds(0, width), :], stacked[pl.ds(2 * span, width), :]
        dot = lambda a, b: jnp.dot(a, b, preferred_element_type=F32)
        return dot(x_high, high) + (dot(x_low, high) + dot(x_high, low))

    spectral = product(value, basis)
    spectral = (spectral.reshape(rows // block, block, width) * table[:, None, :]).reshape(rows, width)
    return value + product(spectral, basis_t)


def clear_gaps(split, width):
    span = tile_count(width) * LANES
    last = width // LANES * LANES
    for i in range(split.shape[1] // span):
        split[:, pl.ds(i * span + last, span - last)] = jnp.zeros((split.shape[0], span - last), BF16)


def stacked_tables(high, low):
    rows, width = high.shape
    gap = np.zeros((tile_count(rows) * LANES - rows, width), high.dtype)
    return jnp.asarray(np.concatenate([high, gap, high, gap, low, gap]))


def gather_messages(me, parts, order):
    peers = len(parts)
    for step, part in enumerate(parts):
        owner = wrapped(me, (peers - step) % peers, peers)
        for place in range(part.shape[0]):
            order[owner * part.shape[0] + place] = part[place]


def copy_all(copies, sems, first=0):
    started = [pltpu.make_async_copy(source, target, sems.at[first + i]) for i, (source, target) in enumerate(copies)]
    for copy in started:
        copy.start()
    return started


def wait_all(copies):
    for copy in copies:
        copy.wait()


def filter_rows(ref, count, table, tables, block):
    width = ref.shape[-1]
    value = ref[pl.ds(0, count)].reshape(count * block, width)
    value = (filtered if len(tables) == 3 else filtered_by_parts)(value, table, *tables, block)
    ref[pl.ds(0, count)] = value.reshape(count, block, width)


def around(x):
    return jnp.roll(x, 1, axis=1)


def upper_final_kernel(
    levels, first, flag, faces, p0, p1, p2, p3, ground, table, zonal, merid, basis, basis_t, after,
    zonal_out, merid_out, thick_out, theta_out, edge_state,
    order, zonal_s, merid_s, thick_s, theta_s, carried, split, sems,
):
    del after
    lat_rows, block, width = zonal.shape
    count = lat_rows - first
    rows = pl.ds(first, count)
    me = lax.axis_index("lev")
    level = (me * block).astype(F32)
    gather_messages(me, (p0, p1, p2, p3), order)
    carried[...] = jnp.zeros_like(carried)

    def one_row(i, _):
        row = first + i
        theta, thick, mid, geopot = column_state(order, (i,), block, width, level, levels, ground[pl.ds(row, 1), :])
        theta_s[i] = theta
        thick_s[i] = thick
        now = (theta, mid, geopot)
        zonal_s[i] = zonal[row] - push(now, tuple(around(x) for x in now))
        before = (carried[0], carried[1], carried[2])
        merid_s[jnp.maximum(i - 1, 0)] = merid[row] - faces[row] * push(now, before)
        for field, x in enumerate(now):
            carried[field] = x

        @pl.when(i == 0)
        def _():
            for field, x in enumerate(now):
                edge_state[field] = x

        return 0

    lax.fori_loop(0, count, one_row, 0)
    early = copy_all([(theta_s, theta_out.at[rows]), (thick_s, thick_out.at[rows])], sems)

    @pl.when(flag[0] != 0)
    def _():
        tables = (basis, basis_t, split)
        clear_gaps(split, width)
        filter_rows(zonal_s, count, table[rows, :], tables, block)

    early += copy_all([(zonal_s, zonal_out.at[rows])], sems, 2)

    @pl.when(flag[0] != 0)
    def _():
        tables = (basis, basis_t, split)
        filter_rows(merid_s, count - 1, table[pl.ds(first + 1, count - 1), :], tables, block)

    late = copy_all([(merid_s.at[pl.ds(0, count - 1)], merid_out.at[pl.ds(first + 1, count - 1)])], sems, 3)
    wait_all(early + late)


def lower_final_kernel(
    levels, flag, faces, south, halo_s, edge_state, p0, p1, p2, p3, ground, table, zonal, merid, basis, basis_t,
    zonal_in, merid_in, thick_in, theta_in,
    zonal_out, merid_out, thick_out, theta_out,
    order, winds_s, thick_s, theta_s, sems,
):
    del zonal_in, merid_in, thick_in, theta_in
    count = order.shape[0]
    _, block, width = zonal.shape
    me = lax.axis_index("lev")
    level = (me * block).astype(F32)
    gather_messages(me, (p0, p1, p2, p3), order)
    state = lambda ref, i, line: column_state(ref, (i,), block, width, level, levels, line)
    theta, _, mid, geopot = state(south, 0, halo_s[pl.ds(2 * block, 1), :])
    before = (theta, mid, geopot)
    for row in range(count):
        theta, thick, mid, geopot = state(order, row, ground[pl.ds(row, 1), :])
        theta_s[row] = theta
        thick_s[row] = thick
        now = (theta, mid, geopot)
        winds_s[row] = zonal[row] - push(now, tuple(around(x) for x in now))
        winds_s[count + row] = merid[row] - faces[row] * push(now, before)
        before = now
    now = tuple(edge_state[field] for field in range(3))
    winds_s[2 * count] = merid[count] - faces[count] * push(now, before)
    rows = pl.ds(0, count)
    early = copy_all([(theta_s, theta_out.at[rows]), (thick_s, thick_out.at[rows])], sems)

    @pl.when(flag[0] != 0)
    def _():
        picked = jnp.concatenate([table[rows, :], table[pl.ds(0, count + 1), :]], axis=0)
        filter_rows(winds_s, 2 * count + 1, picked, (basis, basis_t), block)

    late = copy_all(
        [
            (winds_s.at[rows], zonal_out.at[rows]),
            (winds_s.at[pl.ds(count, count + 1)], merid_out.at[pl.ds(0, count + 1)]),
        ],
        sems,
        2,
    )
    wait_all(early + late)


def exchanged(parts):
    peers = lax.axis_size("lev")
    return [parts[0]] + [
        lax.ppermute(parts[step], "lev", [(i, (i + step) % peers) for i in range(peers)]) for step in range(1, peers)
    ]


def body(
    zonal_wind, meridional_wind, thickness, potential_temp, surface_geo, polar_mask, cutoff, damping
):
    lat_rows, block, width = zonal_wind.shape
    lat_count = lax.axis_size("lat")
    peers = lax.axis_size("lev")
    levels = block * peers
    total_rows = lat_rows * lat_count
    first_row = lax.axis_index("lat") * lat_rows
    row_ids = (first_row + jnp.arange(lat_rows + 1, dtype=jnp.int32)).astype(F32)
    faces = jnp.sin(math.pi * row_ids / total_rows)
    centres = jnp.sin(math.pi * (row_ids[:-1] + 0.5) / total_rows)
    coef = jnp.stack([faces[:-1], faces[1:]]) * (0.5 * COURANT) / centres
    northward = [(i, i + 1) for i in range(lat_count - 1)]
    southward = [(i + 1, i) for i in range(lat_count - 1)]
    shape = lambda *dims: jax.ShapeDtypeStruct(dims, F32)
    hbm = pl.BlockSpec(memory_space=pltpu.HBM)
    rows_of = lambda n: pltpu.VMEM((n, block, width), F32)
    dma = lambda n: pltpu.SemaphoreType.DMA((n,))

    lower_each = 1
    upper_each = lat_rows // peers - lower_each
    first = lower_each * peers
    upper = lat_rows - first
    data_rows = packed_rows(block, width)
    message_rows = data_rows + 16
    stay = lambda *arrays: [pltpu.with_memory_space_constraint(x, pltpu.HBM) for x in arrays]
    field = shape(lat_rows, block, width)

    fields = stay(zonal_wind, meridional_wind, thickness, potential_temp)
    to_south = pl.pallas_call(
        south_edge_kernel,
        out_shape=shape(3 * block, width),
        in_specs=[hbm] * 3,
        out_specs=VMEM,
        scratch_shapes=[rows_of(1), rows_of(1), dma(3)],
        compiler_params=params(8),
        cost_estimate=cost(1),
        name="south_edge",
    )(*fields[1:])
    halo_n = lax.ppermute(to_south, "lat", southward)
    to_north = pl.pallas_call(
        north_edge_kernel,
        out_shape=shape(2 * block + 8, width),
        in_specs=[hbm] * 3 + [pl.BlockSpec(memory_space=pl.ANY)],
        out_specs=VMEM,
        scratch_shapes=[rows_of(1), rows_of(1), pltpu.VMEM((lat_rows, width), F32), dma(3)],
        compiler_params=params(8),
        cost_estimate=cost(1),
        name="north_edge",
    )(*fields[2:], *stay(surface_geo), to_south)

    def advect(start, each, halo, name):
        return pl.pallas_call(
            lambda *refs: advect_kernel(start, each, peers, *refs),
            out_shape=[shape(each, 2, data_rows, LANES)] * peers,
            in_specs=[SMEM, VMEM] + [hbm] * 4,
            out_specs=[VMEM] * peers,
            scratch_shapes=[
                pltpu.VMEM((peers, each + extra, block, width), F32) for extra in (0, 1, 2, 2)
            ]
            + [dma(4 * peers)],
            compiler_params=params(12),
            cost_estimate=cost(1 + 2 * each),
            name=name,
        )(coef, halo, *fields)

    upper_sent = advect(first, upper_each, halo_n, "advect_upper")
    to_north, *upper_sent = lax.optimization_barrier((to_north, *upper_sent))
    upper_columns = exchanged(upper_sent)
    halo_s = lax.ppermute(to_north, "lat", northward)
    lower_sent = advect(0, lower_each, halo_s, "advect_lower")
    upper_columns[1], polar_mask, *lower_sent = lax.optimization_barrier((upper_columns[1], polar_mask, *lower_sent))
    flag = jnp.any(polar_mask != 0).astype(jnp.int32).reshape(1)
    lower_columns = exchanged(lower_sent)

    def remap(columns, each, name, after):
        lanes = tile_count(width) * LANES
        return pl.pallas_call(
            lambda *refs: remap_kernel(width, block, peers, *refs),
            out_shape=[shape(each, message_rows, LANES)] * peers,
            in_specs=[VMEM] * peers + [pl.BlockSpec(memory_space=pl.ANY)] * len(after),
            out_specs=[VMEM] * peers,
            scratch_shapes=[
                pltpu.VMEM((each, 2, levels, lanes), F32),
                pltpu.VMEM((each, levels, lanes), F32),
                pltpu.VMEM((each, tile_count(width), 8, LANES), F32),
                pltpu.VMEM((each, 8, lanes), F32),
            ],
            compiler_params=params(12),
            cost_estimate=cost(3 * each - 2.8),
            name=name,
        )(*columns, *after)

    upper_remapped = remap(upper_columns, upper_each, "remap_upper", lower_columns[:1])
    upper_messages = exchanged(upper_remapped)
    lower_remapped = remap(lower_columns, lower_each, "remap_lower", upper_remapped[:1])
    lower_messages = exchanged(lower_remapped)
    step_of_last = (lax.axis_index("lev") + 1) % peers
    _, *candidates = lax.optimization_barrier((lower_remapped[0], *upper_messages))
    last_message = candidates[0][-1:]
    for step in range(1, peers):
        last_message = jnp.where(step_of_last == step, candidates[step][-1:], last_message)
    south = lax.ppermute(last_message, "lat", northward)

    high, low, wave = fourier_tables(width)
    active = (jnp.asarray(wave)[None, :] >= cutoff[:, None]) & (polar_mask[:, None] != 0)
    table = jnp.where(active, damping - 1.0, 0.0)
    tables = [stacked_tables(high, low), stacked_tables(high.T, low.T)]
    split_of = lambda rows: pltpu.VMEM((rows * block, 3 * tile_count(width) * LANES), BF16)

    *partial, edge_state = pl.pallas_call(
        lambda *refs: upper_final_kernel(levels, first, *refs),
        out_shape=[field] * 4 + [shape(3, block, width)],
        in_specs=[SMEM] * 2 + [VMEM] * (peers + 6) + [pl.BlockSpec(memory_space=pl.ANY)],
        out_specs=[hbm] * 4 + [VMEM],
        scratch_shapes=[pltpu.VMEM((upper, message_rows, LANES), F32)]
        + [rows_of(upper)] * 4
        + [rows_of(3), split_of(upper), dma(4)],
        compiler_params=params(18),
        cost_estimate=cost(7),
        name="final_upper",
    )(
        flag, faces, *upper_messages, surface_geo, table, zonal_wind, meridional_wind, *tables, lower_remapped[0]
    )
    edge_state, *lower_messages = lax.optimization_barrier((edge_state, *lower_messages))
    return tuple(
        pl.pallas_call(
            lambda *refs: lower_final_kernel(levels, *refs),
            out_shape=[field] * 4,
            in_specs=[SMEM] * 2 + [VMEM] * (peers + 9) + [hbm] * 4,
            out_specs=[hbm] * 4,
            scratch_shapes=[pltpu.VMEM((first, message_rows, LANES), F32)]
            + [rows_of(2 * first + 1), rows_of(first), rows_of(first), dma(4)],
            input_output_aliases={peers + 11 + i: i for i in range(4)},
            compiler_params=params(16),
            cost_estimate=cost(6),
            name="final_lower",
        )(
            flag, faces, south, halo_s, edge_state, *lower_messages, surface_geo, table, zonal_wind, meridional_wind, *tables,
            *partial,
        )
    )


def solution(mesh):
    field = P("lat", "lev", None)
    in_specs = (field, field, field, field, P("lat", None), P("lat"), P("lat"), P("lat", None))
    return jax.shard_map(body, mesh=mesh, in_specs=in_specs, out_specs=(field,) * 4, check_vma=False)
```
